512 devices in a mesh: clip: 4 (over y_lo), cfg: 2 (over core), patch: 64 (over z, x, y_hi).
Axes of the slice: x: 4, y: 8 (y_hi: 2, y_lo: 4; y = y_hi * 4 + y_lo), z: 8, core: 2. Of those that a mesh axis runs over, the one named last changes fastest.
Arguments:
- queries: bfloat16 [2, 2, 4096, 4096], P('cfg', None, ('clip', 'patch')), parts along dimension 2, may hold values from -270 to 270
- keys_values: bfloat16 [2, 2, 2, 4096, 4096], P('cfg', None, None, ('clip', 'patch')), parts along dimension 3, may hold values from -8 to 8
- timesteps: int32 [8], P('clip'), parts along dimension 0, may hold values from 0 to 49
- gate_table: float32 [50, 4096], replicated, may hold values from 0.5 to 1.5
Outputs:
- guided: bfloat16 [2, 4096, 32, 128], P(None, ('clip', 'patch'), None, 'cfg'), parts along dimension 1
The draws below stay inside these ranges and needn't reach their ends.
There are 4 independent parts, one for each index of `clip`. The reference program is written for one: setup_inputs(seed, part) draws one part's arguments, and reference() takes and returns one part's arrays. A program takes and returns all parts, laid end to end along the dimension named above; an argument that names none is the same for every part. Nothing has to cross between parts.
All inputs are finite; a program needn't handle non-finite values.
Results may differ from the reference program's by a relative error of at most 0.013.
Values may be sent and summed in bfloat16 or wider, within the bound.
No kernel may reach another device: no remote copies, remote signals or barrier semaphores. Data moves between devices by JAX's collectives and lax.ppermute only.
A program may use at most 64 MiB of HBM per device.

```python
import math
import jax
import jax.numpy as jnp
from jax import lax

HEADS = 32
HEAD_DIM = 128
TOK_DEV = 16
NUM_T = 50
TOKENS = 1024
WIDTH = 4096
N_PATCH = 64


def key_field(key, spread):
    field = jnp.clip(jax.random.normal(key, (2, 2, 2, TOKENS, WIDTH), jnp.float32), -6.0, 6.0)
    scales = 1.0 + spread * jax.random.uniform(jax.random.fold_in(key, 11), (2, 2, 2, TOKENS, 1), jnp.float32, -1.0, 1.0)
    field = field * scales
    return field


def draw_keys_values(key, part):
    field = key_field(key, 0.0)
    return field.astype(jnp.bfloat16)


def draw_queries(key, part):
    key = jax.random.fold_in(key, 2)
    result = 2.0 * jnp.clip(jax.random.normal(key, (2, 2, TOKENS, WIDTH), jnp.float32), -6.0, 6.0)
    return result.astype(jnp.bfloat16)


def setup_inputs(seed: int = 0, part: int = 0) -> dict:
    streams_of = jax.random.split(jax.random.key(seed), 5)
    own_keys = jax.random.split(jax.random.fold_in(streams_of[4], part), 5)
    queries = draw_queries(jax.random.fold_in(jax.random.fold_in(streams_of[4], part), 71), part)
    keys_values = draw_keys_values(jax.random.fold_in(jax.random.fold_in(streams_of[4], part), 71), part)
    timesteps = jax.random.randint(own_keys[2], (2,), 0, NUM_T).astype(jnp.int32)
    gate_table = jnp.clip(1.0 + 0.1 * jax.random.normal(streams_of[3], (NUM_T, WIDTH), jnp.float32), 0.5, 1.5)
    return {"queries": queries, "keys_values": keys_values, "timesteps": timesteps, "gate_table": gate_table}


def split_heads(field):
    return field.reshape(TOKENS, HEADS, HEAD_DIM).transpose(1, 0, 2)

def reference(queries, keys_values, timesteps, gate_table):
    scale = 1.0 / math.sqrt(HEAD_DIM)
    patch_of = jnp.arange(TOKENS) // TOK_DEV
    same = patch_of[:, None] == patch_of[None, :]

    def first_head(args):
        query, key_h, value_h = args
        scores = jnp.dot(query, key_h.T, preferred_element_type=jnp.float32) * scale
        top = lax.optimization_barrier(jnp.max(scores, axis=1, keepdims=True))
        weight = jnp.exp(scores - top)
        total = lax.optimization_barrier(jnp.sum(weight, axis=1, keepdims=True))
        summed = jnp.dot(weight.astype(jnp.bfloat16), value_h, preferred_element_type=jnp.float32)
        return (summed / total).astype(jnp.bfloat16)

    def second_head(args):
        query, key_new, value_new, key_old, value_old = args
        stale_scores = jnp.dot(query, key_old.T, preferred_element_type=jnp.float32) * scale
        stale_scores = jnp.where(same, -jnp.inf, stale_scores)
        query_p = query.reshape(N_PATCH, TOK_DEV, HEAD_DIM).astype(jnp.float32)
        key_p = key_new.reshape(N_PATCH, TOK_DEV, HEAD_DIM).astype(jnp.float32)
        local_scores = jnp.einsum('pqd,pkd->pqk', query_p, key_p) * scale
        top = jnp.maximum(lax.optimization_barrier(jnp.max(stale_scores, axis=1)), lax.optimization_barrier(jnp.max(local_scores, axis=2)).reshape(TOKENS))
        stale_weight = jnp.exp(stale_scores - top[:, None])
        local_weight = jnp.exp(local_scores - top.reshape(N_PATCH, TOK_DEV)[:, :, None])
        total = lax.optimization_barrier(jnp.sum(stale_weight, axis=1)) + lax.optimization_barrier(jnp.sum(local_weight, axis=2)).reshape(TOKENS)
        summed = jnp.dot(stale_weight.astype(jnp.bfloat16), value_old, preferred_element_type=jnp.float32)
        local_b = local_weight.astype(jnp.bfloat16).astype(jnp.float32)
        value_p = value_new.reshape(N_PATCH, TOK_DEV, HEAD_DIM).astype(jnp.float32)
        summed = summed + jnp.einsum('pqk,pkd->pqd', local_b, value_p).reshape(TOKENS, HEAD_DIM)
        return (summed / total[:, None]).astype(jnp.bfloat16)
    attn = []
    for branch in range(2):
        old_keys = split_heads(keys_values[branch, 0, 0])
        old_values = split_heads(keys_values[branch, 0, 1])
        first = lax.map(first_head, (split_heads(queries[branch, 0]), old_keys, old_values))
        second = lax.map(second_head, (split_heads(queries[branch, 1]), split_heads(keys_values[branch, 1, 0]), split_heads(keys_values[branch, 1, 1]), old_keys, old_values))
        attn.append((first, second))
    one_hot = (timesteps[:, None] == jnp.arange(NUM_T)[None, :]).astype(jnp.float32)
    gates = jnp.dot(one_hot, gate_table, precision=lax.Precision.HIGHEST)
    outputs = []
    for step in range(2):
        cond = attn[0][step].astype(jnp.float32).transpose(1, 0, 2)
        uncond = attn[1][step].astype(jnp.float32).transpose(1, 0, 2)
        gate = gates[step].reshape(HEADS, HEAD_DIM)[None]
        outputs.append((gate * (uncond + 5.0 * (cond - uncond))).astype(jnp.bfloat16))
    return jnp.stack(outputs)
```

```python
import math

import jax
import jax.numpy as jnp
from jax import lax
from jax.experimental import pallas as pl
from jax.experimental.pallas import tpu as pltpu
from jax.sharding import PartitionSpec as P

HEADS = 32
DEPTH = 128
COPIES = 2
TOK = 16
HALF = TOK // COPIES
N_PATCH = 64
TOKENS = N_PATCH * TOK
GROUP = 8
FACTOR = math.log2(math.e) / math.sqrt(DEPTH)
BF16 = jnp.bfloat16
F32 = jnp.float32


def head_of(ref, step, h):
    return ref[step, :, h * DEPTH : (h + 1) * DEPTH]


def pack_kernel(q_ref, kv_ref, out_ref):
    for h in range(HEADS):
        first = head_of(q_ref, 0, h)
        second = head_of(q_ref, 1, h)
        key = head_of(kv_ref, 0, h)
        value = head_of(kv_ref, 1, h)
        for copy in range(COPIES):
            rows = slice(copy * HALF, (copy + 1) * HALF)
            chunk = copy * HEADS + h
            out_ref[chunk, 0:16, :] = jnp.concatenate([first[rows], second[rows]], 0)
            out_ref[chunk, 16:32, :] = key
            out_ref[chunk, 32:48, :] = value


def pieces(value):
    high = value.astype(BF16).astype(F32)
    rest = value - high
    mid = rest.astype(BF16).astype(F32)
    return high, mid, rest - mid


def attend_kernel(x_ref, out_ref):
    keys = x_ref[:, 16:32, :].reshape(TOKENS, DEPTH)
    values = x_ref[:, 32:48, :].reshape(TOKENS, DEPTH)
    n = GROUP * TOK
    row = lax.broadcasted_iota(jnp.int32, (n, n), 0)
    col = lax.broadcasted_iota(jnp.int32, (n, n), 1)
    own = jnp.logical_and(row // TOK == col // TOK, row % TOK >= HALF)
    lane = lax.broadcasted_iota(jnp.int32, (GROUP, HALF, DEPTH), 2)
    for g in range(N_PATCH // GROUP):
        patches = slice(g * GROUP, (g + 1) * GROUP)
        query = x_ref[patches, 0:16, :].reshape(n, DEPTH)
        score = lax.dot_general(
            query, keys, (((1,), (1,)), ((), ())), preferred_element_type=F32
        )
        near = jnp.where(own, -jnp.inf, score[:, g * n : (g + 1) * n])
        parts = [score[:, : g * n], near, score[:, (g + 1) * n :]]
        score = jnp.concatenate([p for p in parts if p.shape[1]], axis=1)
        top = jnp.max(score, axis=1, keepdims=True)
        weight = jnp.exp2((score - top) * FACTOR)
        total = jnp.sum(weight, axis=1, keepdims=True)
        summed = jnp.dot(weight.astype(BF16), values, preferred_element_type=F32)
        attn = (summed / total).reshape(GROUP, 2, HALF, DEPTH)
        out_ref[patches, 0] = attn[:, 0].astype(BF16)
        out_ref[patches, 1] = attn[:, 1].astype(BF16)
        top = jnp.broadcast_to(top, (n, DEPTH)).reshape(GROUP, 2, HALF, DEPTH)[:, 1]
        total = jnp.broadcast_to(total, (n, DEPTH)).reshape(GROUP, 2, HALF, DEPTH)[:, 1]
        stats = jnp.zeros((GROUP, HALF, DEPTH), F32)
        for i, piece in enumerate(pieces(top) + pieces(total)):
            stats = jnp.where(lane == i, piece, stats)
        out_ref[patches, 2] = stats.astype(BF16)


def local_kernel(q_ref, kv_ref, sum_ref, top_ref, total_ref):
    n = GROUP * TOK
    row = lax.broadcasted_iota(jnp.int32, (n, n), 0)
    col = lax.broadcasted_iota(jnp.int32, (n, n), 1)
    same = row // TOK == col // TOK

    def rows(ref, step, g):
        return jnp.concatenate(
            [head_of(ref, step, h) for h in range(g * GROUP, (g + 1) * GROUP)], 0
        )

    for g in range(HEADS // GROUP):
        score = lax.dot_general(
            rows(q_ref, 1, g),
            rows(kv_ref, 0, g),
            (((1,), (1,)), ((), ())),
            preferred_element_type=F32,
        )
        score = jnp.where(same, score, -jnp.inf)
        top = jnp.max(score, axis=1, keepdims=True)
        weight = jnp.exp2((score - top) * FACTOR)
        total = jnp.sum(weight, axis=1, keepdims=True)
        summed = jnp.dot(
            weight.astype(BF16), rows(kv_ref, 1, g), preferred_element_type=F32
        )
        for ref, value in ((sum_ref, summed), (top_ref, top), (total_ref, total)):
            value = jnp.broadcast_to(value, (n, DEPTH)).reshape(GROUP, COPIES, HALF, DEPTH)
            for copy in range(COPIES):
                start = copy * HEADS + g * GROUP
                ref[start : start + GROUP] = value[:, copy]


def merge_kernel(y_ref, sum_ref, top_ref, total_ref, out_ref, held):
    n = N_PATCH * HALF
    held[0:n] = y_ref[:, 0].astype(F32).reshape(n, DEPTH)
    stats = y_ref[:, 2].astype(F32).reshape(n, DEPTH).astype(BF16)
    row = lax.broadcasted_iota(jnp.int32, (DEPTH, 2 * DEPTH), 0)
    col = lax.broadcasted_iota(jnp.int32, (DEPTH, 2 * DEPTH), 1)
    pick = jnp.where(
        jnp.logical_and(row < 6, row // 3 == col // DEPTH), 1.0, 0.0
    ).astype(BF16)
    far = jnp.dot(stats, pick, preferred_element_type=F32)
    far_top, far_total = far[:, :DEPTH], far[:, DEPTH:]
    near_top = top_ref[...].reshape(n, DEPTH)
    top = jnp.maximum(far_top, near_top)
    far_scale = jnp.exp2((far_top - top) * FACTOR) * far_total
    near_scale = jnp.exp2((near_top - top) * FACTOR)
    total = far_scale + near_scale * total_ref[...].reshape(n, DEPTH)
    far_attn = y_ref[:, 1].astype(F32).reshape(n, DEPTH)
    summed = far_scale * far_attn + near_scale * sum_ref[...].reshape(n, DEPTH)
    held[n : 2 * n] = summed / total
    for step in range(2):
        for copy in range(COPIES):
            for t in range(HALF):
                start = step * n + copy * HEADS * HALF + t
                out_ref[step, copy * HALF + t] = held[
                    pl.ds(start, HEADS, stride=HALF), :
                ].astype(BF16)


def guide_kernel(both_ref, gate_ref, out_ref):
    upper = lax.axis_index("cfg") == 1
    half = DEPTH // 2
    for step in range(2):
        gate = gate_ref[step]
        for t in range(TOK):
            cond = both_ref[0, step, t].astype(F32)
            uncond = both_ref[1, step, t].astype(F32)
            mixed = gate * (uncond + 5.0 * (cond - uncond))
            out_ref[step, t] = jnp.where(upper, mixed[:, half:], mixed[:, :half]).astype(BF16)


QUERIES = pl.BlockSpec((None, 2, TOK, HEADS * DEPTH), lambda i: (0, 0, 0, 0))


def pairs(step):
    return pl.BlockSpec((None, None, 2, TOK, HEADS * DEPTH), lambda i: (0, step, 0, 0, 0))


def call(kernel, out, args, specs=None, scratch=(), flops=0):
    many = isinstance(out, list)
    shapes = out if many else [out]
    moved = sum(a.size * a.dtype.itemsize for a in list(args) + list(shapes))
    vmem = pl.BlockSpec(memory_space=pltpu.VMEM)
    return pl.pallas_call(
        kernel,
        grid=(1,),
        out_shape=out,
        in_specs=specs or [vmem] * len(args),
        out_specs=[vmem] * len(shapes) if many else vmem,
        scratch_shapes=list(scratch),
        cost_estimate=pl.CostEstimate(flops=flops, bytes_accessed=moved, transcendentals=0),
        compiler_params=pltpu.CompilerParams(vmem_limit_bytes=32 << 20),
    )(*args)


def body(queries, keys_values, timesteps, gate_table):
    shape = jax.ShapeDtypeStruct
    fields = (queries, keys_values)
    sent = call(pack_kernel, shape((N_PATCH, 48, DEPTH), BF16), fields, [QUERIES, pairs(0)])
    held = lax.all_to_all(sent, "patch", split_axis=0, concat_axis=0, tiled=True)
    part = shape((N_PATCH, HALF, DEPTH), F32)
    near = call(local_kernel, [part] * 3, fields, [QUERIES, pairs(1)])
    gates = jnp.take(gate_table, timesteps, axis=0, mode="clip").reshape(2, HEADS, DEPTH)
    far = call(attend_kernel, shape((N_PATCH, 3, HALF, DEPTH), BF16), (held,))
    back = lax.all_to_all(far, "patch", split_axis=0, concat_axis=0, tiled=True)
    attn = call(
        merge_kernel,
        shape((2, TOK, HEADS, DEPTH), BF16),
        (back, *near),
        scratch=[pltpu.VMEM((2 * N_PATCH * HALF, DEPTH), F32)],
    )
    both = lax.all_gather(attn, "cfg", axis=0, tiled=False)
    return call(guide_kernel, shape((2, TOK, HEADS, DEPTH // 2), BF16), (both, gates))


def solution(mesh):
    placed = (
        P("cfg", None, ("clip", "patch"), None),
        P("cfg", None, None, ("clip", "patch"), None),
        P("clip"),
        P(),
    )
    return jax.shard_map(
        body,
        mesh=mesh,
        in_specs=placed,
        out_specs=P(None, ("clip", "patch"), None, "cfg"),
        check_vma=False,
    )
```

```python
import math

import jax
import jax.numpy as jnp
from jax import lax
from jax.experimental import pallas as pl
from jax.experimental.pallas import tpu as pltpu
from jax.sharding import PartitionSpec as P

HEADS = 32
DEPTH = 128
HALF = DEPTH // 2
TOK = 16
SIDES = 2
NEAR = HEADS * TOK
ROWS = 2 * NEAR
GROUP = 8
BLOCK = 256
FACTOR = math.log2(math.e) / math.sqrt(DEPTH)
BF16 = jnp.bfloat16
F32 = jnp.float32
SHAPE = jax.ShapeDtypeStruct


def dot_t(a, b):
    return lax.dot_general(a, b, (((1,), (1,)), ((), ())), preferred_element_type=F32)


def pack_kernel(q_ref, kv_ref, out_ref, held, sems):
    fields = [q_ref.at[0, 0], q_ref.at[0, 1], kv_ref.at[0, 0, 0], kv_ref.at[0, 0, 1]]
    copies = [
        pltpu.make_async_copy(field, held.at[i], sems.at[i]) for i, field in enumerate(fields)
    ]
    for copy in copies:
        copy.start()
    for i, copy in enumerate(copies):
        copy.wait()
        for h in range(HEADS):
            out_ref[h, i * TOK : (i + 1) * TOK, :] = held[i, :, h * DEPTH : (h + 1) * DEPTH]


def split_value(value):
    high = value.astype(BF16).astype(F32)
    rest = value - high
    mid = rest.astype(BF16).astype(F32)
    return high, mid, rest - mid


def write_stats(top, total):
    n = top.shape[0] // TOK
    lane = lax.broadcasted_iota(jnp.int32, (n, TOK // 2, DEPTH), 2)
    both = []
    for value in (top, total):
        wide = jnp.broadcast_to(value, (n * TOK, DEPTH)).reshape(n, 2, TOK // 2, DEPTH)
        both.extend(split_value(jnp.where(lane < HALF, wide[:, 0], wide[:, 1])))
    stats = jnp.zeros((n, TOK // 2, DEPTH), F32)
    for i, piece in enumerate(both):
        stats = jnp.where(lane % HALF == i, piece, stats)
    return stats.astype(BF16)


def read_stats(stats):
    n = stats.shape[0]
    row = lax.broadcasted_iota(jnp.int32, (DEPTH, 4 * DEPTH), 0)
    part = lax.broadcasted_iota(jnp.int32, (DEPTH, 4 * DEPTH), 1) // DEPTH
    first = part % 2 * HALF + part // 2 * 3
    pick = jnp.where(jnp.logical_and(row >= first, row < first + 3), 1.0, 0.0).astype(BF16)
    flat = stats.astype(F32).reshape(n * TOK // 2, DEPTH).astype(BF16)
    wide = jnp.dot(flat, pick, preferred_element_type=F32)
    parts = [
        wide[:, i * DEPTH : (i + 1) * DEPTH].reshape(n, 1, TOK // 2, DEPTH) for i in range(4)
    ]
    top = jnp.concatenate(parts[:2], 1).reshape(n * TOK, DEPTH)
    total = jnp.concatenate(parts[2:], 1).reshape(n * TOK, DEPTH)
    return top, total


def local_kernel(q_ref, kv_ref, out_ref):
    n = GROUP * TOK
    row = lax.broadcasted_iota(jnp.int32, (n, n), 0)
    col = lax.broadcasted_iota(jnp.int32, (n, n), 1)
    same = row // TOK == col // TOK

    for g in range(HEADS // GROUP):
        heads = range(g * GROUP, (g + 1) * GROUP)
        query, key, value = (
            jnp.concatenate([ref[i, :, h * DEPTH : (h + 1) * DEPTH] for h in heads], 0)
            for ref, i in ((q_ref, 0), (kv_ref, 0), (kv_ref, 1))
        )
        score = jnp.where(same, dot_t(query, key), -jnp.inf)
        top = jnp.max(score, axis=1, keepdims=True)
        weight = jnp.exp2((score - top) * FACTOR)
        total = jnp.sum(weight, axis=1, keepdims=True)
        summed = jnp.dot(weight.astype(BF16), value, preferred_element_type=F32)
        here = slice(g * GROUP, (g + 1) * GROUP)
        out_ref[here, 0:TOK] = (summed / total).astype(BF16).reshape(GROUP, TOK, DEPTH)
        out_ref[here, TOK:] = write_stats(top, total)


def own_half_kernel(x_ref, sum_ref, top_ref, total_ref):
    keys = x_ref[:, 2 * TOK : 3 * TOK, :].reshape(NEAR, DEPTH)
    values = x_ref[:, 3 * TOK :, :].reshape(NEAR, DEPTH)
    row = lax.broadcasted_iota(jnp.int32, (BLOCK, BLOCK), 0)
    col = lax.broadcasted_iota(jnp.int32, (BLOCK, BLOCK), 1)
    same = row // TOK == col // TOK
    for step in range(2):
        for i in range(NEAR // BLOCK):
            patches = slice(i * BLOCK // TOK, (i + 1) * BLOCK // TOK)
            query = x_ref[patches, step * TOK : (step + 1) * TOK, :].reshape(BLOCK, DEPTH)
            score = dot_t(query, keys)
            if step == 1:
                near = jnp.where(same, -jnp.inf, score[:, i * BLOCK : (i + 1) * BLOCK])
                parts = [score[:, : i * BLOCK], near, score[:, (i + 1) * BLOCK :]]
                score = jnp.concatenate([p for p in parts if p.shape[1]], axis=1)
            top = jnp.max(score, axis=1, keepdims=True)
            weight = jnp.exp2((score - top) * FACTOR)
            here = slice(step * NEAR + i * BLOCK, step * NEAR + (i + 1) * BLOCK)
            sum_ref[here] = jnp.dot(weight.astype(BF16), values, preferred_element_type=F32)
            top_ref[here] = top
            total_ref[here] = jnp.sum(weight, axis=1, keepdims=True)


def other_half_kernel(x_ref, other_ref, sum_ref, top_ref, total_ref, out_ref):
    keys = other_ref[:, 0:TOK, :].reshape(NEAR, DEPTH)
    values = other_ref[:, TOK:, :].reshape(NEAR, DEPTH)
    lower = lax.broadcasted_iota(jnp.int32, (BLOCK, DEPTH), 1) < HALF
    n = BLOCK // TOK
    for i in range(NEAR // BLOCK):
        patches = slice(i * n, (i + 1) * n)
        attn = []
        for step in range(2):
            query = x_ref[patches, step * TOK : (step + 1) * TOK, :].reshape(BLOCK, DEPTH)
            score = dot_t(query, keys)
            here = slice(step * NEAR + i * BLOCK, step * NEAR + (i + 1) * BLOCK)
            old_top = top_ref[here]
            top = jnp.maximum(jnp.max(score, axis=1, keepdims=True), old_top)
            weight = jnp.exp2((score - top) * FACTOR)
            old = jnp.exp2((old_top - top) * FACTOR)
            total = jnp.sum(weight, axis=1, keepdims=True) + old * total_ref[here]
            summed = jnp.dot(weight.astype(BF16), values, preferred_element_type=F32)
            attn.append((summed + old * sum_ref[here]) / total)
        first, second = attn
        chunks = (
            jnp.where(lower, first, pltpu.roll(second, HALF, 1)),
            jnp.where(lower, pltpu.roll(first, HALF, 1), second),
        )
        stats = write_stats(top, total)
        for core, chunk in enumerate(chunks):
            at = slice(core * HEADS + i * n, core * HEADS + (i + 1) * n)
            out_ref[at, 0:TOK] = chunk.astype(BF16).reshape(n, TOK, DEPTH)
            out_ref[at, TOK:] = stats


def merge_kernel(y_ref, near_ref, gate_ref, out_ref, held):
    upper = lax.axis_index("cfg") == 1
    lower = lax.broadcasted_iota(jnp.int32, (NEAR, DEPTH), 1) < HALF

    def branch(b):
        heads = slice(b * HEADS, (b + 1) * HEADS)
        far = y_ref[heads, 0:TOK].astype(F32).reshape(NEAR, DEPTH)
        near = near_ref[b, :, 0:TOK].astype(F32).reshape(NEAR, DEPTH)
        near = jnp.where(upper, near, pltpu.roll(near, HALF, 1))
        far_top, far_total = read_stats(y_ref[heads, TOK:])
        near_top, near_total = read_stats(near_ref[b, :, TOK:])
        top = jnp.maximum(far_top, near_top)
        far_share = jnp.exp2((far_top - top) * FACTOR) * far_total
        near_share = jnp.exp2((near_top - top) * FACTOR) * near_total
        both = (far_share * far + near_share * near) / (far_share + near_share)
        return jnp.where(lower, far, both).astype(BF16).astype(F32)

    cond = branch(0)
    uncond = branch(1)
    mixed = (uncond + 5.0 * (cond - uncond)).reshape(HEADS, TOK, DEPTH)
    held[...] = (gate_ref[...].reshape(HEADS, 1, DEPTH) * mixed).reshape(NEAR, DEPTH)
    for t in range(TOK):
        rows = held[pl.ds(t, HEADS, stride=TOK), :]
        out_ref[0, t] = rows[:, :HALF].astype(BF16)
        out_ref[1, t] = rows[:, HALF:].astype(BF16)


def call(kernel, out, args, specs=None, scratch=(), flops=0):
    many = isinstance(out, list)
    shapes = out if many else [out]
    moved = sum(a.size * a.dtype.itemsize for a in list(args) + list(shapes))
    vmem = pl.BlockSpec(memory_space=pltpu.VMEM)
    return pl.pallas_call(
        kernel,
        grid=(1,),
        out_shape=out,
        in_specs=specs or [vmem] * len(args),
        out_specs=[vmem] * len(shapes) if many else vmem,
        scratch_shapes=list(scratch),
        cost_estimate=pl.CostEstimate(flops=flops, bytes_accessed=moved, transcendentals=0),
        compiler_params=pltpu.CompilerParams(vmem_limit_bytes=32 << 20),
    )(*args)


def body(queries, keys_values, timesteps, gate_table):
    width = HEADS * DEPTH
    sides = [[SIDES * i + side for i in range(HEADS)] for side in range(SIDES)]
    patches = SIDES * HEADS
    cores = [
        [core * patches + patch for core in range(2) for patch in side] for side in sides
    ]
    whole = pl.BlockSpec(memory_space=pltpu.HBM)
    sent = call(
        pack_kernel,
        SHAPE((HEADS, 4 * TOK, DEPTH), BF16),
        (queries, keys_values),
        [whole, whole],
        [pltpu.VMEM((4, TOK, width), BF16), pltpu.SemaphoreType.DMA((4,))],
    )
    held = lax.all_to_all(
        sent, "patch", split_axis=0, concat_axis=0, tiled=True, axis_index_groups=sides
    )
    near = call(
        local_kernel,
        SHAPE((HEADS, 3 * TOK // 2, DEPTH), BF16),
        (queries, keys_values),
        [
            pl.BlockSpec((None, 1, TOK, width), lambda i: (0, 1, 0, 0)),
            pl.BlockSpec((None, None, 2, TOK, width), lambda i: (0, 1, 0, 0, 0)),
        ],
    )
    near = lax.all_gather(near, "cfg", axis=0, tiled=False)
    gates = jnp.take(gate_table, timesteps, axis=0, mode="clip").reshape(2, HEADS, 2, HALF)
    gate = lax.dynamic_index_in_dim(gates, lax.axis_index("cfg"), 2, keepdims=False)
    gate = jnp.concatenate([gate[0], gate[1]], axis=1)
    other = lax.ppermute(
        held[:, 2 * TOK :, :], "patch", [(i, i ^ 1) for i in range(patches)]
    )
    column = SHAPE((ROWS, 1), F32)
    own = call(
        own_half_kernel,
        [SHAPE((ROWS, DEPTH), F32), column, column],
        (held,),
        flops=4 * ROWS * NEAR * DEPTH,
    )
    far = call(
        other_half_kernel,
        SHAPE((2 * HEADS, 3 * TOK // 2, DEPTH), BF16),
        (held, other, *own),
        flops=4 * ROWS * NEAR * DEPTH,
    )
    back = lax.all_to_all(
        far, ("cfg", "patch"), split_axis=0, concat_axis=0, tiled=True, axis_index_groups=cores
    )
    return call(
        merge_kernel,
        SHAPE((2, TOK, HEADS, HALF), BF16),
        (back, near, gate),
        scratch=[pltpu.VMEM((NEAR, DEPTH), F32)],
    )


def solution(mesh):
    placed = (
        P("cfg", None, ("clip", "patch"), None),
        P("cfg", None, None, ("clip", "patch"), None),
        P("clip"),
        P(),
    )
    return jax.shard_map(
        body,
        mesh=mesh,
        in_specs=placed,
        out_specs=P(None, ("clip", "patch"), None, "cfg"),
        check_vma=False,
    )
```

```python
import math

import jax
import jax.numpy as jnp
from jax import lax
from jax.experimental import pallas as pl
from jax.experimental.pallas import tpu as pltpu
from jax.sharding import PartitionSpec as P

HEADS = 32
DEPTH = 128
HALF = DEPTH // 2
TOK = 16
SIDES = 2
NEAR = HEADS * TOK
ROWS = 2 * NEAR
PAIRS = TOK // 2
SLOTS = DEPTH // TOK
GROUP = 8
BLOCK = 256
FACTOR = math.log2(math.e) / math.sqrt(DEPTH)
BF16 = jnp.bfloat16
F32 = jnp.float32
SHAPE = jax.ShapeDtypeStruct


def dot_t(a, b):
    return lax.dot_general(a, b, (((1,), (1,)), ((), ())), preferred_element_type=F32)


def pack_kernel(q_ref, kv_ref, out_ref, held, sems):
    fields = [q_ref.at[0, 0], q_ref.at[0, 1], kv_ref.at[0, 0, 0], kv_ref.at[0, 0, 1]]
    copies = [
        pltpu.make_async_copy(field, held.at[i], sems.at[i]) for i, field in enumerate(fields)
    ]
    for copy in copies:
        copy.start()
    for i, copy in enumerate(copies):
        copy.wait()
        for h in range(HEADS):
            out_ref[h, i * TOK : (i + 1) * TOK, :] = held[i, :, h * DEPTH : (h + 1) * DEPTH]


def split_value(value):
    high = value.astype(BF16).astype(F32)
    rest = value - high
    mid = rest.astype(BF16).astype(F32)
    return high, mid, rest - mid


def write_stats(top, total):
    rows = top.shape[0]
    n = rows // TOK
    lane = lax.broadcasted_iota(jnp.int32, (rows, DEPTH), 1)
    token = lax.broadcasted_iota(jnp.int32, (rows, DEPTH), 0) % TOK
    slot = jnp.where(lane // SLOTS == token, lane % SLOTS, SLOTS)
    value = jnp.where(slot < 3, top, total)
    high, mid, low = split_value(value)
    piece = jnp.where(slot % 3 == 0, high, jnp.where(slot % 3 == 1, mid, low))
    piece = jnp.where(slot < 6, piece, 0.0).astype(BF16)
    out_row = lax.broadcasted_iota(jnp.int32, (2 * n, rows), 0)
    in_row = lax.broadcasted_iota(jnp.int32, (2 * n, rows), 1)
    gather = jnp.where(out_row == in_row // TOK * 2, 1.0, 0.0).astype(BF16)
    return jnp.dot(gather, piece, preferred_element_type=F32).reshape(n, 2, DEPTH).astype(BF16)


def read_stats(stats):
    n = stats.shape[0]
    out_row = lax.broadcasted_iota(jnp.int32, (n * TOK, 2 * n), 0)
    in_row = lax.broadcasted_iota(jnp.int32, (n * TOK, 2 * n), 1)
    spread = jnp.where(in_row == out_row // TOK * 2, 1.0, 0.0).astype(BF16)
    flat = stats.astype(F32).reshape(2 * n, DEPTH).astype(BF16)
    wide = jnp.dot(spread, flat, preferred_element_type=F32)
    lane = lax.broadcasted_iota(jnp.int32, (n * TOK, DEPTH), 1)
    token = lax.broadcasted_iota(jnp.int32, (n * TOK, DEPTH), 0) % TOK
    wide = jnp.where(lane // SLOTS == token, wide, 0.0).astype(BF16)
    slot = lax.broadcasted_iota(jnp.int32, (DEPTH, 2 * DEPTH), 0) % SLOTS
    part = lax.broadcasted_iota(jnp.int32, (DEPTH, 2 * DEPTH), 1) // DEPTH
    pick = jnp.where(jnp.logical_and(slot < 6, slot // 3 == part), 1.0, 0.0).astype(BF16)
    both = jnp.dot(wide, pick, preferred_element_type=F32)
    return both[:, :DEPTH], both[:, DEPTH:]


def write_rows(rows):
    return rows.reshape(-1, TOK // 2, 2, DEPTH).astype(BF16)


def read_rows(pairs):
    return pairs.astype(F32).reshape(-1, DEPTH)


def local_kernel(q_ref, kv_ref, out_ref):
    n = GROUP * TOK
    row = lax.broadcasted_iota(jnp.int32, (n, n), 0)
    col = lax.broadcasted_iota(jnp.int32, (n, n), 1)
    same = row // TOK == col // TOK

    for g in range(HEADS // GROUP):
        heads = range(g * GROUP, (g + 1) * GROUP)
        query, key, value = (
            jnp.concatenate([ref[i, :, h * DEPTH : (h + 1) * DEPTH] for h in heads], 0)
            for ref, i in ((q_ref, 0), (kv_ref, 0), (kv_ref, 1))
        )
        score = jnp.where(same, dot_t(query, key), -jnp.inf)
        top = jnp.max(score, axis=1, keepdims=True)
        weight = jnp.exp2((score - top) * FACTOR)
        total = jnp.sum(weight, axis=1, keepdims=True)
        summed = jnp.dot(weight.astype(BF16), value, preferred_element_type=F32)
        here = slice(g * GROUP, (g + 1) * GROUP)
        out_ref[here, 0:PAIRS] = write_rows(summed / total)
        out_ref[here, PAIRS] = write_stats(top, total)


def attend_kernel(x_ref, kv_ref, out_ref):
    side = lax.axis_index("patch") % SIDES
    row = lax.broadcasted_iota(jnp.int32, (BLOCK, BLOCK), 0)
    col = lax.broadcasted_iota(jnp.int32, (BLOCK, BLOCK), 1)
    same = row // TOK == col // TOK
    lower = lax.broadcasted_iota(jnp.int32, (BLOCK, DEPTH), 1) < HALF
    n = BLOCK // TOK
    for i in range(NEAR // BLOCK):
        patches = slice(i * n, (i + 1) * n)
        attn = []
        for step in range(2):
            query = x_ref[patches, step * TOK : (step + 1) * TOK, :].reshape(BLOCK, DEPTH)
            scores = []
            for half in range(SIDES):
                score = dot_t(query, kv_ref[half, :, 0:TOK, :].reshape(NEAR, DEPTH))
                if step == 1:
                    own = jnp.logical_and(same, side == half)
                    near = jnp.where(own, -jnp.inf, score[:, i * BLOCK : (i + 1) * BLOCK])
                    parts = [score[:, : i * BLOCK], near, score[:, (i + 1) * BLOCK :]]
                    score = jnp.concatenate([p for p in parts if p.shape[1]], axis=1)
                scores.append(score)
            tops = [jnp.max(score, axis=1, keepdims=True) for score in scores]
            top = jnp.maximum(tops[0], tops[1])
            total, summed = 0.0, 0.0
            for half in range(SIDES):
                weight = jnp.exp2((scores[half] - top) * FACTOR)
                total += jnp.sum(weight, axis=1, keepdims=True)
                values = kv_ref[half, :, TOK:, :].reshape(NEAR, DEPTH)
                summed += jnp.dot(weight.astype(BF16), values, preferred_element_type=F32)
            attn.append(summed / total)
        first, second = attn
        chunks = (
            jnp.where(lower, first, pltpu.roll(second, HALF, 1)),
            jnp.where(lower, pltpu.roll(first, HALF, 1), second),
        )
        stats = write_stats(top, total)
        for core, chunk in enumerate(chunks):
            at = slice(core * HEADS + i * n, core * HEADS + (i + 1) * n)
            out_ref[at, 0:PAIRS] = write_rows(chunk)
            out_ref[at, PAIRS] = stats


def merge_kernel(y_ref, near_ref, gate_ref, out_ref, held):
    upper = lax.axis_index("cfg") == 1
    lower = lax.broadcasted_iota(jnp.int32, (NEAR, DEPTH), 1) < HALF

    def branch(b):
        heads = slice(b * HEADS, (b + 1) * HEADS)
        far = read_rows(y_ref[heads, 0:PAIRS])
        near = read_rows(near_ref[b, :, 0:PAIRS])
        near = jnp.where(upper, near, pltpu.roll(near, HALF, 1))
        far_top, far_total = read_stats(y_ref[heads, PAIRS])
        near_top, near_total = read_stats(near_ref[b, :, PAIRS])
        top = jnp.maximum(far_top, near_top)
        far_share = jnp.exp2((far_top - top) * FACTOR) * far_total
        near_share = jnp.exp2((near_top - top) * FACTOR) * near_total
        both = (far_share * far + near_share * near) / (far_share + near_share)
        return jnp.where(lower, far, both).astype(BF16).astype(F32)

    cond = branch(0)
    uncond = branch(1)
    mixed = (uncond + 5.0 * (cond - uncond)).reshape(HEADS, TOK, DEPTH)
    held[...] = (gate_ref[...].reshape(HEADS, 1, DEPTH) * mixed).reshape(NEAR, DEPTH)
    for t in range(TOK):
        rows = held[pl.ds(t, HEADS, stride=TOK), :]
        out_ref[0, t] = rows[:, :HALF].astype(BF16)
        out_ref[1, t] = rows[:, HALF:].astype(BF16)


def call(kernel, out, args, specs=None, scratch=(), flops=0):
    many = isinstance(out, list)
    shapes = out if many else [out]
    moved = sum(a.size * a.dtype.itemsize for a in list(args) + list(shapes))
    vmem = pl.BlockSpec(memory_space=pltpu.VMEM)
    return pl.pallas_call(
        kernel,
        grid=(1,),
        out_shape=out,
        in_specs=specs or [vmem] * len(args),
        out_specs=[vmem] * len(shapes) if many else vmem,
        scratch_shapes=list(scratch),
        cost_estimate=pl.CostEstimate(flops=flops, bytes_accessed=moved, transcendentals=0),
        compiler_params=pltpu.CompilerParams(vmem_limit_bytes=32 << 20),
    )(*args)


def body(queries, keys_values, timesteps, gate_table):
    width = HEADS * DEPTH
    sides = [[SIDES * i + side for i in range(HEADS)] for side in range(SIDES)]
    patches = SIDES * HEADS
    cores = [
        [core * patches + patch for core in range(2) for patch in side] for side in sides
    ]
    whole = pl.BlockSpec(memory_space=pltpu.HBM)
    sent = call(
        pack_kernel,
        SHAPE((HEADS, 4 * TOK, DEPTH), BF16),
        (queries, keys_values),
        [whole, whole],
        [pltpu.VMEM((4, TOK, width), BF16), pltpu.SemaphoreType.DMA((4,))],
    )
    held = lax.all_to_all(
        sent, "patch", split_axis=0, concat_axis=0, tiled=True, axis_index_groups=sides
    )
    near = call(
        local_kernel,
        SHAPE((HEADS, PAIRS + 1, 2, DEPTH), BF16),
        (queries, keys_values),
        [
            pl.BlockSpec((None, 1, TOK, width), lambda i: (0, 1, 0, 0)),
            pl.BlockSpec((None, None, 2, TOK, width), lambda i: (0, 1, 0, 0, 0)),
        ],
    )
    near = lax.all_gather(near, "cfg", axis=0, tiled=False)
    gates = jnp.take(gate_table, timesteps, axis=0, mode="clip").reshape(2, HEADS, 2, HALF)
    gate = lax.dynamic_index_in_dim(gates, lax.axis_index("cfg"), 2, keepdims=False)
    gate = jnp.concatenate([gate[0], gate[1]], axis=1)
    held, near, gate = lax.optimization_barrier((held, near, gate))
    pairs = [[SIDES * i, SIDES * i + 1] for i in range(HEADS)]
    stale = lax.all_gather(
        held[:, 2 * TOK :, :], "patch", axis=0, tiled=False, axis_index_groups=pairs
    )
    far = call(
        attend_kernel,
        SHAPE((2 * HEADS, PAIRS + 1, 2, DEPTH), BF16),
        (held, stale),
        flops=8 * ROWS * NEAR * DEPTH,
    )
    back = lax.all_to_all(
        far, ("cfg", "patch"), split_axis=0, concat_axis=0, tiled=True, axis_index_groups=cores
    )
    return call(
        merge_kernel,
        SHAPE((2, TOK, HEADS, HALF), BF16),
        (back, near, gate),
        scratch=[pltpu.VMEM((NEAR, DEPTH), F32)],
    )


def solution(mesh):
    placed = (
        P("cfg", None, ("clip", "patch"), None),
        P("cfg", None, None, ("clip", "patch"), None),
        P("clip"),
        P(),
    )
    return jax.shard_map(
        body,
        mesh=mesh,
        in_specs=placed,
        out_specs=P(None, ("clip", "patch"), None, "cfg"),
        check_vma=False,
    )
```

```python
import math

import jax
import jax.numpy as jnp
from jax import lax
from jax.experimental import pallas as pl
from jax.experimental.pallas import tpu as pltpu
from jax.sharding import PartitionSpec as P

HEADS = 32
DEPTH = 128
HALF = DEPTH // 2
TOK = 16
SIDES = 2
NEAR = HEADS * TOK
ROWS = 2 * NEAR
PAIRS = TOK // 2
SLOTS = DEPTH // TOK
GROUP = 8
TOKENS = SIDES * NEAR
BLOCK = 128
FACTOR = math.log2(math.e) / math.sqrt(DEPTH)
BF16 = jnp.bfloat16
F32 = jnp.float32
SHAPE = jax.ShapeDtypeStruct


def dot_t(a, b):
    return lax.dot_general(a, b, (((1,), (1,)), ((), ())), preferred_element_type=F32)


def pack_kernel(q_ref, kv_ref, out_ref, held, packed, in_sems, out_sems):
    fields = [q_ref.at[0, 0], q_ref.at[0, 1], kv_ref.at[0, 0, 0], kv_ref.at[0, 0, 1]]
    copies = [
        pltpu.make_async_copy(field, held.at[i], in_sems.at[i]) for i, field in enumerate(fields)
    ]
    for copy in copies:
        copy.start()
    results = []
    for i, copy in enumerate(copies):
        copy.wait()
        for h in range(HEADS):
            packed[i, h] = held[i, :, h * DEPTH : (h + 1) * DEPTH]
        rows = out_ref.at[:, i * TOK : (i + 1) * TOK, :]
        results.append(pltpu.make_async_copy(packed.at[i], rows, out_sems.at[i]))
        results[-1].start()
    for result in results:
        result.wait()


def split_value(value):
    high = value.astype(BF16).astype(F32)
    rest = value - high
    mid = rest.astype(BF16).astype(F32)
    return high, mid, rest - mid


def write_stats(top, total):
    rows = top.shape[0]
    n = rows // TOK
    lane = lax.broadcasted_iota(jnp.int32, (rows, DEPTH), 1)
    token = lax.broadcasted_iota(jnp.int32, (rows, DEPTH), 0) % TOK
    slot = jnp.where(lane // SLOTS == token, lane % SLOTS, SLOTS)
    value = jnp.where(slot < 3, top, total)
    high, mid, low = split_value(value)
    piece = jnp.where(slot % 3 == 0, high, jnp.where(slot % 3 == 1, mid, low))
    piece = jnp.where(slot < 6, piece, 0.0).astype(BF16)
    out_row = lax.broadcasted_iota(jnp.int32, (2 * n, rows), 0)
    in_row = lax.broadcasted_iota(jnp.int32, (2 * n, rows), 1)
    gather = jnp.where(out_row == in_row // TOK * 2, 1.0, 0.0).astype(BF16)
    return jnp.dot(gather, piece, preferred_element_type=F32).reshape(n, 2, DEPTH).astype(BF16)


def read_stats(stats):
    n = stats.shape[0]
    out_row = lax.broadcasted_iota(jnp.int32, (n * TOK, 2 * n), 0)
    in_row = lax.broadcasted_iota(jnp.int32, (n * TOK, 2 * n), 1)
    spread = jnp.where(in_row == out_row // TOK * 2, 1.0, 0.0).astype(BF16)
    flat = stats.astype(F32).reshape(2 * n, DEPTH).astype(BF16)
    wide = jnp.dot(spread, flat, preferred_element_type=F32)
    lane = lax.broadcasted_iota(jnp.int32, (n * TOK, DEPTH), 1)
    token = lax.broadcasted_iota(jnp.int32, (n * TOK, DEPTH), 0) % TOK
    wide = jnp.where(lane // SLOTS == token, wide, 0.0).astype(BF16)
    slot = lax.broadcasted_iota(jnp.int32, (DEPTH, 2 * DEPTH), 0) % SLOTS
    part = lax.broadcasted_iota(jnp.int32, (DEPTH, 2 * DEPTH), 1) // DEPTH
    pick = jnp.where(jnp.logical_and(slot < 6, slot // 3 == part), 1.0, 0.0).astype(BF16)
    both = jnp.dot(wide, pick, preferred_element_type=F32)
    return both[:, :DEPTH], both[:, DEPTH:]


def write_rows(rows):
    return rows.reshape(-1, TOK // 2, 2, DEPTH).astype(BF16)


def read_rows(pairs):
    return pairs.astype(F32).reshape(-1, DEPTH)


def local_kernel(q_ref, kv_ref, out_ref):
    n = GROUP * TOK
    row = lax.broadcasted_iota(jnp.int32, (n, n), 0)
    col = lax.broadcasted_iota(jnp.int32, (n, n), 1)
    same = row // TOK == col // TOK

    for g in range(HEADS // GROUP):
        heads = range(g * GROUP, (g + 1) * GROUP)
        query, key, value = (
            jnp.concatenate([ref[i, :, h * DEPTH : (h + 1) * DEPTH] for h in heads], 0)
            for ref, i in ((q_ref, 0), (kv_ref, 0), (kv_ref, 1))
        )
        score = jnp.where(same, dot_t(query, key), -jnp.inf)
        top = jnp.max(score, axis=1, keepdims=True)
        weight = jnp.exp2((score - top) * FACTOR)
        total = jnp.sum(weight, axis=1, keepdims=True)
        summed = jnp.dot(weight.astype(BF16), value, preferred_element_type=F32)
        here = slice(g * GROUP, (g + 1) * GROUP)
        out_ref[here, 0:PAIRS] = write_rows(summed / total)
        out_ref[here, PAIRS] = write_stats(top, total)


def attend_kernel(x_ref, kv_ref, out_ref, score, weight, top, total):
    side = lax.axis_index("patch") % SIDES
    row = lax.broadcasted_iota(jnp.int32, (BLOCK, BLOCK), 0)
    col = lax.broadcasted_iota(jnp.int32, (BLOCK, BLOCK), 1)
    same = row // TOK == col // TOK
    lower = lax.broadcasted_iota(jnp.int32, (BLOCK, DEPTH), 1) < HALF
    n = BLOCK // TOK
    steps = [slice(step * NEAR, (step + 1) * NEAR) for step in range(2)]
    for step in range(2):
        query = x_ref[:, step * TOK : (step + 1) * TOK, :].reshape(NEAR, DEPTH)
        for half in range(SIDES):
            keys = kv_ref[half, :, 0:TOK, :].reshape(NEAR, DEPTH)
            score[steps[step], half * NEAR : (half + 1) * NEAR] = dot_t(query, keys)
    for step in range(2):
        for i in range(NEAR // BLOCK):
            here = slice(step * NEAR + i * BLOCK, step * NEAR + (i + 1) * BLOCK)
            if step == 1:
                for half in range(SIDES):
                    cols = slice(half * NEAR + i * BLOCK, half * NEAR + (i + 1) * BLOCK)
                    own = jnp.logical_and(same, side == half)
                    score[here, cols] = jnp.where(own, -jnp.inf, score[here, cols])
            block = score[here]
            most = jnp.max(block, axis=1, keepdims=True)
            weights = jnp.exp2((block - most) * FACTOR)
            added = jnp.sum(weights, axis=1, keepdims=True)
            top[here] = jnp.broadcast_to(most, (BLOCK, DEPTH))
            total[here] = jnp.broadcast_to(added, (BLOCK, DEPTH))
            weight[here] = weights.astype(BF16)
    values = kv_ref[:, :, TOK:, :].reshape(TOKENS, DEPTH)
    attn = score.at[:, 0:DEPTH]
    for step in range(2):
        attn[steps[step]] = jnp.dot(weight[steps[step]], values, preferred_element_type=F32)
    for i in range(NEAR // BLOCK):
        zero = slice(i * BLOCK, (i + 1) * BLOCK)
        one = slice(NEAR + i * BLOCK, NEAR + (i + 1) * BLOCK)
        first = attn[zero] / total[zero]
        second = attn[one] / total[one]
        chunks = (
            jnp.where(lower, first, pltpu.roll(second, HALF, 1)),
            jnp.where(lower, pltpu.roll(first, HALF, 1), second),
        )
        stats = write_stats(top[one], total[one])
        for core, chunk in enumerate(chunks):
            at = slice(core * HEADS + i * n, core * HEADS + (i + 1) * n)
            out_ref[at, 0:PAIRS] = write_rows(chunk)
            out_ref[at, PAIRS] = stats


def near_kernel(near_ref, attn_ref, top_ref, total_ref):
    upper = lax.axis_index("cfg") == 1
    for b in range(2):
        near = read_rows(near_ref[b, :, 0:PAIRS])
        attn_ref[b] = jnp.where(upper, near, pltpu.roll(near, HALF, 1))
        top_ref[b], total_ref[b] = read_stats(near_ref[b, :, PAIRS])


def merge_kernel(y_ref, near_ref, top_ref, total_ref, gate_ref, out_ref, held):
    lower = lax.broadcasted_iota(jnp.int32, (NEAR, DEPTH), 1) < HALF

    def branch(b):
        heads = slice(b * HEADS, (b + 1) * HEADS)
        far = read_rows(y_ref[heads, 0:PAIRS])
        far_top, far_total = read_stats(y_ref[heads, PAIRS])
        near_top = top_ref[b]
        top = jnp.maximum(far_top, near_top)
        far_share = jnp.exp2((far_top - top) * FACTOR) * far_total
        near_share = jnp.exp2((near_top - top) * FACTOR) * total_ref[b]
        both = (far_share * far + near_share * near_ref[b]) / (far_share + near_share)
        return jnp.where(lower, far, both).astype(BF16).astype(F32)

    cond = branch(0)
    uncond = branch(1)
    mixed = (uncond + 5.0 * (cond - uncond)).reshape(HEADS, TOK, DEPTH)
    held[...] = (gate_ref[...].reshape(HEADS, 1, DEPTH) * mixed).reshape(NEAR, DEPTH)
    for t in range(TOK):
        rows = held[pl.ds(t, HEADS, stride=TOK), :]
        out_ref[0, t] = rows[:, :HALF].astype(BF16)
        out_ref[1, t] = rows[:, HALF:].astype(BF16)


def call(kernel, out, args, specs=None, scratch=(), flops=0, out_space=pltpu.VMEM, limit=32):
    many = isinstance(out, list)
    shapes = out if many else [out]
    moved = sum(a.size * a.dtype.itemsize for a in list(args) + list(shapes))
    vmem = pl.BlockSpec(memory_space=pltpu.VMEM)
    result = pl.BlockSpec(memory_space=out_space)
    return pl.pallas_call(
        kernel,
        grid=(1,),
        out_shape=out,
        in_specs=specs or [vmem] * len(args),
        out_specs=[result] * len(shapes) if many else result,
        scratch_shapes=list(scratch),
        cost_estimate=pl.CostEstimate(flops=flops, bytes_accessed=moved, transcendentals=0),
        compiler_params=pltpu.CompilerParams(vmem_limit_bytes=limit << 20),
    )(*args)


def body(queries, keys_values, timesteps, gate_table):
    width = HEADS * DEPTH
    sides = [[SIDES * i + side for i in range(HEADS)] for side in range(SIDES)]
    patches = SIDES * HEADS
    cores = [
        [core * patches + patch for core in range(2) for patch in side] for side in sides
    ]
    whole = pl.BlockSpec(memory_space=pltpu.HBM)
    sent = call(
        pack_kernel,
        SHAPE((HEADS, 4 * TOK, DEPTH), BF16),
        (queries, keys_values),
        [whole, whole],
        [
            pltpu.VMEM((4, TOK, width), BF16),
            pltpu.VMEM((4, HEADS, TOK, DEPTH), BF16),
            pltpu.SemaphoreType.DMA((4,)),
            pltpu.SemaphoreType.DMA((4,)),
        ],
        out_space=pltpu.HBM,
        limit=60,
    )
    held = lax.all_to_all(
        sent, "patch", split_axis=0, concat_axis=0, tiled=True, axis_index_groups=sides
    )
    near = call(
        local_kernel,
        SHAPE((HEADS, PAIRS + 1, 2, DEPTH), BF16),
        (queries, keys_values),
        [
            pl.BlockSpec((None, 1, TOK, width), lambda i: (0, 1, 0, 0)),
            pl.BlockSpec((None, None, 2, TOK, width), lambda i: (0, 1, 0, 0, 0)),
        ],
    )
    near = lax.all_gather(near, "cfg", axis=0, tiled=False)
    near = call(near_kernel, [SHAPE((2, NEAR, DEPTH), F32)] * 3, (near,))
    gates = jnp.take(gate_table, timesteps, axis=0, mode="clip").reshape(2, HEADS, 2, HALF)
    gate = lax.dynamic_index_in_dim(gates, lax.axis_index("cfg"), 2, keepdims=False)
    gate = jnp.concatenate([gate[0], gate[1]], axis=1)
    held, near, gate = lax.optimization_barrier((held, near, gate))
    pairs = [[SIDES * i, SIDES * i + 1] for i in range(HEADS)]
    stale = lax.all_gather(
        held[:, 2 * TOK :, :], "patch", axis=0, tiled=False, axis_index_groups=pairs
    )
    far = call(
        attend_kernel,
        SHAPE((2 * HEADS, PAIRS + 1, 2, DEPTH), BF16),
        (held, stale),
        scratch=[
            pltpu.VMEM((ROWS, TOKENS), F32),
            pltpu.VMEM((ROWS, TOKENS), BF16),
            pltpu.VMEM((ROWS, DEPTH), F32),
            pltpu.VMEM((ROWS, DEPTH), F32),
        ],
        flops=4 * ROWS * TOKENS * DEPTH,
    )
    back = lax.all_to_all(
        far, ("cfg", "patch"), split_axis=0, concat_axis=0, tiled=True, axis_index_groups=cores
    )
    return call(
        merge_kernel,
        SHAPE((2, TOK, HEADS, HALF), BF16),
        (back, *near, gate),
        scratch=[pltpu.VMEM((NEAR, DEPTH), F32)],
    )


def solution(mesh):
    placed = (
        P("cfg", None, ("clip", "patch"), None),
        P("cfg", None, None, ("clip", "patch"), None),
        P("clip"),
        P(),
    )
    return jax.shard_map(
        body,
        mesh=mesh,
        in_specs=placed,
        out_specs=P(None, ("clip", "patch"), None, "cfg"),
        check_vma=False,
    )
```

```python
import math

import jax
import jax.numpy as jnp
from jax import lax
from jax.experimental import pallas as pl
from jax.experimental.pallas import tpu as pltpu
from jax.sharding import PartitionSpec as P

HEADS = 32
DEPTH = 128
HALF = DEPTH // 2
TOK = 16
SIDES = 2
NEAR = HEADS * TOK
ROWS = 2 * NEAR
PAIRS = TOK // 2
SLOTS = DEPTH // TOK
GROUP = 8
TOKENS = SIDES * NEAR
BLOCK = 128
FACTOR = math.log2(math.e) / math.sqrt(DEPTH)
BF16 = jnp.bfloat16
F32 = jnp.float32
SHAPE = jax.ShapeDtypeStruct


def dot_t(a, b):
    return lax.dot_general(a, b, (((1,), (1,)), ((), ())), preferred_element_type=F32)


def pack_kernel(q_ref, kv_ref, out_ref, held, packed, in_sems, out_sems):
    fields = [q_ref.at[0, 0], q_ref.at[0, 1], kv_ref.at[0, 0, 0], kv_ref.at[0, 0, 1]]
    copies = [
        pltpu.make_async_copy(field, held.at[i], in_sems.at[i]) for i, field in enumerate(fields)
    ]
    for copy in copies:
        copy.start()
    results = []
    for i, copy in enumerate(copies):
        copy.wait()
        for h in range(HEADS):
            packed[i, h] = held[i, :, h * DEPTH : (h + 1) * DEPTH]
        rows = out_ref.at[:, i * TOK : (i + 1) * TOK, :]
        results.append(pltpu.make_async_copy(packed.at[i], rows, out_sems.at[i]))
        results[-1].start()
    for result in results:
        result.wait()


def split_value(value):
    high = value.astype(BF16).astype(F32)
    rest = value - high
    mid = rest.astype(BF16).astype(F32)
    return high, mid, rest - mid


def write_stats(top, total):
    rows = top.shape[0]
    n = rows // TOK
    lane = lax.broadcasted_iota(jnp.int32, (rows, DEPTH), 1)
    token = lax.broadcasted_iota(jnp.int32, (rows, DEPTH), 0) % TOK
    slot = jnp.where(lane // SLOTS == token, lane % SLOTS, SLOTS)
    value = jnp.where(slot < 3, top, total)
    high, mid, low = split_value(value)
    piece = jnp.where(slot % 3 == 0, high, jnp.where(slot % 3 == 1, mid, low))
    piece = jnp.where(slot < 6, piece, 0.0).astype(BF16)
    out_row = lax.broadcasted_iota(jnp.int32, (2 * n, rows), 0)
    in_row = lax.broadcasted_iota(jnp.int32, (2 * n, rows), 1)
    gather = jnp.where(out_row == in_row // TOK * 2, 1.0, 0.0).astype(BF16)
    return jnp.dot(gather, piece, preferred_element_type=F32).reshape(n, 2, DEPTH).astype(BF16)


def read_stats(stats):
    n = stats.shape[0]
    out_row = lax.broadcasted_iota(jnp.int32, (n * TOK, 2 * n), 0)
    in_row = lax.broadcasted_iota(jnp.int32, (n * TOK, 2 * n), 1)
    spread = jnp.where(in_row == out_row // TOK * 2, 1.0, 0.0).astype(BF16)
    flat = stats.astype(F32).reshape(2 * n, DEPTH).astype(BF16)
    wide = jnp.dot(spread, flat, preferred_element_type=F32)
    lane = lax.broadcasted_iota(jnp.int32, (n * TOK, DEPTH), 1)
    token = lax.broadcasted_iota(jnp.int32, (n * TOK, DEPTH), 0) % TOK
    wide = jnp.where(lane // SLOTS == token, wide, 0.0).astype(BF16)
    slot = lax.broadcasted_iota(jnp.int32, (DEPTH, 2 * DEPTH), 0) % SLOTS
    part = lax.broadcasted_iota(jnp.int32, (DEPTH, 2 * DEPTH), 1) // DEPTH
    pick = jnp.where(jnp.logical_and(slot < 6, slot // 3 == part), 1.0, 0.0).astype(BF16)
    both = jnp.dot(wide, pick, preferred_element_type=F32)
    return both[:, :DEPTH], both[:, DEPTH:]


def write_rows(rows):
    return rows.reshape(-1, TOK // 2, 2, DEPTH).astype(BF16)


def read_rows(pairs):
    return pairs.astype(F32).reshape(-1, DEPTH)


def local_kernel(q_ref, kv_ref, out_ref):
    n = GROUP * TOK
    row = lax.broadcasted_iota(jnp.int32, (n, n), 0)
    col = lax.broadcasted_iota(jnp.int32, (n, n), 1)
    same = row // TOK == col // TOK

    for g in range(HEADS // GROUP):
        heads = range(g * GROUP, (g + 1) * GROUP)
        query, key, value = (
            jnp.concatenate([ref[i, :, h * DEPTH : (h + 1) * DEPTH] for h in heads], 0)
            for ref, i in ((q_ref, 0), (kv_ref, 0), (kv_ref, 1))
        )
        score = jnp.where(same, dot_t(query, key), -jnp.inf)
        top = jnp.max(score, axis=1, keepdims=True)
        weight = jnp.exp2((score - top) * FACTOR)
        total = jnp.sum(weight, axis=1, keepdims=True)
        summed = jnp.dot(weight.astype(BF16), value, preferred_element_type=F32)
        here = slice(g * GROUP, (g + 1) * GROUP)
        out_ref[here, 0:PAIRS] = write_rows(summed / total)
        out_ref[here, PAIRS] = write_stats(top, total)


def attend_kernel(x_ref, kv_ref, out_ref, score, weight, top, total):
    side = lax.axis_index("patch") % SIDES
    row = lax.broadcasted_iota(jnp.int32, (BLOCK, BLOCK), 0)
    col = lax.broadcasted_iota(jnp.int32, (BLOCK, BLOCK), 1)
    same = row // TOK == col // TOK
    n = BLOCK // TOK
    steps = [slice(step * NEAR, (step + 1) * NEAR) for step in range(2)]
    for step in range(2):
        query = x_ref[:, step * TOK : (step + 1) * TOK, :].reshape(NEAR, DEPTH)
        for half in range(SIDES):
            keys = kv_ref[half, :, 0:TOK, :].reshape(NEAR, DEPTH)
            score[steps[step], half * NEAR : (half + 1) * NEAR] = dot_t(query, keys)
    for step in range(2):
        for i in range(NEAR // BLOCK):
            here = slice(step * NEAR + i * BLOCK, step * NEAR + (i + 1) * BLOCK)
            if step == 1:
                for half in range(SIDES):
                    cols = slice(half * NEAR + i * BLOCK, half * NEAR + (i + 1) * BLOCK)
                    own = jnp.logical_and(same, side == half)
                    score[here, cols] = jnp.where(own, -jnp.inf, score[here, cols])
            block = score[here]
            most = jnp.max(block, axis=1, keepdims=True)
            weights = jnp.exp2((block - most) * FACTOR)
            added = jnp.sum(weights, axis=1, keepdims=True)
            top[here] = jnp.broadcast_to(most, (BLOCK, DEPTH))
            total[here] = jnp.broadcast_to(added, (BLOCK, DEPTH))
            weight[here] = weights.astype(BF16)
    values = kv_ref[:, :, TOK:, :].reshape(TOKENS, DEPTH)
    for step in range(2):
        rows = steps[step]
        attn = jnp.dot(weight[rows], values, preferred_element_type=F32) / total[rows]
        out_ref[:, step * PAIRS : (step + 1) * PAIRS] = write_rows(attn)
    for i in range(NEAR // BLOCK):
        rows = slice(NEAR + i * BLOCK, NEAR + (i + 1) * BLOCK)
        out_ref[i * n : (i + 1) * n, 2 * PAIRS] = write_stats(top[rows], total[rows])


def near_kernel(near_ref, attn_ref, top_ref, total_ref):
    upper = lax.axis_index("cfg") == 1
    for b in range(2):
        near = read_rows(near_ref[b, :, 0:PAIRS])
        attn_ref[b] = jnp.where(upper, near, pltpu.roll(near, HALF, 1))
        top_ref[b], total_ref[b] = read_stats(near_ref[b, :, PAIRS])


def merge_kernel(y_ref, near_ref, top_ref, total_ref, gate_ref, out_ref, held):
    upper = lax.axis_index("cfg") == 1
    lower = lax.broadcasted_iota(jnp.int32, (NEAR, DEPTH), 1) < HALF

    def branch(b):
        first = read_rows(y_ref[b, :, 0:PAIRS])
        second = read_rows(y_ref[b, :, PAIRS : 2 * PAIRS])
        turned = pltpu.roll(jnp.where(upper, first, second), HALF, 1)
        far = jnp.where(lower, jnp.where(upper, turned, first), jnp.where(upper, second, turned))
        far_top, far_total = read_stats(y_ref[b, :, 2 * PAIRS])
        near_top = top_ref[b]
        top = jnp.maximum(far_top, near_top)
        far_share = jnp.exp2((far_top - top) * FACTOR) * far_total
        near_share = jnp.exp2((near_top - top) * FACTOR) * total_ref[b]
        both = (far_share * far + near_share * near_ref[b]) / (far_share + near_share)
        return jnp.where(lower, far, both).astype(BF16).astype(F32)

    cond = branch(0)
    uncond = branch(1)
    mixed = (uncond + 5.0 * (cond - uncond)).reshape(HEADS, TOK, DEPTH)
    held[...] = (gate_ref[...].reshape(HEADS, 1, DEPTH) * mixed).reshape(NEAR, DEPTH)
    for t in range(TOK):
        rows = held[pl.ds(t, HEADS, stride=TOK), :]
        out_ref[0, t] = rows[:, :HALF].astype(BF16)
        out_ref[1, t] = rows[:, HALF:].astype(BF16)


def call(kernel, out, args, specs=None, scratch=(), flops=0, out_space=pltpu.VMEM, limit=32):
    many = isinstance(out, list)
    shapes = out if many else [out]
    moved = sum(a.size * a.dtype.itemsize for a in list(args) + list(shapes))
    vmem = pl.BlockSpec(memory_space=pltpu.VMEM)
    result = pl.BlockSpec(memory_space=out_space)
    return pl.pallas_call(
        kernel,
        grid=(1,),
        out_shape=out,
        in_specs=specs or [vmem] * len(args),
        out_specs=[result] * len(shapes) if many else result,
        scratch_shapes=list(scratch),
        cost_estimate=pl.CostEstimate(flops=flops, bytes_accessed=moved, transcendentals=0),
        compiler_params=pltpu.CompilerParams(vmem_limit_bytes=limit << 20),
    )(*args)


def body(queries, keys_values, timesteps, gate_table):
    width = HEADS * DEPTH
    sides = [[SIDES * i + side for i in range(HEADS)] for side in range(SIDES)]
    patches = SIDES * HEADS
    whole = pl.BlockSpec(memory_space=pltpu.HBM)
    sent = call(
        pack_kernel,
        SHAPE((HEADS, 4 * TOK, DEPTH), BF16),
        (queries, keys_values),
        [whole, whole],
        [
            pltpu.VMEM((4, TOK, width), BF16),
            pltpu.VMEM((4, HEADS, TOK, DEPTH), BF16),
            pltpu.SemaphoreType.DMA((4,)),
            pltpu.SemaphoreType.DMA((4,)),
        ],
        out_space=pltpu.HBM,
        limit=60,
    )
    held = lax.all_to_all(
        sent, "patch", split_axis=0, concat_axis=0, tiled=True, axis_index_groups=sides
    )
    near = call(
        local_kernel,
        SHAPE((HEADS, PAIRS + 1, 2, DEPTH), BF16),
        (queries, keys_values),
        [
            pl.BlockSpec((None, 1, TOK, width), lambda i: (0, 1, 0, 0)),
            pl.BlockSpec((None, None, 2, TOK, width), lambda i: (0, 1, 0, 0, 0)),
        ],
    )
    near = lax.all_gather(near, "cfg", axis=0, tiled=False)
    near = call(near_kernel, [SHAPE((2, NEAR, DEPTH), F32)] * 3, (near,))
    gates = jnp.take(gate_table, timesteps, axis=0, mode="clip").reshape(2, HEADS, 2, HALF)
    gate = lax.dynamic_index_in_dim(gates, lax.axis_index("cfg"), 2, keepdims=False)
    gate = jnp.concatenate([gate[0], gate[1]], axis=1)
    held, near, gate = lax.optimization_barrier((held, near, gate))
    pairs = [[SIDES * i, SIDES * i + 1] for i in range(HEADS)]
    stale = lax.all_gather(
        held[:, 2 * TOK :, :], "patch", axis=0, tiled=False, axis_index_groups=pairs
    )
    far = call(
        attend_kernel,
        SHAPE((HEADS, 2 * PAIRS + 1, 2, DEPTH), BF16),
        (held, stale),
        scratch=[
            pltpu.VMEM((ROWS, TOKENS), F32),
            pltpu.VMEM((ROWS, TOKENS), BF16),
            pltpu.VMEM((ROWS, DEPTH), F32),
            pltpu.VMEM((ROWS, DEPTH), F32),
        ],
        flops=4 * ROWS * TOKENS * DEPTH,
    )
    back = lax.all_to_all(
        far, "patch", split_axis=0, concat_axis=0, tiled=True, axis_index_groups=sides
    )
    back = lax.all_gather(back, "cfg", axis=0, tiled=False)
    return call(
        merge_kernel,
        SHAPE((2, TOK, HEADS, HALF), BF16),
        (back, *near, gate),
        scratch=[pltpu.VMEM((NEAR, DEPTH), F32)],
    )


def solution(mesh):
    placed = (
        P("cfg", None, ("clip", "patch"), None),
        P("cfg", None, None, ("clip", "patch"), None),
        P("clip"),
        P(),
    )
    return jax.shard_map(
        body,
        mesh=mesh,
        in_specs=placed,
        out_specs=P(None, ("clip", "patch"), None, "cfg"),
        check_vma=False,
    )
```

```python
import math

import jax
import jax.numpy as jnp
from jax import lax
from jax.experimental import pallas as pl
from jax.experimental.pallas import tpu as pltpu
from jax.sharding import PartitionSpec as P

HEADS = 32
DEPTH = 128
HALF = DEPTH // 2
TOK = 16
SIDES = 2
SIDE_STRIDE = 2
NEAR = HEADS * TOK
ROWS = 2 * NEAR
PAIRS = TOK // 2
SLOTS = DEPTH // TOK
GROUP = 8
TOKENS = SIDES * NEAR
BLOCK = 128
FACTOR = math.log2(math.e) / math.sqrt(DEPTH)
BF16 = jnp.bfloat16
F32 = jnp.float32
SHAPE = jax.ShapeDtypeStruct


def dot_t(a, b):
    return lax.dot_general(a, b, (((1,), (1,)), ((), ())), preferred_element_type=F32)


def pack_kernel(q_ref, kv_ref, out_ref, held, packed, in_sems, out_sems):
    fields = [q_ref.at[0, 0], q_ref.at[0, 1], kv_ref.at[0, 0, 0], kv_ref.at[0, 0, 1]]
    copies = [
        pltpu.make_async_copy(field, held.at[i], in_sems.at[i]) for i, field in enumerate(fields)
    ]
    for copy in copies:
        copy.start()
    results = []
    for i, copy in enumerate(copies):
        copy.wait()
        for h in range(HEADS):
            packed[i, h] = held[i, :, h * DEPTH : (h + 1) * DEPTH]
        rows = out_ref.at[:, i * TOK : (i + 1) * TOK, :]
        results.append(pltpu.make_async_copy(packed.at[i], rows, out_sems.at[i]))
        results[-1].start()
    for result in results:
        result.wait()


def split_value(value):
    high = value.astype(BF16).astype(F32)
    rest = value - high
    mid = rest.astype(BF16).astype(F32)
    return high, mid, rest - mid


def write_stats(top, total):
    rows = top.shape[0]
    n = rows // TOK
    lane = lax.broadcasted_iota(jnp.int32, (rows, DEPTH), 1)
    token = lax.broadcasted_iota(jnp.int32, (rows, DEPTH), 0) % TOK
    slot = jnp.where(lane // SLOTS == token, lane % SLOTS, SLOTS)
    value = jnp.where(slot < 3, top, total)
    high, mid, low = split_value(value)
    piece = jnp.where(slot % 3 == 0, high, jnp.where(slot % 3 == 1, mid, low))
    piece = jnp.where(slot < 6, piece, 0.0).astype(BF16)
    out_row = lax.broadcasted_iota(jnp.int32, (2 * n, rows), 0)
    in_row = lax.broadcasted_iota(jnp.int32, (2 * n, rows), 1)
    gather = jnp.where(out_row == in_row // TOK * 2, 1.0, 0.0).astype(BF16)
    return jnp.dot(gather, piece, preferred_element_type=F32).reshape(n, 2, DEPTH).astype(BF16)


def read_stats(stats):
    n = stats.shape[0]
    out_row = lax.broadcasted_iota(jnp.int32, (n * TOK, 2 * n), 0)
    in_row = lax.broadcasted_iota(jnp.int32, (n * TOK, 2 * n), 1)
    spread = jnp.where(in_row == out_row // TOK * 2, 1.0, 0.0).astype(BF16)
    flat = stats.astype(F32).reshape(2 * n, DEPTH).astype(BF16)
    wide = jnp.dot(spread, flat, preferred_element_type=F32)
    lane = lax.broadcasted_iota(jnp.int32, (n * TOK, DEPTH), 1)
    token = lax.broadcasted_iota(jnp.int32, (n * TOK, DEPTH), 0) % TOK
    wide = jnp.where(lane // SLOTS == token, wide, 0.0).astype(BF16)
    slot = lax.broadcasted_iota(jnp.int32, (DEPTH, 2 * DEPTH), 0) % SLOTS
    part = lax.broadcasted_iota(jnp.int32, (DEPTH, 2 * DEPTH), 1) // DEPTH
    pick = jnp.where(jnp.logical_and(slot < 6, slot // 3 == part), 1.0, 0.0).astype(BF16)
    both = jnp.dot(wide, pick, preferred_element_type=F32)
    return both[:, :DEPTH], both[:, DEPTH:]


def write_rows(rows):
    return rows.reshape(-1, TOK // 2, 2, DEPTH).astype(BF16)


def read_rows(pairs):
    return pairs.astype(F32).reshape(-1, DEPTH)


def local_kernel(q_ref, kv_ref, out_ref):
    n = GROUP * TOK
    row = lax.broadcasted_iota(jnp.int32, (n, n), 0)
    col = lax.broadcasted_iota(jnp.int32, (n, n), 1)
    same = row // TOK == col // TOK

    for g in range(HEADS // GROUP):
        heads = range(g * GROUP, (g + 1) * GROUP)
        query, key, value = (
            jnp.concatenate([ref[i, :, h * DEPTH : (h + 1) * DEPTH] for h in heads], 0)
            for ref, i in ((q_ref, 0), (kv_ref, 0), (kv_ref, 1))
        )
        score = jnp.where(same, dot_t(query, key), -jnp.inf)
        top = jnp.max(score, axis=1, keepdims=True)
        weight = jnp.exp2((score - top) * FACTOR)
        total = jnp.sum(weight, axis=1, keepdims=True)
        summed = jnp.dot(weight.astype(BF16), value, preferred_element_type=F32)
        here = slice(g * GROUP, (g + 1) * GROUP)
        out_ref[here, 0:PAIRS] = write_rows(summed / total)
        out_ref[here, PAIRS] = write_stats(top, total)


def attend_kernel(x_ref, kv_ref, out_ref, score, weight, top, total):
    side = lax.axis_index("patch") // SIDE_STRIDE % SIDES
    row = lax.broadcasted_iota(jnp.int32, (BLOCK, BLOCK), 0)
    col = lax.broadcasted_iota(jnp.int32, (BLOCK, BLOCK), 1)
    same = row // TOK == col // TOK
    lower = lax.broadcasted_iota(jnp.int32, (BLOCK, DEPTH), 1) < HALF
    n = BLOCK // TOK
    steps = [slice(step * NEAR, (step + 1) * NEAR) for step in range(2)]
    for step in range(2):
        query = x_ref[:, step * TOK : (step + 1) * TOK, :].reshape(NEAR, DEPTH)
        for half in range(SIDES):
            keys = kv_ref[half, :, 0:TOK, :].reshape(NEAR, DEPTH)
            score[steps[step], half * NEAR : (half + 1) * NEAR] = dot_t(query, keys)
    for step in range(2):
        for i in range(NEAR // BLOCK):
            here = slice(step * NEAR + i * BLOCK, step * NEAR + (i + 1) * BLOCK)
            if step == 1:
                for half in range(SIDES):
                    cols = slice(half * NEAR + i * BLOCK, half * NEAR + (i + 1) * BLOCK)
                    own = jnp.logical_and(same, side == half)
                    score[here, cols] = jnp.where(own, -jnp.inf, score[here, cols])
            block = score[here]
            most = jnp.max(block, axis=1, keepdims=True)
            weights = jnp.exp2((block - most) * FACTOR)
            added = jnp.sum(weights, axis=1, keepdims=True)
            top[here] = jnp.broadcast_to(most, (BLOCK, DEPTH))
            total[here] = jnp.broadcast_to(added, (BLOCK, DEPTH))
            weight[here] = weights.astype(BF16)
    values = kv_ref[:, :, TOK:, :].reshape(TOKENS, DEPTH)
    attn = score.at[:, 0:DEPTH]
    for step in range(2):
        attn[steps[step]] = jnp.dot(weight[steps[step]], values, preferred_element_type=F32)
    for i in range(NEAR // BLOCK):
        zero = slice(i * BLOCK, (i + 1) * BLOCK)
        one = slice(NEAR + i * BLOCK, NEAR + (i + 1) * BLOCK)
        first = attn[zero] / total[zero]
        second = attn[one] / total[one]
        chunks = (
            jnp.where(lower, first, pltpu.roll(second, HALF, 1)),
            jnp.where(lower, pltpu.roll(first, HALF, 1), second),
        )
        stats = write_stats(top[one], total[one])
        for core, chunk in enumerate(chunks):
            at = slice(core * HEADS + i * n, core * HEADS + (i + 1) * n)
            out_ref[at, 0:PAIRS] = write_rows(chunk)
            out_ref[at, PAIRS] = stats


def near_kernel(near_ref, attn_ref, top_ref, total_ref):
    upper = lax.axis_index("cfg") == 1
    for b in range(2):
        near = read_rows(near_ref[b, :, 0:PAIRS])
        attn_ref[b] = jnp.where(upper, near, pltpu.roll(near, HALF, 1))
        top_ref[b], total_ref[b] = read_stats(near_ref[b, :, PAIRS])


def merge_kernel(y_ref, near_ref, top_ref, total_ref, gate_ref, out_ref, held):
    lower = lax.broadcasted_iota(jnp.int32, (NEAR, DEPTH), 1) < HALF

    def branch(b):
        heads = slice(b * HEADS, (b + 1) * HEADS)
        far = read_rows(y_ref[heads, 0:PAIRS])
        far_top, far_total = read_stats(y_ref[heads, PAIRS])
        near_top = top_ref[b]
        top = jnp.maximum(far_top, near_top)
        far_share = jnp.exp2((far_top - top) * FACTOR) * far_total
        near_share = jnp.exp2((near_top - top) * FACTOR) * total_ref[b]
        both = (far_share * far + near_share * near_ref[b]) / (far_share + near_share)
        return jnp.where(lower, far, both).astype(BF16).astype(F32)

    cond = branch(0)
    uncond = branch(1)
    mixed = (uncond + 5.0 * (cond - uncond)).reshape(HEADS, TOK, DEPTH)
    held[...] = (gate_ref[...].reshape(HEADS, 1, DEPTH) * mixed).reshape(NEAR, DEPTH)
    for t in range(TOK):
        rows = held[pl.ds(t, HEADS, stride=TOK), :]
        out_ref[0, t] = rows[:, :HALF].astype(BF16)
        out_ref[1, t] = rows[:, HALF:].astype(BF16)


def call(kernel, out, args, specs=None, scratch=(), flops=0, out_space=pltpu.VMEM, limit=32):
    many = isinstance(out, list)
    shapes = out if many else [out]
    moved = sum(a.size * a.dtype.itemsize for a in list(args) + list(shapes))
    vmem = pl.BlockSpec(memory_space=pltpu.VMEM)
    result = pl.BlockSpec(memory_space=out_space)
    return pl.pallas_call(
        kernel,
        grid=(1,),
        out_shape=out,
        in_specs=specs or [vmem] * len(args),
        out_specs=[result] * len(shapes) if many else result,
        scratch_shapes=list(scratch),
        cost_estimate=pl.CostEstimate(flops=flops, bytes_accessed=moved, transcendentals=0),
        compiler_params=pltpu.CompilerParams(vmem_limit_bytes=limit << 20),
    )(*args)


def body(queries, keys_values, timesteps, gate_table):
    width = HEADS * DEPTH
    patches = SIDES * HEADS
    sides = [
        [p for p in range(patches) if p // SIDE_STRIDE % SIDES == side] for side in range(SIDES)
    ]
    cores = [
        [core * patches + patch for core in range(2) for patch in side] for side in sides
    ]
    whole = pl.BlockSpec(memory_space=pltpu.HBM)
    sent = call(
        pack_kernel,
        SHAPE((HEADS, 4 * TOK, DEPTH), BF16),
        (queries, keys_values),
        [whole, whole],
        [
            pltpu.VMEM((4, TOK, width), BF16),
            pltpu.VMEM((4, HEADS, TOK, DEPTH), BF16),
            pltpu.SemaphoreType.DMA((4,)),
            pltpu.SemaphoreType.DMA((4,)),
        ],
        out_space=pltpu.HBM,
        limit=60,
    )
    held = lax.all_to_all(
        sent, "patch", split_axis=0, concat_axis=0, tiled=True, axis_index_groups=sides
    )
    near = call(
        local_kernel,
        SHAPE((HEADS, PAIRS + 1, 2, DEPTH), BF16),
        (queries, keys_values),
        [
            pl.BlockSpec((None, 1, TOK, width), lambda i: (0, 1, 0, 0)),
            pl.BlockSpec((None, None, 2, TOK, width), lambda i: (0, 1, 0, 0, 0)),
        ],
    )
    near = lax.all_gather(near, "cfg", axis=0, tiled=False)
    near = call(near_kernel, [SHAPE((2, NEAR, DEPTH), F32)] * 3, (near,))
    gates = jnp.take(gate_table, timesteps, axis=0, mode="clip").reshape(2, HEADS, 2, HALF)
    gate = lax.dynamic_index_in_dim(gates, lax.axis_index("cfg"), 2, keepdims=False)
    gate = jnp.concatenate([gate[0], gate[1]], axis=1)
    held, near, gate = lax.optimization_barrier((held, near, gate))
    pairs = [[p, p + SIDE_STRIDE] for p in sides[0]]
    stale = lax.all_gather(
        held[:, 2 * TOK :, :], "patch", axis=0, tiled=False, axis_index_groups=pairs
    )
    far = call(
        attend_kernel,
        SHAPE((2 * HEADS, PAIRS + 1, 2, DEPTH), BF16),
        (held, stale),
        scratch=[
            pltpu.VMEM((ROWS, TOKENS), F32),
            pltpu.VMEM((ROWS, TOKENS), BF16),
            pltpu.VMEM((ROWS, DEPTH), F32),
            pltpu.VMEM((ROWS, DEPTH), F32),
        ],
        flops=4 * ROWS * TOKENS * DEPTH,
    )
    back = lax.all_to_all(
        far, ("cfg", "patch"), split_axis=0, concat_axis=0, tiled=True, axis_index_groups=cores
    )
    return call(
        merge_kernel,
        SHAPE((2, TOK, HEADS, HALF), BF16),
        (back, *near, gate),
        scratch=[pltpu.VMEM((NEAR, DEPTH), F32)],
    )


def solution(mesh):
    placed = (
        P("cfg", None, ("clip", "patch"), None),
        P("cfg", None, None, ("clip", "patch"), None),
        P("clip"),
        P(),
    )
    return jax.shard_map(
        body,
        mesh=mesh,
        in_specs=placed,
        out_specs=P(None, ("clip", "patch"), None, "cfg"),
        check_vma=False,
    )
```

```python
import math

import jax
import jax.numpy as jnp
from jax import lax
from jax.experimental import pallas as pl
from jax.experimental.pallas import tpu as pltpu
from jax.sharding import PartitionSpec as P

HEADS = 32
DEPTH = 128
HALF = DEPTH // 2
TOK = 16
SIDES = 2
NEAR = HEADS * TOK
ROWS = 2 * NEAR
PAIRS = TOK // 2
SLOTS = DEPTH // TOK
GROUP = 8
TOKENS = SIDES * NEAR
BLOCK = 128
FACTOR = math.log2(math.e) / math.sqrt(DEPTH)
BF16 = jnp.bfloat16
F32 = jnp.float32
SHAPE = jax.ShapeDtypeStruct


def dot_t(a, b):
    return lax.dot_general(a, b, (((1,), (1,)), ((), ())), preferred_element_type=F32)


def pack_kernel(q_ref, kv_ref, out_ref, held, packed, in_sems, out_sems):
    fields = [q_ref.at[0, 0], q_ref.at[0, 1], kv_ref.at[0, 0, 0], kv_ref.at[0, 0, 1]]
    loads = [
        pltpu.make_async_copy(field, held.at[i], in_sems.at[i]) for i, field in enumerate(fields)
    ]
    stores = [
        pltpu.make_async_copy(
            packed.at[i], out_ref.at[:, i * TOK : (i + 1) * TOK, :], out_sems.at[i]
        )
        for i in range(len(fields))
    ]

    def by_head(i):
        for h in range(HEADS):
            packed[i, h] = held[i, :, h * DEPTH : (h + 1) * DEPTH]

    odd = lax.axis_index("cfg") == 1

    @pl.when(odd)
    def _():
        for load in loads:
            load.start()
        for i, load in enumerate(loads):
            load.wait()
            by_head(i)
            stores[i].start()
        for store in stores:
            store.wait()

    @pl.when(jnp.logical_not(odd))
    def _():
        for i, load in enumerate(loads):
            load.start()
            load.wait()
            by_head(i)
            stores[i].start()
            stores[i].wait()


def split_value(value):
    high = value.astype(BF16).astype(F32)
    rest = value - high
    mid = rest.astype(BF16).astype(F32)
    return high, mid, rest - mid


def write_stats(top, total):
    rows = top.shape[0]
    n = rows // TOK
    lane = lax.broadcasted_iota(jnp.int32, (rows, DEPTH), 1)
    token = lax.broadcasted_iota(jnp.int32, (rows, DEPTH), 0) % TOK
    slot = jnp.where(lane // SLOTS == token, lane % SLOTS, SLOTS)
    value = jnp.where(slot < 3, top, total)
    high, mid, low = split_value(value)
    piece = jnp.where(slot % 3 == 0, high, jnp.where(slot % 3 == 1, mid, low))
    piece = jnp.where(slot < 6, piece, 0.0).astype(BF16)
    out_row = lax.broadcasted_iota(jnp.int32, (2 * n, rows), 0)
    in_row = lax.broadcasted_iota(jnp.int32, (2 * n, rows), 1)
    gather = jnp.where(out_row == in_row // TOK * 2, 1.0, 0.0).astype(BF16)
    return jnp.dot(gather, piece, preferred_element_type=F32).reshape(n, 2, DEPTH).astype(BF16)


def read_stats(stats):
    n = stats.shape[0]
    out_row = lax.broadcasted_iota(jnp.int32, (n * TOK, 2 * n), 0)
    in_row = lax.broadcasted_iota(jnp.int32, (n * TOK, 2 * n), 1)
    spread = jnp.where(in_row == out_row // TOK * 2, 1.0, 0.0).astype(BF16)
    flat = stats.astype(F32).reshape(2 * n, DEPTH).astype(BF16)
    wide = jnp.dot(spread, flat, preferred_element_type=F32)
    lane = lax.broadcasted_iota(jnp.int32, (n * TOK, DEPTH), 1)
    token = lax.broadcasted_iota(jnp.int32, (n * TOK, DEPTH), 0) % TOK
    wide = jnp.where(lane // SLOTS == token, wide, 0.0).astype(BF16)
    slot = lax.broadcasted_iota(jnp.int32, (DEPTH, 2 * DEPTH), 0) % SLOTS
    part = lax.broadcasted_iota(jnp.int32, (DEPTH, 2 * DEPTH), 1) // DEPTH
    pick = jnp.where(jnp.logical_and(slot < 6, slot // 3 == part), 1.0, 0.0).astype(BF16)
    both = jnp.dot(wide, pick, preferred_element_type=F32)
    return both[:, :DEPTH], both[:, DEPTH:]


def write_rows(rows):
    return rows.reshape(-1, TOK // 2, 2, DEPTH).astype(BF16)


def read_rows(pairs):
    return pairs.astype(F32).reshape(-1, DEPTH)


def local_kernel(q_ref, kv_ref, out_ref):
    n = GROUP * TOK
    row = lax.broadcasted_iota(jnp.int32, (n, n), 0)
    col = lax.broadcasted_iota(jnp.int32, (n, n), 1)
    same = row // TOK == col // TOK

    for g in range(HEADS // GROUP):
        heads = range(g * GROUP, (g + 1) * GROUP)
        query, key, value = (
            jnp.concatenate([ref[i, :, h * DEPTH : (h + 1) * DEPTH] for h in heads], 0)
            for ref, i in ((q_ref, 0), (kv_ref, 0), (kv_ref, 1))
        )
        score = jnp.where(same, dot_t(query, key), -jnp.inf)
        top = jnp.max(score, axis=1, keepdims=True)
        weight = jnp.exp2((score - top) * FACTOR)
        total = jnp.sum(weight, axis=1, keepdims=True)
        summed = jnp.dot(weight.astype(BF16), value, preferred_element_type=F32)
        here = slice(g * GROUP, (g + 1) * GROUP)
        out_ref[here, 0:PAIRS] = write_rows(summed / total)
        out_ref[here, PAIRS] = write_stats(top, total)


def attend_kernel(x_ref, kv_ref, out_ref, score, weight, top, total):
    side = lax.axis_index("patch") % SIDES
    row = lax.broadcasted_iota(jnp.int32, (BLOCK, BLOCK), 0)
    col = lax.broadcasted_iota(jnp.int32, (BLOCK, BLOCK), 1)
    same = row // TOK == col // TOK
    lower = lax.broadcasted_iota(jnp.int32, (BLOCK, DEPTH), 1) < HALF
    n = BLOCK // TOK
    steps = [slice(step * NEAR, (step + 1) * NEAR) for step in range(2)]
    for step in range(2):
        query = x_ref[:, step * TOK : (step + 1) * TOK, :].reshape(NEAR, DEPTH)
        for half in range(SIDES):
            keys = kv_ref[half, :, 0:TOK, :].reshape(NEAR, DEPTH)
            score[steps[step], half * NEAR : (half + 1) * NEAR] = dot_t(query, keys)
    for step in range(2):
        for i in range(NEAR // BLOCK):
            here = slice(step * NEAR + i * BLOCK, step * NEAR + (i + 1) * BLOCK)
            if step == 1:
                for half in range(SIDES):
                    cols = slice(half * NEAR + i * BLOCK, half * NEAR + (i + 1) * BLOCK)
                    own = jnp.logical_and(same, side == half)
                    score[here, cols] = jnp.where(own, -jnp.inf, score[here, cols])
            block = score[here]
            most = jnp.max(block, axis=1, keepdims=True)
            weights = jnp.exp2((block - most) * FACTOR)
            added = jnp.sum(weights, axis=1, keepdims=True)
            top[here] = jnp.broadcast_to(most, (BLOCK, DEPTH))
            total[here] = jnp.broadcast_to(added, (BLOCK, DEPTH))
            weight[here] = weights.astype(BF16)
    values = kv_ref[:, :, TOK:, :].reshape(TOKENS, DEPTH)
    attn = score.at[:, 0:DEPTH]
    for step in range(2):
        attn[steps[step]] = jnp.dot(weight[steps[step]], values, preferred_element_type=F32)
    for i in range(NEAR // BLOCK):
        zero = slice(i * BLOCK, (i + 1) * BLOCK)
        one = slice(NEAR + i * BLOCK, NEAR + (i + 1) * BLOCK)
        first = attn[zero] / total[zero]
        second = attn[one] / total[one]
        chunks = (
            jnp.where(lower, first, pltpu.roll(second, HALF, 1)),
            jnp.where(lower, pltpu.roll(first, HALF, 1), second),
        )
        stats = write_stats(top[one], total[one])
        for core, chunk in enumerate(chunks):
            at = slice(core * HEADS + i * n, core * HEADS + (i + 1) * n)
            out_ref[at, 0:PAIRS] = write_rows(chunk)
            out_ref[at, PAIRS] = stats


def near_kernel(near_ref, attn_ref, top_ref, total_ref):
    upper = lax.axis_index("cfg") == 1
    for b in range(2):
        near = read_rows(near_ref[b, :, 0:PAIRS])
        attn_ref[b] = jnp.where(upper, near, pltpu.roll(near, HALF, 1))
        top_ref[b], total_ref[b] = read_stats(near_ref[b, :, PAIRS])


def merge_kernel(y_ref, near_ref, top_ref, total_ref, gate_ref, out_ref, held):
    lower = lax.broadcasted_iota(jnp.int32, (NEAR, DEPTH), 1) < HALF

    def branch(b):
        heads = slice(b * HEADS, (b + 1) * HEADS)
        far = read_rows(y_ref[heads, 0:PAIRS])
        far_top, far_total = read_stats(y_ref[heads, PAIRS])
        near_top = top_ref[b]
        top = jnp.maximum(far_top, near_top)
        far_share = jnp.exp2((far_top - top) * FACTOR) * far_total
        near_share = jnp.exp2((near_top - top) * FACTOR) * total_ref[b]
        both = (far_share * far + near_share * near_ref[b]) / (far_share + near_share)
        return jnp.where(lower, far, both).astype(BF16).astype(F32)

    cond = branch(0)
    uncond = branch(1)
    mixed = (uncond + 5.0 * (cond - uncond)).reshape(HEADS, TOK, DEPTH)
    held[...] = (gate_ref[...].reshape(HEADS, 1, DEPTH) * mixed).reshape(NEAR, DEPTH)
    for t in range(TOK):
        rows = held[pl.ds(t, HEADS, stride=TOK), :]
        out_ref[0, t] = rows[:, :HALF].astype(BF16)
        out_ref[1, t] = rows[:, HALF:].astype(BF16)


def call(kernel, out, args, specs=None, scratch=(), flops=0, out_space=pltpu.VMEM, limit=32):
    many = isinstance(out, list)
    shapes = out if many else [out]
    moved = sum(a.size * a.dtype.itemsize for a in list(args) + list(shapes))
    vmem = pl.BlockSpec(memory_space=pltpu.VMEM)
    result = pl.BlockSpec(memory_space=out_space)
    return pl.pallas_call(
        kernel,
        grid=(1,),
        out_shape=out,
        in_specs=specs or [vmem] * len(args),
        out_specs=[result] * len(shapes) if many else result,
        scratch_shapes=list(scratch),
        cost_estimate=pl.CostEstimate(flops=flops, bytes_accessed=moved, transcendentals=0),
        compiler_params=pltpu.CompilerParams(vmem_limit_bytes=limit << 20),
    )(*args)


def body(queries, keys_values, timesteps, gate_table):
    width = HEADS * DEPTH
    sides = [[SIDES * i + side for i in range(HEADS)] for side in range(SIDES)]
    patches = SIDES * HEADS
    cores = [
        [core * patches + patch for core in range(2) for patch in side] for side in sides
    ]
    whole = pl.BlockSpec(memory_space=pltpu.HBM)
    sent = call(
        pack_kernel,
        SHAPE((HEADS, 4 * TOK, DEPTH), BF16),
        (queries, keys_values),
        [whole, whole],
        [
            pltpu.VMEM((4, TOK, width), BF16),
            pltpu.VMEM((4, HEADS, TOK, DEPTH), BF16),
            pltpu.SemaphoreType.DMA((4,)),
            pltpu.SemaphoreType.DMA((4,)),
        ],
        out_space=pltpu.HBM,
        limit=60,
    )
    held = lax.all_to_all(
        sent, "patch", split_axis=0, concat_axis=0, tiled=True, axis_index_groups=sides
    )
    near = call(
        local_kernel,
        SHAPE((HEADS, PAIRS + 1, 2, DEPTH), BF16),
        (queries, keys_values),
        [
            pl.BlockSpec((None, 1, TOK, width), lambda i: (0, 1, 0, 0)),
            pl.BlockSpec((None, None, 2, TOK, width), lambda i: (0, 1, 0, 0, 0)),
        ],
    )
    near = lax.all_gather(near, "cfg", axis=0, tiled=False)
    near = call(near_kernel, [SHAPE((2, NEAR, DEPTH), F32)] * 3, (near,))
    gates = jnp.take(gate_table, timesteps, axis=0, mode="clip").reshape(2, HEADS, 2, HALF)
    gate = lax.dynamic_index_in_dim(gates, lax.axis_index("cfg"), 2, keepdims=False)
    gate = jnp.concatenate([gate[0], gate[1]], axis=1)
    held, near, gate = lax.optimization_barrier((held, near, gate))
    pairs = [[SIDES * i, SIDES * i + 1] for i in range(HEADS)]
    stale = lax.all_gather(
        held[:, 2 * TOK :, :], "patch", axis=0, tiled=False, axis_index_groups=pairs
    )
    far = call(
        attend_kernel,
        SHAPE((2 * HEADS, PAIRS + 1, 2, DEPTH), BF16),
        (held, stale),
        scratch=[
            pltpu.VMEM((ROWS, TOKENS), F32),
            pltpu.VMEM((ROWS, TOKENS), BF16),
            pltpu.VMEM((ROWS, DEPTH), F32),
            pltpu.VMEM((ROWS, DEPTH), F32),
        ],
        flops=4 * ROWS * TOKENS * DEPTH,
    )
    back = lax.all_to_all(
        far, ("cfg", "patch"), split_axis=0, concat_axis=0, tiled=True, axis_index_groups=cores
    )
    return call(
        merge_kernel,
        SHAPE((2, TOK, HEADS, HALF), BF16),
        (back, *near, gate),
        scratch=[pltpu.VMEM((NEAR, DEPTH), F32)],
    )


def solution(mesh):
    placed = (
        P("cfg", None, ("clip", "patch"), None),
        P("cfg", None, None, ("clip", "patch"), None),
        P("clip"),
        P(),
    )
    return jax.shard_map(
        body,
        mesh=mesh,
        in_specs=placed,
        out_specs=P(None, ("clip", "patch"), None, "cfg"),
        check_vma=False,
    )
```

```python
import math

import jax
import jax.numpy as jnp
from jax import lax
from jax.experimental import pallas as pl
from jax.experimental.pallas import tpu as pltpu
from jax.sharding import PartitionSpec as P

HEADS = 32
DEPTH = 128
HALF = DEPTH // 2
TOK = 16
SIDES = 2
NEAR = HEADS * TOK
ROWS = 2 * NEAR
PAIRS = TOK // 2
SLOTS = DEPTH // TOK
GROUP = 8
TOKENS = SIDES * NEAR
BLOCK = 128
FACTOR = math.log2(math.e) / math.sqrt(DEPTH)
BF16 = jnp.bfloat16
F32 = jnp.float32
SHAPE = jax.ShapeDtypeStruct


def dot_t(a, b):
    return lax.dot_general(a, b, (((1,), (1,)), ((), ())), preferred_element_type=F32)


def pack_kernel(q_ref, kv_ref, out_ref, held, packed, in_sems, out_sems):
    fields = [q_ref.at[0, 0], q_ref.at[0, 1], kv_ref.at[0, 0, 0], kv_ref.at[0, 0, 1]]
    loads = [
        pltpu.make_async_copy(field, held.at[i], in_sems.at[i]) for i, field in enumerate(fields)
    ]
    stores = [
        pltpu.make_async_copy(
            packed.at[i], out_ref.at[:, i * TOK : (i + 1) * TOK, :], out_sems.at[i]
        )
        for i in range(len(fields))
    ]

    def by_head(i):
        for h in range(HEADS):
            packed[i, h] = held[i, :, h * DEPTH : (h + 1) * DEPTH]

    odd = lax.axis_index("cfg") == 1

    @pl.when(odd)
    def _():
        for load in loads:
            load.start()
        for i, load in enumerate(loads):
            load.wait()
            by_head(i)
            stores[i].start()
        for store in stores:
            store.wait()

    @pl.when(jnp.logical_not(odd))
    def _():
        for i, load in enumerate(loads):
            load.start()
            load.wait()
            by_head(i)
            stores[i].start()
            stores[i].wait()


def split_value(value):
    high = value.astype(BF16).astype(F32)
    rest = value - high
    mid = rest.astype(BF16).astype(F32)
    return high, mid, rest - mid


def write_stats(top, total):
    rows = top.shape[0]
    n = rows // TOK
    lane = lax.broadcasted_iota(jnp.int32, (rows, DEPTH), 1)
    token = lax.broadcasted_iota(jnp.int32, (rows, DEPTH), 0) % TOK
    slot = jnp.where(lane // SLOTS == token, lane % SLOTS, SLOTS)
    value = jnp.where(slot < 3, top, total)
    high, mid, low = split_value(value)
    piece = jnp.where(slot % 3 == 0, high, jnp.where(slot % 3 == 1, mid, low))
    piece = jnp.where(slot < 6, piece, 0.0).astype(BF16)
    out_row = lax.broadcasted_iota(jnp.int32, (2 * n, rows), 0)
    in_row = lax.broadcasted_iota(jnp.int32, (2 * n, rows), 1)
    gather = jnp.where(out_row == in_row // TOK * 2, 1.0, 0.0).astype(BF16)
    return jnp.dot(gather, piece, preferred_element_type=F32).reshape(n, 2, DEPTH).astype(BF16)


def read_stats(stats):
    n = stats.shape[0]
    out_row = lax.broadcasted_iota(jnp.int32, (n * TOK, 2 * n), 0)
    in_row = lax.broadcasted_iota(jnp.int32, (n * TOK, 2 * n), 1)
    spread = jnp.where(in_row == out_row // TOK * 2, 1.0, 0.0).astype(BF16)
    flat = stats.astype(F32).reshape(2 * n, DEPTH).astype(BF16)
    wide = jnp.dot(spread, flat, preferred_element_type=F32)
    lane = lax.broadcasted_iota(jnp.int32, (n * TOK, DEPTH), 1)
    token = lax.broadcasted_iota(jnp.int32, (n * TOK, DEPTH), 0) % TOK
    wide = jnp.where(lane // SLOTS == token, wide, 0.0).astype(BF16)
    slot = lax.broadcasted_iota(jnp.int32, (DEPTH, 2 * DEPTH), 0) % SLOTS
    part = lax.broadcasted_iota(jnp.int32, (DEPTH, 2 * DEPTH), 1) // DEPTH
    pick = jnp.where(jnp.logical_and(slot < 6, slot // 3 == part), 1.0, 0.0).astype(BF16)
    both = jnp.dot(wide, pick, preferred_element_type=F32)
    return both[:, :DEPTH], both[:, DEPTH:]


def write_rows(rows):
    return rows.reshape(-1, TOK // 2, 2, DEPTH).astype(BF16)


def read_rows(pairs):
    return pairs.astype(F32).reshape(-1, DEPTH)


def local_kernel(q_ref, kv_ref, attn_ref, top_ref, total_ref):
    n = GROUP * TOK
    row = lax.broadcasted_iota(jnp.int32, (n, n), 0)
    col = lax.broadcasted_iota(jnp.int32, (n, n), 1)
    same = row // TOK == col // TOK

    for g in range(HEADS // GROUP):
        heads = range(g * GROUP, (g + 1) * GROUP)
        query, key, value = (
            jnp.concatenate([ref[i, :, h * DEPTH : (h + 1) * DEPTH] for h in heads], 0)
            for ref, i in ((q_ref, 0), (kv_ref, 0), (kv_ref, 1))
        )
        score = jnp.where(same, dot_t(query, key), -jnp.inf)
        top = jnp.max(score, axis=1, keepdims=True)
        weight = jnp.exp2((score - top) * FACTOR)
        total = jnp.sum(weight, axis=1, keepdims=True)
        summed = jnp.dot(weight.astype(BF16), value, preferred_element_type=F32)
        here = slice(g * n, (g + 1) * n)
        attn_ref[here] = summed / total
        top_ref[here] = jnp.broadcast_to(top, (n, DEPTH))
        total_ref[here] = jnp.broadcast_to(total, (n, DEPTH))


def attend_kernel(x_ref, kv_ref, out_ref, score, weight, top, total):
    side = lax.axis_index("patch") % SIDES
    row = lax.broadcasted_iota(jnp.int32, (BLOCK, BLOCK), 0)
    col = lax.broadcasted_iota(jnp.int32, (BLOCK, BLOCK), 1)
    same = row // TOK == col // TOK
    n = BLOCK // TOK
    steps = [slice(step * NEAR, (step + 1) * NEAR) for step in range(2)]
    for step in range(2):
        query = x_ref[:, step * TOK : (step + 1) * TOK, :].reshape(NEAR, DEPTH)
        for half in range(SIDES):
            keys = kv_ref[half, :, 0:TOK, :].reshape(NEAR, DEPTH)
            score[steps[step], half * NEAR : (half + 1) * NEAR] = dot_t(query, keys)
    for step in range(2):
        for i in range(NEAR // BLOCK):
            here = slice(step * NEAR + i * BLOCK, step * NEAR + (i + 1) * BLOCK)
            if step == 1:
                for half in range(SIDES):
                    cols = slice(half * NEAR + i * BLOCK, half * NEAR + (i + 1) * BLOCK)
                    own = jnp.logical_and(same, side == half)
                    score[here, cols] = jnp.where(own, -jnp.inf, score[here, cols])
            block = score[here]
            most = jnp.max(block, axis=1, keepdims=True)
            weights = jnp.exp2((block - most) * FACTOR)
            added = jnp.sum(weights, axis=1, keepdims=True)
            top[here] = jnp.broadcast_to(most, (BLOCK, DEPTH))
            total[here] = jnp.broadcast_to(added, (BLOCK, DEPTH))
            weight[here] = weights.astype(BF16)
    values = kv_ref[:, :, TOK:, :].reshape(TOKENS, DEPTH)
    for step in range(2):
        rows = steps[step]
        attn = jnp.dot(weight[rows], values, preferred_element_type=F32) / total[rows]
        out_ref[:, step * PAIRS : (step + 1) * PAIRS] = write_rows(attn)
    for i in range(NEAR // BLOCK):
        rows = slice(NEAR + i * BLOCK, NEAR + (i + 1) * BLOCK)
        out_ref[i * n : (i + 1) * n, 2 * PAIRS] = write_stats(top[rows], total[rows])


def merge_kernel(y_ref, near_ref, top_ref, total_ref, out_ref):
    lower = lax.broadcasted_iota(jnp.int32, (NEAR, DEPTH), 1) < HALF
    first = read_rows(y_ref[:, 0:PAIRS])
    far = read_rows(y_ref[:, PAIRS : 2 * PAIRS])
    far_top, far_total = read_stats(y_ref[:, 2 * PAIRS])
    near_top = top_ref[...]
    top = jnp.maximum(far_top, near_top)
    far_share = jnp.exp2((far_top - top) * FACTOR) * far_total
    near_share = jnp.exp2((near_top - top) * FACTOR) * total_ref[...]
    second = (far_share * far + near_share * near_ref[...]) / (far_share + near_share)
    out_ref[0] = jnp.where(lower, first, pltpu.roll(second, HALF, 1)).astype(BF16)
    out_ref[1] = jnp.where(lower, pltpu.roll(first, HALF, 1), second).astype(BF16)


def guide_kernel(both_ref, gate_ref, out_ref, held):
    core = lax.axis_index("cfg")
    cond = both_ref[0, core].astype(F32)
    uncond = both_ref[1, core].astype(F32)
    mixed = (uncond + 5.0 * (cond - uncond)).reshape(HEADS, TOK, DEPTH)
    held[...] = (gate_ref[...].reshape(HEADS, 1, DEPTH) * mixed).reshape(NEAR, DEPTH)
    for t in range(TOK):
        rows = held[pl.ds(t, HEADS, stride=TOK), :]
        out_ref[0, t] = rows[:, :HALF].astype(BF16)
        out_ref[1, t] = rows[:, HALF:].astype(BF16)


def call(kernel, out, args, specs=None, scratch=(), flops=0, out_space=pltpu.VMEM, limit=32):
    many = isinstance(out, list)
    shapes = out if many else [out]
    moved = sum(a.size * a.dtype.itemsize for a in list(args) + list(shapes))
    vmem = pl.BlockSpec(memory_space=pltpu.VMEM)
    result = pl.BlockSpec(memory_space=out_space)
    return pl.pallas_call(
        kernel,
        grid=(1,),
        out_shape=out,
        in_specs=specs or [vmem] * len(args),
        out_specs=[result] * len(shapes) if many else result,
        scratch_shapes=list(scratch),
        cost_estimate=pl.CostEstimate(flops=flops, bytes_accessed=moved, transcendentals=0),
        compiler_params=pltpu.CompilerParams(vmem_limit_bytes=limit << 20),
    )(*args)


def body(queries, keys_values, timesteps, gate_table):
    width = HEADS * DEPTH
    sides = [[SIDES * i + side for i in range(HEADS)] for side in range(SIDES)]
    patches = SIDES * HEADS
    whole = pl.BlockSpec(memory_space=pltpu.HBM)
    sent = call(
        pack_kernel,
        SHAPE((HEADS, 4 * TOK, DEPTH), BF16),
        (queries, keys_values),
        [whole, whole],
        [
            pltpu.VMEM((4, TOK, width), BF16),
            pltpu.VMEM((4, HEADS, TOK, DEPTH), BF16),
            pltpu.SemaphoreType.DMA((4,)),
            pltpu.SemaphoreType.DMA((4,)),
        ],
        out_space=pltpu.HBM,
        limit=60,
    )
    held = lax.all_to_all(
        sent, "patch", split_axis=0, concat_axis=0, tiled=True, axis_index_groups=sides
    )
    near = call(
        local_kernel,
        [SHAPE((NEAR, DEPTH), F32)] * 3,
        (queries, keys_values),
        [
            pl.BlockSpec((None, 1, TOK, width), lambda i: (0, 1, 0, 0)),
            pl.BlockSpec((None, None, 2, TOK, width), lambda i: (0, 1, 0, 0, 0)),
        ],
    )
    gates = jnp.take(gate_table, timesteps, axis=0, mode="clip").reshape(2, HEADS, 2, HALF)
    gate = lax.dynamic_index_in_dim(gates, lax.axis_index("cfg"), 2, keepdims=False)
    gate = jnp.concatenate([gate[0], gate[1]], axis=1)
    held, near, gate = lax.optimization_barrier((held, near, gate))
    pairs = [[SIDES * i, SIDES * i + 1] for i in range(HEADS)]
    stale = lax.all_gather(
        held[:, 2 * TOK :, :], "patch", axis=0, tiled=False, axis_index_groups=pairs
    )
    far = call(
        attend_kernel,
        SHAPE((HEADS, 2 * PAIRS + 1, 2, DEPTH), BF16),
        (held, stale),
        scratch=[
            pltpu.VMEM((ROWS, TOKENS), F32),
            pltpu.VMEM((ROWS, TOKENS), BF16),
            pltpu.VMEM((ROWS, DEPTH), F32),
            pltpu.VMEM((ROWS, DEPTH), F32),
        ],
        flops=4 * ROWS * TOKENS * DEPTH,
    )
    back = lax.all_to_all(
        far, "patch", split_axis=0, concat_axis=0, tiled=True, axis_index_groups=sides
    )
    attn = call(merge_kernel, SHAPE((2, NEAR, DEPTH), BF16), (back, *near))
    both = lax.all_gather(attn, "cfg", axis=0, tiled=False)
    return call(
        guide_kernel,
        SHAPE((2, TOK, HEADS, HALF), BF16),
        (both, gate),
        scratch=[pltpu.VMEM((NEAR, DEPTH), F32)],
    )


def solution(mesh):
    placed = (
        P("cfg", None, ("clip", "patch"), None),
        P("cfg", None, None, ("clip", "patch"), None),
        P("clip"),
        P(),
    )
    return jax.shard_map(
        body,
        mesh=mesh,
        in_specs=placed,
        out_specs=P(None, ("clip", "patch"), None, "cfg"),
        check_vma=False,
    )
```

```python
import math

import jax
import jax.numpy as jnp
from jax import lax
from jax.experimental import pallas as pl
from jax.experimental.pallas import tpu as pltpu
from jax.sharding import PartitionSpec as P

HEADS = 32
DEPTH = 128
HALF = DEPTH // 2
TOK = 16
SIDES = 2
NEAR = HEADS * TOK
ROWS = 2 * NEAR
PAIRS = TOK // 2
SLOTS = DEPTH // TOK
GROUP = 8
TOKENS = SIDES * NEAR
BLOCK = 128
FACTOR = math.log2(math.e) / math.sqrt(DEPTH)
BF16 = jnp.bfloat16
F32 = jnp.float32
SHAPE = jax.ShapeDtypeStruct


def dot_t(a, b):
    return lax.dot_general(a, b, (((1,), (1,)), ((), ())), preferred_element_type=F32)


def pack_kernel(q_ref, kv_ref, out_ref, held, packed, in_sems, out_sems):
    fields = [q_ref.at[0, 0], q_ref.at[0, 1], kv_ref.at[0, 0, 0], kv_ref.at[0, 0, 1]]
    loads = [
        pltpu.make_async_copy(field, held.at[i], in_sems.at[i]) for i, field in enumerate(fields)
    ]
    stores = [
        pltpu.make_async_copy(
            packed.at[i], out_ref.at[:, i * TOK : (i + 1) * TOK, :], out_sems.at[i]
        )
        for i in range(len(fields))
    ]

    def by_head(i):
        for h in range(HEADS):
            packed[i, h] = held[i, :, h * DEPTH : (h + 1) * DEPTH]

    odd = lax.axis_index("cfg") == 1

    @pl.when(odd)
    def _():
        for load in loads:
            load.start()
        for i, load in enumerate(loads):
            load.wait()
            by_head(i)
            stores[i].start()
        for store in stores:
            store.wait()

    @pl.when(jnp.logical_not(odd))
    def _():
        for both in ((0, 1), (2, 3)):
            for i in both:
                loads[i].start()
            for i in both:
                loads[i].wait()
                by_head(i)
                stores[i].start()
            for i in both:
                stores[i].wait()


def split_value(value):
    high = value.astype(BF16).astype(F32)
    rest = value - high
    mid = rest.astype(BF16).astype(F32)
    return high, mid, rest - mid


def write_stats(top, total):
    rows = top.shape[0]
    n = rows // TOK
    lane = lax.broadcasted_iota(jnp.int32, (rows, DEPTH), 1)
    token = lax.broadcasted_iota(jnp.int32, (rows, DEPTH), 0) % TOK
    slot = jnp.where(lane // SLOTS == token, lane % SLOTS, SLOTS)
    value = jnp.where(slot < 3, top, total)
    high, mid, low = split_value(value)
    piece = jnp.where(slot % 3 == 0, high, jnp.where(slot % 3 == 1, mid, low))
    piece = jnp.where(slot < 6, piece, 0.0).astype(BF16)
    out_row = lax.broadcasted_iota(jnp.int32, (2 * n, rows), 0)
    in_row = lax.broadcasted_iota(jnp.int32, (2 * n, rows), 1)
    gather = jnp.where(out_row == in_row // TOK * 2, 1.0, 0.0).astype(BF16)
    return jnp.dot(gather, piece, preferred_element_type=F32).reshape(n, 2, DEPTH).astype(BF16)


def read_stats(stats):
    n = stats.shape[0]
    out_row = lax.broadcasted_iota(jnp.int32, (n * TOK, 2 * n), 0)
    in_row = lax.broadcasted_iota(jnp.int32, (n * TOK, 2 * n), 1)
    spread = jnp.where(in_row == out_row // TOK * 2, 1.0, 0.0).astype(BF16)
    flat = stats.astype(F32).reshape(2 * n, DEPTH).astype(BF16)
    wide = jnp.dot(spread, flat, preferred_element_type=F32)
    lane = lax.broadcasted_iota(jnp.int32, (n * TOK, DEPTH), 1)
    token = lax.broadcasted_iota(jnp.int32, (n * TOK, DEPTH), 0) % TOK
    wide = jnp.where(lane // SLOTS == token, wide, 0.0).astype(BF16)
    slot = lax.broadcasted_iota(jnp.int32, (DEPTH, 2 * DEPTH), 0) % SLOTS
    part = lax.broadcasted_iota(jnp.int32, (DEPTH, 2 * DEPTH), 1) // DEPTH
    pick = jnp.where(jnp.logical_and(slot < 6, slot // 3 == part), 1.0, 0.0).astype(BF16)
    both = jnp.dot(wide, pick, preferred_element_type=F32)
    return both[:, :DEPTH], both[:, DEPTH:]


def write_rows(rows):
    return rows.reshape(-1, TOK // 2, 2, DEPTH).astype(BF16)


def read_rows(pairs):
    return pairs.astype(F32).reshape(-1, DEPTH)


def local_kernel(q_ref, kv_ref, attn_ref, top_ref, total_ref):
    n = GROUP * TOK
    row = lax.broadcasted_iota(jnp.int32, (n, n), 0)
    col = lax.broadcasted_iota(jnp.int32, (n, n), 1)
    same = row // TOK == col // TOK

    for g in range(HEADS // GROUP):
        heads = range(g * GROUP, (g + 1) * GROUP)
        query, key, value = (
            jnp.concatenate([ref[i, :, h * DEPTH : (h + 1) * DEPTH] for h in heads], 0)
            for ref, i in ((q_ref, 0), (kv_ref, 0), (kv_ref, 1))
        )
        score = jnp.where(same, dot_t(query, key), -jnp.inf)
        top = jnp.max(score, axis=1, keepdims=True)
        weight = jnp.exp2((score - top) * FACTOR)
        total = jnp.sum(weight, axis=1, keepdims=True)
        summed = jnp.dot(weight.astype(BF16), value, preferred_element_type=F32)
        here = slice(g * n, (g + 1) * n)
        attn_ref[here] = summed / total
        top_ref[here] = jnp.broadcast_to(top, (n, DEPTH))
        total_ref[here] = jnp.broadcast_to(total, (n, DEPTH))


def attend_kernel(x_ref, kv_ref, out_ref, score, weight, top, total):
    side = lax.axis_index("patch") % SIDES
    row = lax.broadcasted_iota(jnp.int32, (BLOCK, BLOCK), 0)
    col = lax.broadcasted_iota(jnp.int32, (BLOCK, BLOCK), 1)
    same = row // TOK == col // TOK
    n = BLOCK // TOK
    steps = [slice(step * NEAR, (step + 1) * NEAR) for step in range(2)]
    for step in range(2):
        query = x_ref[:, step * TOK : (step + 1) * TOK, :].reshape(NEAR, DEPTH)
        for half in range(SIDES):
            keys = kv_ref[half, :, 0:TOK, :].reshape(NEAR, DEPTH)
            score[steps[step], half * NEAR : (half + 1) * NEAR] = dot_t(query, keys)
    for step in range(2):
        for i in range(NEAR // BLOCK):
            here = slice(step * NEAR + i * BLOCK, step * NEAR + (i + 1) * BLOCK)
            if step == 1:
                for half in range(SIDES):
                    cols = slice(half * NEAR + i * BLOCK, half * NEAR + (i + 1) * BLOCK)
                    own = jnp.logical_and(same, side == half)
                    score[here, cols] = jnp.where(own, -jnp.inf, score[here, cols])
            block = score[here]
            most = jnp.max(block, axis=1, keepdims=True)
            weights = jnp.exp2((block - most) * FACTOR)
            added = jnp.sum(weights, axis=1, keepdims=True)
            top[here] = jnp.broadcast_to(most, (BLOCK, DEPTH))
            total[here] = jnp.broadcast_to(added, (BLOCK, DEPTH))
            weight[here] = weights.astype(BF16)
    values = kv_ref[:, :, TOK:, :].reshape(TOKENS, DEPTH)
    for step in range(2):
        rows = steps[step]
        attn = jnp.dot(weight[rows], values, preferred_element_type=F32) / total[rows]
        out_ref[:, step * PAIRS : (step + 1) * PAIRS] = write_rows(attn)
    for i in range(NEAR // BLOCK):
        rows = slice(NEAR + i * BLOCK, NEAR + (i + 1) * BLOCK)
        out_ref[i * n : (i + 1) * n, 2 * PAIRS] = write_stats(top[rows], total[rows])


def merge_kernel(y_ref, near_ref, top_ref, total_ref, out_ref):
    lower = lax.broadcasted_iota(jnp.int32, (NEAR, DEPTH), 1) < HALF
    first = read_rows(y_ref[:, 0:PAIRS])
    far = read_rows(y_ref[:, PAIRS : 2 * PAIRS])
    far_top, far_total = read_stats(y_ref[:, 2 * PAIRS])
    near_top = top_ref[...]
    top = jnp.maximum(far_top, near_top)
    far_share = jnp.exp2((far_top - top) * FACTOR) * far_total
    near_share = jnp.exp2((near_top - top) * FACTOR) * total_ref[...]
    second = (far_share * far + near_share * near_ref[...]) / (far_share + near_share)
    out_ref[0] = jnp.where(lower, first, pltpu.roll(second, HALF, 1)).astype(BF16)
    out_ref[1] = jnp.where(lower, pltpu.roll(first, HALF, 1), second).astype(BF16)


def guide_kernel(both_ref, gate_ref, out_ref, held):
    core = lax.axis_index("cfg")
    cond = both_ref[0, core].astype(F32)
    uncond = both_ref[1, core].astype(F32)
    mixed = (uncond + 5.0 * (cond - uncond)).reshape(HEADS, TOK, DEPTH)
    held[...] = (gate_ref[...].reshape(HEADS, 1, DEPTH) * mixed).reshape(NEAR, DEPTH)
    for t in range(TOK):
        rows = held[pl.ds(t, HEADS, stride=TOK), :]
        out_ref[0, t] = rows[:, :HALF].astype(BF16)
        out_ref[1, t] = rows[:, HALF:].astype(BF16)


def call(kernel, out, args, specs=None, scratch=(), flops=0, out_space=pltpu.VMEM, limit=32):
    many = isinstance(out, list)
    shapes = out if many else [out]
    moved = sum(a.size * a.dtype.itemsize for a in list(args) + list(shapes))
    vmem = pl.BlockSpec(memory_space=pltpu.VMEM)
    result = pl.BlockSpec(memory_space=out_space)
    return pl.pallas_call(
        kernel,
        grid=(1,),
        out_shape=out,
        in_specs=specs or [vmem] * len(args),
        out_specs=[result] * len(shapes) if many else result,
        scratch_shapes=list(scratch),
        cost_estimate=pl.CostEstimate(flops=flops, bytes_accessed=moved, transcendentals=0),
        compiler_params=pltpu.CompilerParams(vmem_limit_bytes=limit << 20),
    )(*args)


def body(queries, keys_values, timesteps, gate_table):
    width = HEADS * DEPTH
    sides = [[SIDES * i + side for i in range(HEADS)] for side in range(SIDES)]
    patches = SIDES * HEADS
    whole = pl.BlockSpec(memory_space=pltpu.HBM)
    sent = call(
        pack_kernel,
        SHAPE((HEADS, 4 * TOK, DEPTH), BF16),
        (queries, keys_values),
        [whole, whole],
        [
            pltpu.VMEM((4, TOK, width), BF16),
            pltpu.VMEM((4, HEADS, TOK, DEPTH), BF16),
            pltpu.SemaphoreType.DMA((4,)),
            pltpu.SemaphoreType.DMA((4,)),
        ],
        out_space=pltpu.HBM,
        limit=60,
    )
    held = lax.all_to_all(
        sent, "patch", split_axis=0, concat_axis=0, tiled=True, axis_index_groups=sides
    )
    near = call(
        local_kernel,
        [SHAPE((NEAR, DEPTH), F32)] * 3,
        (queries, keys_values),
        [
            pl.BlockSpec((None, 1, TOK, width), lambda i: (0, 1, 0, 0)),
            pl.BlockSpec((None, None, 2, TOK, width), lambda i: (0, 1, 0, 0, 0)),
        ],
    )
    gates = jnp.take(gate_table, timesteps, axis=0, mode="clip").reshape(2, HEADS, 2, HALF)
    gate = lax.dynamic_index_in_dim(gates, lax.axis_index("cfg"), 2, keepdims=False)
    gate = jnp.concatenate([gate[0], gate[1]], axis=1)
    held, near, gate = lax.optimization_barrier((held, near, gate))
    pairs = [[SIDES * i, SIDES * i + 1] for i in range(HEADS)]
    stale = lax.all_gather(
        held[:, 2 * TOK :, :], "patch", axis=0, tiled=False, axis_index_groups=pairs
    )
    far = call(
        attend_kernel,
        SHAPE((HEADS, 2 * PAIRS + 1, 2, DEPTH), BF16),
        (held, stale),
        scratch=[
            pltpu.VMEM((ROWS, TOKENS), F32),
            pltpu.VMEM((ROWS, TOKENS), BF16),
            pltpu.VMEM((ROWS, DEPTH), F32),
            pltpu.VMEM((ROWS, DEPTH), F32),
        ],
        flops=4 * ROWS * TOKENS * DEPTH,
    )
    back = lax.all_to_all(
        far, "patch", split_axis=0, concat_axis=0, tiled=True, axis_index_groups=sides
    )
    attn = call(merge_kernel, SHAPE((2, NEAR, DEPTH), BF16), (back, *near))
    both = lax.all_gather(attn, "cfg", axis=0, tiled=False)
    return call(
        guide_kernel,
        SHAPE((2, TOK, HEADS, HALF), BF16),
        (both, gate),
        scratch=[pltpu.VMEM((NEAR, DEPTH), F32)],
    )


def solution(mesh):
    placed = (
        P("cfg", None, ("clip", "patch"), None),
        P("cfg", None, None, ("clip", "patch"), None),
        P("clip"),
        P(),
    )
    return jax.shard_map(
        body,
        mesh=mesh,
        in_specs=placed,
        out_specs=P(None, ("clip", "patch"), None, "cfg"),
        check_vma=False,
    )
```

```python
import math

import jax
import jax.numpy as jnp
from jax import lax
from jax.experimental import pallas as pl
from jax.experimental.pallas import tpu as pltpu
from jax.sharding import PartitionSpec as P

HEADS = 32
DEPTH = 128
HALF = DEPTH // 2
TOK = 16
SIDES = 2
EVEN_CUTS = ((0, 16, 32), (0, 16, 32), (0, 32), (0, 32))
NEAR = HEADS * TOK
ROWS = 2 * NEAR
PAIRS = TOK // 2
SLOTS = DEPTH // TOK
GROUP = 8
TOKENS = SIDES * NEAR
BLOCK = 128
FACTOR = math.log2(math.e) / math.sqrt(DEPTH)
BF16 = jnp.bfloat16
F32 = jnp.float32
SHAPE = jax.ShapeDtypeStruct


def dot_t(a, b):
    return lax.dot_general(a, b, (((1,), (1,)), ((), ())), preferred_element_type=F32)


def pack_kernel(q_ref, kv_ref, out_ref, held, packed, in_sems, out_sems):
    fields = [q_ref.at[0, 0], q_ref.at[0, 1], kv_ref.at[0, 0, 0], kv_ref.at[0, 0, 1]]
    def piece(i, first, last):
        lanes = pl.ds(first * DEPTH, (last - first) * DEPTH)
        load = pltpu.make_async_copy(
            fields[i].at[:, lanes], held.at[i, :, lanes], in_sems.at[i]
        )
        heads = pl.ds(first, last - first)
        store = pltpu.make_async_copy(
            packed.at[i, heads], out_ref.at[heads, pl.ds(i * TOK, TOK), :], out_sems.at[i]
        )
        return load, store

    def by_head(i, first, last):
        for h in range(first, last):
            packed[i, h] = held[i, :, h * DEPTH : (h + 1) * DEPTH]

    odd = lax.axis_index("cfg") == 1

    @pl.when(odd)
    def _():
        pieces = [piece(i, 0, HEADS) for i in range(len(fields))]
        for load, _ in pieces:
            load.start()
        for i, (load, store) in enumerate(pieces):
            load.wait()
            by_head(i, 0, HEADS)
            store.start()
        for _, store in pieces:
            store.wait()

    @pl.when(jnp.logical_not(odd))
    def _():
        for i, cuts in enumerate(EVEN_CUTS):
            for first, last in zip(cuts[:-1], cuts[1:]):
                load, store = piece(i, first, last)
                load.start()
                load.wait()
                by_head(i, first, last)
                store.start()
                store.wait()


def split_value(value):
    high = value.astype(BF16).astype(F32)
    rest = value - high
    mid = rest.astype(BF16).astype(F32)
    return high, mid, rest - mid


def write_stats(top, total):
    rows = top.shape[0]
    n = rows // TOK
    lane = lax.broadcasted_iota(jnp.int32, (rows, DEPTH), 1)
    token = lax.broadcasted_iota(jnp.int32, (rows, DEPTH), 0) % TOK
    slot = jnp.where(lane // SLOTS == token, lane % SLOTS, SLOTS)
    value = jnp.where(slot < 3, top, total)
    high, mid, low = split_value(value)
    piece = jnp.where(slot % 3 == 0, high, jnp.where(slot % 3 == 1, mid, low))
    piece = jnp.where(slot < 6, piece, 0.0).astype(BF16)
    out_row = lax.broadcasted_iota(jnp.int32, (2 * n, rows), 0)
    in_row = lax.broadcasted_iota(jnp.int32, (2 * n, rows), 1)
    gather = jnp.where(out_row == in_row // TOK * 2, 1.0, 0.0).astype(BF16)
    return jnp.dot(gather, piece, preferred_element_type=F32).reshape(n, 2, DEPTH).astype(BF16)


def read_stats(stats):
    n = stats.shape[0]
    out_row = lax.broadcasted_iota(jnp.int32, (n * TOK, 2 * n), 0)
    in_row = lax.broadcasted_iota(jnp.int32, (n * TOK, 2 * n), 1)
    spread = jnp.where(in_row == out_row // TOK * 2, 1.0, 0.0).astype(BF16)
    flat = stats.astype(F32).reshape(2 * n, DEPTH).astype(BF16)
    wide = jnp.dot(spread, flat, preferred_element_type=F32)
    lane = lax.broadcasted_iota(jnp.int32, (n * TOK, DEPTH), 1)
    token = lax.broadcasted_iota(jnp.int32, (n * TOK, DEPTH), 0) % TOK
    wide = jnp.where(lane // SLOTS == token, wide, 0.0).astype(BF16)
    slot = lax.broadcasted_iota(jnp.int32, (DEPTH, 2 * DEPTH), 0) % SLOTS
    part = lax.broadcasted_iota(jnp.int32, (DEPTH, 2 * DEPTH), 1) // DEPTH
    pick = jnp.where(jnp.logical_and(slot < 6, slot // 3 == part), 1.0, 0.0).astype(BF16)
    both = jnp.dot(wide, pick, preferred_element_type=F32)
    return both[:, :DEPTH], both[:, DEPTH:]


def write_rows(rows):
    return rows.reshape(-1, TOK // 2, 2, DEPTH).astype(BF16)


def read_rows(pairs):
    return pairs.astype(F32).reshape(-1, DEPTH)


def local_kernel(q_ref, kv_ref, attn_ref, top_ref, total_ref):
    n = GROUP * TOK
    row = lax.broadcasted_iota(jnp.int32, (n, n), 0)
    col = lax.broadcasted_iota(jnp.int32, (n, n), 1)
    same = row // TOK == col // TOK

    for g in range(HEADS // GROUP):
        heads = range(g * GROUP, (g + 1) * GROUP)
        query, key, value = (
            jnp.concatenate([ref[i, :, h * DEPTH : (h + 1) * DEPTH] for h in heads], 0)
            for ref, i in ((q_ref, 0), (kv_ref, 0), (kv_ref, 1))
        )
        score = jnp.where(same, dot_t(query, key), -jnp.inf)
        top = jnp.max(score, axis=1, keepdims=True)
        weight = jnp.exp2((score - top) * FACTOR)
        total = jnp.sum(weight, axis=1, keepdims=True)
        summed = jnp.dot(weight.astype(BF16), value, preferred_element_type=F32)
        here = slice(g * n, (g + 1) * n)
        attn_ref[here] = summed / total
        top_ref[here] = jnp.broadcast_to(top, (n, DEPTH))
        total_ref[here] = jnp.broadcast_to(total, (n, DEPTH))


def attend_kernel(x_ref, kv_ref, out_ref, score, weight, top, total):
    side = lax.axis_index("patch") % SIDES
    row = lax.broadcasted_iota(jnp.int32, (BLOCK, BLOCK), 0)
    col = lax.broadcasted_iota(jnp.int32, (BLOCK, BLOCK), 1)
    same = row // TOK == col // TOK
    n = BLOCK // TOK
    steps = [slice(step * NEAR, (step + 1) * NEAR) for step in range(2)]
    for step in range(2):
        query = x_ref[:, step * TOK : (step + 1) * TOK, :].reshape(NEAR, DEPTH)
        for half in range(SIDES):
            keys = kv_ref[half, :, 0:TOK, :].reshape(NEAR, DEPTH)
            score[steps[step], half * NEAR : (half + 1) * NEAR] = dot_t(query, keys)
    for step in range(2):
        for i in range(NEAR // BLOCK):
            here = slice(step * NEAR + i * BLOCK, step * NEAR + (i + 1) * BLOCK)
            if step == 1:
                for half in range(SIDES):
                    cols = slice(half * NEAR + i * BLOCK, half * NEAR + (i + 1) * BLOCK)
                    own = jnp.logical_and(same, side == half)
                    score[here, cols] = jnp.where(own, -jnp.inf, score[here, cols])
            block = score[here]
            most = jnp.max(block, axis=1, keepdims=True)
            weights = jnp.exp2((block - most) * FACTOR)
            added = jnp.sum(weights, axis=1, keepdims=True)
            top[here] = jnp.broadcast_to(most, (BLOCK, DEPTH))
            total[here] = jnp.broadcast_to(added, (BLOCK, DEPTH))
            weight[here] = weights.astype(BF16)
    values = kv_ref[:, :, TOK:, :].reshape(TOKENS, DEPTH)
    for step in range(2):
        rows = steps[step]
        attn = jnp.dot(weight[rows], values, preferred_element_type=F32) / total[rows]
        out_ref[:, step * PAIRS : (step + 1) * PAIRS] = write_rows(attn)
    for i in range(NEAR // BLOCK):
        rows = slice(NEAR + i * BLOCK, NEAR + (i + 1) * BLOCK)
        out_ref[i * n : (i + 1) * n, 2 * PAIRS] = write_stats(top[rows], total[rows])


def merge_kernel(y_ref, near_ref, top_ref, total_ref, out_ref):
    lower = lax.broadcasted_iota(jnp.int32, (NEAR, DEPTH), 1) < HALF
    first = read_rows(y_ref[:, 0:PAIRS])
    far = read_rows(y_ref[:, PAIRS : 2 * PAIRS])
    far_top, far_total = read_stats(y_ref[:, 2 * PAIRS])
    near_top = top_ref[...]
    top = jnp.maximum(far_top, near_top)
    far_share = jnp.exp2((far_top - top) * FACTOR) * far_total
    near_share = jnp.exp2((near_top - top) * FACTOR) * total_ref[...]
    second = (far_share * far + near_share * near_ref[...]) / (far_share + near_share)
    out_ref[0] = jnp.where(lower, first, pltpu.roll(second, HALF, 1)).astype(BF16)
    out_ref[1] = jnp.where(lower, pltpu.roll(first, HALF, 1), second).astype(BF16)


def guide_kernel(both_ref, gate_ref, out_ref, held):
    core = lax.axis_index("cfg")
    cond = both_ref[0, core].astype(F32)
    uncond = both_ref[1, core].astype(F32)
    mixed = (uncond + 5.0 * (cond - uncond)).reshape(HEADS, TOK, DEPTH)
    held[...] = (gate_ref[...].reshape(HEADS, 1, DEPTH) * mixed).reshape(NEAR, DEPTH)
    for t in range(TOK):
        rows = held[pl.ds(t, HEADS, stride=TOK), :]
        out_ref[0, t] = rows[:, :HALF].astype(BF16)
        out_ref[1, t] = rows[:, HALF:].astype(BF16)


def call(kernel, out, args, specs=None, scratch=(), flops=0, out_space=pltpu.VMEM, limit=32):
    many = isinstance(out, list)
    shapes = out if many else [out]
    moved = sum(a.size * a.dtype.itemsize for a in list(args) + list(shapes))
    vmem = pl.BlockSpec(memory_space=pltpu.VMEM)
    result = pl.BlockSpec(memory_space=out_space)
    return pl.pallas_call(
        kernel,
        grid=(1,),
        out_shape=out,
        in_specs=specs or [vmem] * len(args),
        out_specs=[result] * len(shapes) if many else result,
        scratch_shapes=list(scratch),
        cost_estimate=pl.CostEstimate(flops=flops, bytes_accessed=moved, transcendentals=0),
        compiler_params=pltpu.CompilerParams(vmem_limit_bytes=limit << 20),
    )(*args)


def body(queries, keys_values, timesteps, gate_table):
    width = HEADS * DEPTH
    sides = [[SIDES * i + side for i in range(HEADS)] for side in range(SIDES)]
    patches = SIDES * HEADS
    whole = pl.BlockSpec(memory_space=pltpu.HBM)
    sent = call(
        pack_kernel,
        SHAPE((HEADS, 4 * TOK, DEPTH), BF16),
        (queries, keys_values),
        [whole, whole],
        [
            pltpu.VMEM((4, TOK, width), BF16),
            pltpu.VMEM((4, HEADS, TOK, DEPTH), BF16),
            pltpu.SemaphoreType.DMA((4,)),
            pltpu.SemaphoreType.DMA((4,)),
        ],
        out_space=pltpu.HBM,
        limit=60,
    )
    held = lax.all_to_all(
        sent, "patch", split_axis=0, concat_axis=0, tiled=True, axis_index_groups=sides
    )
    near = call(
        local_kernel,
        [SHAPE((NEAR, DEPTH), F32)] * 3,
        (queries, keys_values),
        [
            pl.BlockSpec((None, 1, TOK, width), lambda i: (0, 1, 0, 0)),
            pl.BlockSpec((None, None, 2, TOK, width), lambda i: (0, 1, 0, 0, 0)),
        ],
    )
    gates = jnp.take(gate_table, timesteps, axis=0, mode="clip").reshape(2, HEADS, 2, HALF)
    gate = lax.dynamic_index_in_dim(gates, lax.axis_index("cfg"), 2, keepdims=False)
    gate = jnp.concatenate([gate[0], gate[1]], axis=1)
    held, near, gate = lax.optimization_barrier((held, near, gate))
    pairs = [[SIDES * i, SIDES * i + 1] for i in range(HEADS)]
    stale = lax.all_gather(
        held[:, 2 * TOK :, :], "patch", axis=0, tiled=False, axis_index_groups=pairs
    )
    far = call(
        attend_kernel,
        SHAPE((HEADS, 2 * PAIRS + 1, 2, DEPTH), BF16),
        (held, stale),
        scratch=[
            pltpu.VMEM((ROWS, TOKENS), F32),
            pltpu.VMEM((ROWS, TOKENS), BF16),
            pltpu.VMEM((ROWS, DEPTH), F32),
            pltpu.VMEM((ROWS, DEPTH), F32),
        ],
        flops=4 * ROWS * TOKENS * DEPTH,
    )
    back = lax.all_to_all(
        far, "patch", split_axis=0, concat_axis=0, tiled=True, axis_index_groups=sides
    )
    attn = call(merge_kernel, SHAPE((2, NEAR, DEPTH), BF16), (back, *near))
    both = lax.all_gather(attn, "cfg", axis=0, tiled=False)
    return call(
        guide_kernel,
        SHAPE((2, TOK, HEADS, HALF), BF16),
        (both, gate),
        scratch=[pltpu.VMEM((NEAR, DEPTH), F32)],
    )


def solution(mesh):
    placed = (
        P("cfg", None, ("clip", "patch"), None),
        P("cfg", None, None, ("clip", "patch"), None),
        P("clip"),
        P(),
    )
    return jax.shard_map(
        body,
        mesh=mesh,
        in_specs=placed,
        out_specs=P(None, ("clip", "patch"), None, "cfg"),
        check_vma=False,
    )
```

```python
import math

import jax
import jax.numpy as jnp
from jax import lax
from jax.experimental import pallas as pl
from jax.experimental.pallas import tpu as pltpu
from jax.sharding import PartitionSpec as P

HEADS = 32
DEPTH = 128
HALF = DEPTH // 2
TOK = 16
SIDES = 2
NEAR = HEADS * TOK
ROWS = 2 * NEAR
PAIRS = TOK // 2
SLOTS = DEPTH // TOK
GROUP = 8
TOKENS = SIDES * NEAR
BLOCK = 128
FACTOR = math.log2(math.e) / math.sqrt(DEPTH)
BF16 = jnp.bfloat16
F32 = jnp.float32
SHAPE = jax.ShapeDtypeStruct


def dot_t(a, b):
    return lax.dot_general(a, b, (((1,), (1,)), ((), ())), preferred_element_type=F32)


def pack_kernel(q_ref, kv_ref, out_ref, held, packed, in_sems, out_sems):
    fields = [q_ref.at[0, 0], q_ref.at[0, 1], kv_ref.at[0, 0, 0], kv_ref.at[0, 0, 1]]
    loads = [
        pltpu.make_async_copy(field, held.at[i], in_sems.at[i]) for i, field in enumerate(fields)
    ]
    stores = [
        pltpu.make_async_copy(
            packed.at[i], out_ref.at[:, i * TOK : (i + 1) * TOK, :], out_sems.at[i]
        )
        for i in range(len(fields))
    ]

    def by_head(i):
        for h in range(HEADS):
            packed[i, h] = held[i, :, h * DEPTH : (h + 1) * DEPTH]

    first = lax.axis_index("cfg") == 0

    @pl.when(first)
    def _():
        for load in loads:
            load.start()
        for i, load in enumerate(loads):
            load.wait()
            by_head(i)
            stores[i].start()
        for store in stores:
            store.wait()

    @pl.when(jnp.logical_not(first))
    def _():
        for i, load in enumerate(loads):
            load.start()
            load.wait()
            by_head(i)
            stores[i].start()
            stores[i].wait()


def split_value(value):
    high = value.astype(BF16).astype(F32)
    rest = value - high
    mid = rest.astype(BF16).astype(F32)
    return high, mid, rest - mid


def write_stats(top, total):
    rows = top.shape[0]
    n = rows // TOK
    lane = lax.broadcasted_iota(jnp.int32, (rows, DEPTH), 1)
    token = lax.broadcasted_iota(jnp.int32, (rows, DEPTH), 0) % TOK
    slot = jnp.where(lane // SLOTS == token, lane % SLOTS, SLOTS)
    value = jnp.where(slot < 3, top, total)
    high, mid, low = split_value(value)
    piece = jnp.where(slot % 3 == 0, high, jnp.where(slot % 3 == 1, mid, low))
    piece = jnp.where(slot < 6, piece, 0.0).astype(BF16)
    out_row = lax.broadcasted_iota(jnp.int32, (2 * n, rows), 0)
    in_row = lax.broadcasted_iota(jnp.int32, (2 * n, rows), 1)
    gather = jnp.where(out_row == in_row // TOK * 2, 1.0, 0.0).astype(BF16)
    return jnp.dot(gather, piece, preferred_element_type=F32).reshape(n, 2, DEPTH).astype(BF16)


def read_stats(stats):
    n = stats.shape[0]
    out_row = lax.broadcasted_iota(jnp.int32, (n * TOK, 2 * n), 0)
    in_row = lax.broadcasted_iota(jnp.int32, (n * TOK, 2 * n), 1)
    spread = jnp.where(in_row == out_row // TOK * 2, 1.0, 0.0).astype(BF16)
    flat = stats.astype(F32).reshape(2 * n, DEPTH).astype(BF16)
    wide = jnp.dot(spread, flat, preferred_element_type=F32)
    lane = lax.broadcasted_iota(jnp.int32, (n * TOK, DEPTH), 1)
    token = lax.broadcasted_iota(jnp.int32, (n * TOK, DEPTH), 0) % TOK
    wide = jnp.where(lane // SLOTS == token, wide, 0.0).astype(BF16)
    slot = lax.broadcasted_iota(jnp.int32, (DEPTH, 2 * DEPTH), 0) % SLOTS
    part = lax.broadcasted_iota(jnp.int32, (DEPTH, 2 * DEPTH), 1) // DEPTH
    pick = jnp.where(jnp.logical_and(slot < 6, slot // 3 == part), 1.0, 0.0).astype(BF16)
    both = jnp.dot(wide, pick, preferred_element_type=F32)
    return both[:, :DEPTH], both[:, DEPTH:]


def write_rows(rows):
    return rows.reshape(-1, TOK // 2, 2, DEPTH).astype(BF16)


def read_rows(pairs):
    return pairs.astype(F32).reshape(-1, DEPTH)


def local_kernel(q_ref, kv_ref, attn_ref, top_ref, total_ref):
    n = GROUP * TOK
    row = lax.broadcasted_iota(jnp.int32, (n, n), 0)
    col = lax.broadcasted_iota(jnp.int32, (n, n), 1)
    same = row // TOK == col // TOK

    for g in range(HEADS // GROUP):
        heads = range(g * GROUP, (g + 1) * GROUP)
        query, key, value = (
            jnp.concatenate([ref[i, :, h * DEPTH : (h + 1) * DEPTH] for h in heads], 0)
            for ref, i in ((q_ref, 0), (kv_ref, 0), (kv_ref, 1))
        )
        score = jnp.where(same, dot_t(query, key), -jnp.inf)
        top = jnp.max(score, axis=1, keepdims=True)
        weight = jnp.exp2((score - top) * FACTOR)
        total = jnp.sum(weight, axis=1, keepdims=True)
        summed = jnp.dot(weight.astype(BF16), value, preferred_element_type=F32)
        here = slice(g * n, (g + 1) * n)
        attn_ref[here] = summed / total
        top_ref[here] = jnp.broadcast_to(top, (n, DEPTH))
        total_ref[here] = jnp.broadcast_to(total, (n, DEPTH))


def attend_kernel(x_ref, kv_ref, out_ref, score, weight, top, total):
    side = lax.axis_index("patch") % SIDES
    row = lax.broadcasted_iota(jnp.int32, (BLOCK, BLOCK), 0)
    col = lax.broadcasted_iota(jnp.int32, (BLOCK, BLOCK), 1)
    same = row // TOK == col // TOK
    n = BLOCK // TOK
    steps = [slice(step * NEAR, (step + 1) * NEAR) for step in range(2)]
    for step in range(2):
        query = x_ref[:, step * TOK : (step + 1) * TOK, :].reshape(NEAR, DEPTH)
        for half in range(SIDES):
            keys = kv_ref[half, :, 0:TOK, :].reshape(NEAR, DEPTH)
            score[steps[step], half * NEAR : (half + 1) * NEAR] = dot_t(query, keys)
    for step in range(2):
        for i in range(NEAR // BLOCK):
            here = slice(step * NEAR + i * BLOCK, step * NEAR + (i + 1) * BLOCK)
            if step == 1:
                for half in range(SIDES):
                    cols = slice(half * NEAR + i * BLOCK, half * NEAR + (i + 1) * BLOCK)
                    own = jnp.logical_and(same, side == half)
                    score[here, cols] = jnp.where(own, -jnp.inf, score[here, cols])
            block = score[here]
            most = jnp.max(block, axis=1, keepdims=True)
            weights = jnp.exp2((block - most) * FACTOR)
            added = jnp.sum(weights, axis=1, keepdims=True)
            top[here] = jnp.broadcast_to(most, (BLOCK, DEPTH))
            total[here] = jnp.broadcast_to(added, (BLOCK, DEPTH))
            weight[here] = weights.astype(BF16)
    values = kv_ref[:, :, TOK:, :].reshape(TOKENS, DEPTH)
    for step in range(2):
        rows = steps[step]
        attn = jnp.dot(weight[rows], values, preferred_element_type=F32) / total[rows]
        out_ref[:, step * PAIRS : (step + 1) * PAIRS] = write_rows(attn)
    for i in range(NEAR // BLOCK):
        rows = slice(NEAR + i * BLOCK, NEAR + (i + 1) * BLOCK)
        out_ref[i * n : (i + 1) * n, 2 * PAIRS] = write_stats(top[rows], total[rows])


def merge_kernel(y_ref, near_ref, top_ref, total_ref, out_ref):
    lower = lax.broadcasted_iota(jnp.int32, (NEAR, DEPTH), 1) < HALF
    first = read_rows(y_ref[:, 0:PAIRS])
    far = read_rows(y_ref[:, PAIRS : 2 * PAIRS])
    far_top, far_total = read_stats(y_ref[:, 2 * PAIRS])
    near_top = top_ref[...]
    top = jnp.maximum(far_top, near_top)
    far_share = jnp.exp2((far_top - top) * FACTOR) * far_total
    near_share = jnp.exp2((near_top - top) * FACTOR) * total_ref[...]
    second = (far_share * far + near_share * near_ref[...]) / (far_share + near_share)
    out_ref[0] = jnp.where(lower, first, pltpu.roll(second, HALF, 1)).astype(BF16)
    out_ref[1] = jnp.where(lower, pltpu.roll(first, HALF, 1), second).astype(BF16)


def guide_kernel(both_ref, gate_ref, out_ref, held):
    core = lax.axis_index("cfg")
    cond = both_ref[0, core].astype(F32)
    uncond = both_ref[1, core].astype(F32)
    mixed = (uncond + 5.0 * (cond - uncond)).reshape(HEADS, TOK, DEPTH)
    held[...] = (gate_ref[...].reshape(HEADS, 1, DEPTH) * mixed).reshape(NEAR, DEPTH)
    for t in range(TOK):
        rows = held[pl.ds(t, HEADS, stride=TOK), :]
        out_ref[0, t] = rows[:, :HALF].astype(BF16)
        out_ref[1, t] = rows[:, HALF:].astype(BF16)


def call(kernel, out, args, specs=None, scratch=(), flops=0, out_space=pltpu.VMEM, limit=32):
    many = isinstance(out, list)
    shapes = out if many else [out]
    moved = sum(a.size * a.dtype.itemsize for a in list(args) + list(shapes))
    vmem = pl.BlockSpec(memory_space=pltpu.VMEM)
    result = pl.BlockSpec(memory_space=out_space)
    return pl.pallas_call(
        kernel,
        grid=(1,),
        out_shape=out,
        in_specs=specs or [vmem] * len(args),
        out_specs=[result] * len(shapes) if many else result,
        scratch_shapes=list(scratch),
        cost_estimate=pl.CostEstimate(flops=flops, bytes_accessed=moved, transcendentals=0),
        compiler_params=pltpu.CompilerParams(vmem_limit_bytes=limit << 20),
    )(*args)


def body(queries, keys_values, timesteps, gate_table):
    width = HEADS * DEPTH
    sides = [[SIDES * i + side for i in range(HEADS)] for side in range(SIDES)]
    patches = SIDES * HEADS
    whole = pl.BlockSpec(memory_space=pltpu.HBM)
    sent = call(
        pack_kernel,
        SHAPE((HEADS, 4 * TOK, DEPTH), BF16),
        (queries, keys_values),
        [whole, whole],
        [
            pltpu.VMEM((4, TOK, width), BF16),
            pltpu.VMEM((4, HEADS, TOK, DEPTH), BF16),
            pltpu.SemaphoreType.DMA((4,)),
            pltpu.SemaphoreType.DMA((4,)),
        ],
        out_space=pltpu.HBM,
        limit=60,
    )
    held = lax.all_to_all(
        sent, "patch", split_axis=0, concat_axis=0, tiled=True, axis_index_groups=sides
    )
    near = call(
        local_kernel,
        [SHAPE((NEAR, DEPTH), F32)] * 3,
        (queries, keys_values),
        [
            pl.BlockSpec((None, 1, TOK, width), lambda i: (0, 1, 0, 0)),
            pl.BlockSpec((None, None, 2, TOK, width), lambda i: (0, 1, 0, 0, 0)),
        ],
    )
    gates = jnp.take(gate_table, timesteps, axis=0, mode="clip").reshape(2, HEADS, 2, HALF)
    gate = lax.dynamic_index_in_dim(gates, lax.axis_index("cfg"), 2, keepdims=False)
    gate = jnp.concatenate([gate[0], gate[1]], axis=1)
    held, near, gate = lax.optimization_barrier((held, near, gate))
    pairs = [[SIDES * i, SIDES * i + 1] for i in range(HEADS)]
    stale = lax.all_gather(
        held[:, 2 * TOK :, :], "patch", axis=0, tiled=False, axis_index_groups=pairs
    )
    far = call(
        attend_kernel,
        SHAPE((HEADS, 2 * PAIRS + 1, 2, DEPTH), BF16),
        (held, stale),
        scratch=[
            pltpu.VMEM((ROWS, TOKENS), F32),
            pltpu.VMEM((ROWS, TOKENS), BF16),
            pltpu.VMEM((ROWS, DEPTH), F32),
            pltpu.VMEM((ROWS, DEPTH), F32),
        ],
        flops=4 * ROWS * TOKENS * DEPTH,
    )
    back = lax.all_to_all(
        far, "patch", split_axis=0, concat_axis=0, tiled=True, axis_index_groups=sides
    )
    attn = call(merge_kernel, SHAPE((2, NEAR, DEPTH), BF16), (back, *near))
    both = lax.all_gather(attn, "cfg", axis=0, tiled=False)
    return call(
        guide_kernel,
        SHAPE((2, TOK, HEADS, HALF), BF16),
        (both, gate),
        scratch=[pltpu.VMEM((NEAR, DEPTH), F32)],
    )


def solution(mesh):
    placed = (
        P("cfg", None, ("clip", "patch"), None),
        P("cfg", None, None, ("clip", "patch"), None),
        P("clip"),
        P(),
    )
    return jax.shard_map(
        body,
        mesh=mesh,
        in_specs=placed,
        out_specs=P(None, ("clip", "patch"), None, "cfg"),
        check_vma=False,
    )
```

```python
import math

import jax
import jax.numpy as jnp
from jax import lax
from jax.experimental import pallas as pl
from jax.experimental.pallas import tpu as pltpu
from jax.sharding import PartitionSpec as P

HEADS = 32
DEPTH = 128
HALF = DEPTH // 2
TOK = 16
SIDES = 2
NEAR = HEADS * TOK
ROWS = 2 * NEAR
PAIRS = TOK // 2
SLOTS = DEPTH // TOK
GROUP = 8
TOKENS = SIDES * NEAR
BLOCK = 128
FACTOR = math.log2(math.e) / math.sqrt(DEPTH)
BF16 = jnp.bfloat16
F32 = jnp.float32
SHAPE = jax.ShapeDtypeStruct


def dot_t(a, b):
    return lax.dot_general(a, b, (((1,), (1,)), ((), ())), preferred_element_type=F32)


def pack_kernel(q_ref, kv_ref, out_ref, held, packed, in_sems, out_sems):
    fields = [q_ref.at[0, 0], q_ref.at[0, 1], kv_ref.at[0, 0, 0], kv_ref.at[0, 0, 1]]
    loads = [
        pltpu.make_async_copy(field, held.at[i], in_sems.at[i]) for i, field in enumerate(fields)
    ]
    stores = [
        pltpu.make_async_copy(
            packed.at[i], out_ref.at[:, i * TOK : (i + 1) * TOK, :], out_sems.at[i]
        )
        for i in range(len(fields))
    ]

    def by_head(i):
        for h in range(HEADS):
            packed[i, h] = held[i, :, h * DEPTH : (h + 1) * DEPTH]

    odd = lax.axis_index("cfg") == 1

    @pl.when(odd)
    def _():
        for load in loads:
            load.start()
        for i, load in enumerate(loads):
            load.wait()
            by_head(i)
            stores[i].start()
        for store in stores:
            store.wait()

    @pl.when(jnp.logical_not(odd))
    def _():
        for group in ((0,), (1,), (2, 3)):
            for i in group:
                loads[i].start()
            for i in group:
                loads[i].wait()
                by_head(i)
                stores[i].start()
            for i in group:
                stores[i].wait()


def split_value(value):
    high = value.astype(BF16).astype(F32)
    rest = value - high
    mid = rest.astype(BF16).astype(F32)
    return high, mid, rest - mid


def write_stats(top, total):
    rows = top.shape[0]
    n = rows // TOK
    lane = lax.broadcasted_iota(jnp.int32, (rows, DEPTH), 1)
    token = lax.broadcasted_iota(jnp.int32, (rows, DEPTH), 0) % TOK
    slot = jnp.where(lane // SLOTS == token, lane % SLOTS, SLOTS)
    value = jnp.where(slot < 3, top, total)
    high, mid, low = split_value(value)
    piece = jnp.where(slot % 3 == 0, high, jnp.where(slot % 3 == 1, mid, low))
    piece = jnp.where(slot < 6, piece, 0.0).astype(BF16)
    out_row = lax.broadcasted_iota(jnp.int32, (2 * n, rows), 0)
    in_row = lax.broadcasted_iota(jnp.int32, (2 * n, rows), 1)
    gather = jnp.where(out_row == in_row // TOK * 2, 1.0, 0.0).astype(BF16)
    return jnp.dot(gather, piece, preferred_element_type=F32).reshape(n, 2, DEPTH).astype(BF16)


def read_stats(stats):
    n = stats.shape[0]
    out_row = lax.broadcasted_iota(jnp.int32, (n * TOK, 2 * n), 0)
    in_row = lax.broadcasted_iota(jnp.int32, (n * TOK, 2 * n), 1)
    spread = jnp.where(in_row == out_row // TOK * 2, 1.0, 0.0).astype(BF16)
    flat = stats.astype(F32).reshape(2 * n, DEPTH).astype(BF16)
    wide = jnp.dot(spread, flat, preferred_element_type=F32)
    lane = lax.broadcasted_iota(jnp.int32, (n * TOK, DEPTH), 1)
    token = lax.broadcasted_iota(jnp.int32, (n * TOK, DEPTH), 0) % TOK
    wide = jnp.where(lane // SLOTS == token, wide, 0.0).astype(BF16)
    slot = lax.broadcasted_iota(jnp.int32, (DEPTH, 2 * DEPTH), 0) % SLOTS
    part = lax.broadcasted_iota(jnp.int32, (DEPTH, 2 * DEPTH), 1) // DEPTH
    pick = jnp.where(jnp.logical_and(slot < 6, slot // 3 == part), 1.0, 0.0).astype(BF16)
    both = jnp.dot(wide, pick, preferred_element_type=F32)
    return both[:, :DEPTH], both[:, DEPTH:]


def write_rows(rows):
    return rows.reshape(-1, TOK // 2, 2, DEPTH).astype(BF16)


def read_rows(pairs):
    return pairs.astype(F32).reshape(-1, DEPTH)


def local_kernel(q_ref, kv_ref, attn_ref, top_ref, total_ref):
    n = GROUP * TOK
    row = lax.broadcasted_iota(jnp.int32, (n, n), 0)
    col = lax.broadcasted_iota(jnp.int32, (n, n), 1)
    same = row // TOK == col // TOK

    for g in range(HEADS // GROUP):
        heads = range(g * GROUP, (g + 1) * GROUP)
        query, key, value = (
            jnp.concatenate([ref[i, :, h * DEPTH : (h + 1) * DEPTH] for h in heads], 0)
            for ref, i in ((q_ref, 0), (kv_ref, 0), (kv_ref, 1))
        )
        score = jnp.where(same, dot_t(query, key), -jnp.inf)
        top = jnp.max(score, axis=1, keepdims=True)
        weight = jnp.exp2((score - top) * FACTOR)
        total = jnp.sum(weight, axis=1, keepdims=True)
        summed = jnp.dot(weight.astype(BF16), value, preferred_element_type=F32)
        here = slice(g * n, (g + 1) * n)
        attn_ref[here] = summed / total
        top_ref[here] = jnp.broadcast_to(top, (n, DEPTH))
        total_ref[here] = jnp.broadcast_to(total, (n, DEPTH))


def attend_kernel(x_ref, kv_ref, out_ref, score, weight, top, total):
    side = lax.axis_index("patch") % SIDES
    row = lax.broadcasted_iota(jnp.int32, (BLOCK, BLOCK), 0)
    col = lax.broadcasted_iota(jnp.int32, (BLOCK, BLOCK), 1)
    same = row // TOK == col // TOK
    n = BLOCK // TOK
    steps = [slice(step * NEAR, (step + 1) * NEAR) for step in range(2)]
    for step in range(2):
        query = x_ref[:, step * TOK : (step + 1) * TOK, :].reshape(NEAR, DEPTH)
        for half in range(SIDES):
            keys = kv_ref[half, :, 0:TOK, :].reshape(NEAR, DEPTH)
            score[steps[step], half * NEAR : (half + 1) * NEAR] = dot_t(query, keys)
    for step in range(2):
        for i in range(NEAR // BLOCK):
            here = slice(step * NEAR + i * BLOCK, step * NEAR + (i + 1) * BLOCK)
            if step == 1:
                for half in range(SIDES):
                    cols = slice(half * NEAR + i * BLOCK, half * NEAR + (i + 1) * BLOCK)
                    own = jnp.logical_and(same, side == half)
                    score[here, cols] = jnp.where(own, -jnp.inf, score[here, cols])
            block = score[here]
            most = jnp.max(block, axis=1, keepdims=True)
            weights = jnp.exp2((block - most) * FACTOR)
            added = jnp.sum(weights, axis=1, keepdims=True)
            top[here] = jnp.broadcast_to(most, (BLOCK, DEPTH))
            total[here] = jnp.broadcast_to(added, (BLOCK, DEPTH))
            weight[here] = weights.astype(BF16)
    values = kv_ref[:, :, TOK:, :].reshape(TOKENS, DEPTH)
    for step in range(2):
        rows = steps[step]
        attn = jnp.dot(weight[rows], values, preferred_element_type=F32) / total[rows]
        out_ref[:, step * PAIRS : (step + 1) * PAIRS] = write_rows(attn)
    for i in range(NEAR // BLOCK):
        rows = slice(NEAR + i * BLOCK, NEAR + (i + 1) * BLOCK)
        out_ref[i * n : (i + 1) * n, 2 * PAIRS] = write_stats(top[rows], total[rows])


def merge_kernel(y_ref, near_ref, top_ref, total_ref, out_ref):
    lower = lax.broadcasted_iota(jnp.int32, (NEAR, DEPTH), 1) < HALF
    first = read_rows(y_ref[:, 0:PAIRS])
    far = read_rows(y_ref[:, PAIRS : 2 * PAIRS])
    far_top, far_total = read_stats(y_ref[:, 2 * PAIRS])
    near_top = top_ref[...]
    top = jnp.maximum(far_top, near_top)
    far_share = jnp.exp2((far_top - top) * FACTOR) * far_total
    near_share = jnp.exp2((near_top - top) * FACTOR) * total_ref[...]
    second = (far_share * far + near_share * near_ref[...]) / (far_share + near_share)
    out_ref[0] = jnp.where(lower, first, pltpu.roll(second, HALF, 1)).astype(BF16)
    out_ref[1] = jnp.where(lower, pltpu.roll(first, HALF, 1), second).astype(BF16)


def guide_kernel(both_ref, gate_ref, out_ref, held):
    core = lax.axis_index("cfg")
    cond = both_ref[0, core].astype(F32)
    uncond = both_ref[1, core].astype(F32)
    mixed = (uncond + 5.0 * (cond - uncond)).reshape(HEADS, TOK, DEPTH)
    held[...] = (gate_ref[...].reshape(HEADS, 1, DEPTH) * mixed).reshape(NEAR, DEPTH)
    for t in range(TOK):
        rows = held[pl.ds(t, HEADS, stride=TOK), :]
        out_ref[0, t] = rows[:, :HALF].astype(BF16)
        out_ref[1, t] = rows[:, HALF:].astype(BF16)


def call(kernel, out, args, specs=None, scratch=(), flops=0, out_space=pltpu.VMEM, limit=32):
    many = isinstance(out, list)
    shapes = out if many else [out]
    moved = sum(a.size * a.dtype.itemsize for a in list(args) + list(shapes))
    vmem = pl.BlockSpec(memory_space=pltpu.VMEM)
    result = pl.BlockSpec(memory_space=out_space)
    return pl.pallas_call(
        kernel,
        grid=(1,),
        out_shape=out,
        in_specs=specs or [vmem] * len(args),
        out_specs=[result] * len(shapes) if many else result,
        scratch_shapes=list(scratch),
        cost_estimate=pl.CostEstimate(flops=flops, bytes_accessed=moved, transcendentals=0),
        compiler_params=pltpu.CompilerParams(vmem_limit_bytes=limit << 20),
    )(*args)


def body(queries, keys_values, timesteps, gate_table):
    width = HEADS * DEPTH
    sides = [[SIDES * i + side for i in range(HEADS)] for side in range(SIDES)]
    patches = SIDES * HEADS
    whole = pl.BlockSpec(memory_space=pltpu.HBM)
    sent = call(
        pack_kernel,
        SHAPE((HEADS, 4 * TOK, DEPTH), BF16),
        (queries, keys_values),
        [whole, whole],
        [
            pltpu.VMEM((4, TOK, width), BF16),
            pltpu.VMEM((4, HEADS, TOK, DEPTH), BF16),
            pltpu.SemaphoreType.DMA((4,)),
            pltpu.SemaphoreType.DMA((4,)),
        ],
        out_space=pltpu.HBM,
        limit=60,
    )
    held = lax.all_to_all(
        sent, "patch", split_axis=0, concat_axis=0, tiled=True, axis_index_groups=sides
    )
    near = call(
        local_kernel,
        [SHAPE((NEAR, DEPTH), F32)] * 3,
        (queries, keys_values),
        [
            pl.BlockSpec((None, 1, TOK, width), lambda i: (0, 1, 0, 0)),
            pl.BlockSpec((None, None, 2, TOK, width), lambda i: (0, 1, 0, 0, 0)),
        ],
    )
    gates = jnp.take(gate_table, timesteps, axis=0, mode="clip").reshape(2, HEADS, 2, HALF)
    gate = lax.dynamic_index_in_dim(gates, lax.axis_index("cfg"), 2, keepdims=False)
    gate = jnp.concatenate([gate[0], gate[1]], axis=1)
    held, near, gate = lax.optimization_barrier((held, near, gate))
    pairs = [[SIDES * i, SIDES * i + 1] for i in range(HEADS)]
    stale = lax.all_gather(
        held[:, 2 * TOK :, :], "patch", axis=0, tiled=False, axis_index_groups=pairs
    )
    far = call(
        attend_kernel,
        SHAPE((HEADS, 2 * PAIRS + 1, 2, DEPTH), BF16),
        (held, stale),
        scratch=[
            pltpu.VMEM((ROWS, TOKENS), F32),
            pltpu.VMEM((ROWS, TOKENS), BF16),
            pltpu.VMEM((ROWS, DEPTH), F32),
            pltpu.VMEM((ROWS, DEPTH), F32),
        ],
        flops=4 * ROWS * TOKENS * DEPTH,
    )
    back = lax.all_to_all(
        far, "patch", split_axis=0, concat_axis=0, tiled=True, axis_index_groups=sides
    )
    attn = call(merge_kernel, SHAPE((2, NEAR, DEPTH), BF16), (back, *near))
    both = lax.all_gather(attn, "cfg", axis=0, tiled=False)
    return call(
        guide_kernel,
        SHAPE((2, TOK, HEADS, HALF), BF16),
        (both, gate),
        scratch=[pltpu.VMEM((NEAR, DEPTH), F32)],
    )


def solution(mesh):
    placed = (
        P("cfg", None, ("clip", "patch"), None),
        P("cfg", None, None, ("clip", "patch"), None),
        P("clip"),
        P(),
    )
    return jax.shard_map(
        body,
        mesh=mesh,
        in_specs=placed,
        out_specs=P(None, ("clip", "patch"), None, "cfg"),
        check_vma=False,
    )
```

```python
import math

import jax
import jax.numpy as jnp
from jax import lax
from jax.experimental import pallas as pl
from jax.experimental.pallas import tpu as pltpu
from jax.sharding import PartitionSpec as P

HEADS = 32
DEPTH = 128
HALF = DEPTH // 2
TOK = 16
SIDES = 2
Y_FIRST = 1
NEAR = HEADS * TOK
ROWS = 2 * NEAR
PAIRS = TOK // 2
SLOTS = DEPTH // TOK
GROUP = 8
TOKENS = SIDES * NEAR
BLOCK = 128
FACTOR = math.log2(math.e) / math.sqrt(DEPTH)
BF16 = jnp.bfloat16
F32 = jnp.float32
SHAPE = jax.ShapeDtypeStruct


def dot_t(a, b):
    return lax.dot_general(a, b, (((1,), (1,)), ((), ())), preferred_element_type=F32)


def pack_kernel(fields, out_ref, held, packed, in_sems, out_sems):
    loads = [
        pltpu.make_async_copy(field, held.at[i], in_sems.at[i]) for i, field in enumerate(fields)
    ]
    for load in loads:
        load.start()
    stores = []
    for i, load in enumerate(loads):
        load.wait()
        for h in range(HEADS):
            packed[i, h] = held[i, :, h * DEPTH : (h + 1) * DEPTH]
        rows = out_ref.at[:, i * TOK : (i + 1) * TOK, :]
        stores.append(pltpu.make_async_copy(packed.at[i], rows, out_sems.at[i]))
        stores[-1].start()
    for store in stores:
        store.wait()


def pack_own_kernel(q_ref, kv_ref, *refs):
    pack_kernel([q_ref.at[0, i] for i in range(2)] + [kv_ref.at[0, 0, i] for i in range(2)], *refs)


def pack_both_kernel(q_ref, stale_ref, *refs):
    fields = [q_ref.at[0, i] for i in range(2)]
    fields += [stale_ref.at[side, i] for side in range(SIDES) for i in range(2)]
    pack_kernel(fields, *refs)


def split_value(value):
    high = value.astype(BF16).astype(F32)
    rest = value - high
    mid = rest.astype(BF16).astype(F32)
    return high, mid, rest - mid


def write_stats(top, total):
    rows = top.shape[0]
    n = rows // TOK
    lane = lax.broadcasted_iota(jnp.int32, (rows, DEPTH), 1)
    token = lax.broadcasted_iota(jnp.int32, (rows, DEPTH), 0) % TOK
    slot = jnp.where(lane // SLOTS == token, lane % SLOTS, SLOTS)
    value = jnp.where(slot < 3, top, total)
    high, mid, low = split_value(value)
    piece = jnp.where(slot % 3 == 0, high, jnp.where(slot % 3 == 1, mid, low))
    piece = jnp.where(slot < 6, piece, 0.0).astype(BF16)
    out_row = lax.broadcasted_iota(jnp.int32, (2 * n, rows), 0)
    in_row = lax.broadcasted_iota(jnp.int32, (2 * n, rows), 1)
    gather = jnp.where(out_row == in_row // TOK * 2, 1.0, 0.0).astype(BF16)
    return jnp.dot(gather, piece, preferred_element_type=F32).reshape(n, 2, DEPTH).astype(BF16)


def read_stats(stats):
    n = stats.shape[0]
    out_row = lax.broadcasted_iota(jnp.int32, (n * TOK, 2 * n), 0)
    in_row = lax.broadcasted_iota(jnp.int32, (n * TOK, 2 * n), 1)
    spread = jnp.where(in_row == out_row // TOK * 2, 1.0, 0.0).astype(BF16)
    flat = stats.astype(F32).reshape(2 * n, DEPTH).astype(BF16)
    wide = jnp.dot(spread, flat, preferred_element_type=F32)
    lane = lax.broadcasted_iota(jnp.int32, (n * TOK, DEPTH), 1)
    token = lax.broadcasted_iota(jnp.int32, (n * TOK, DEPTH), 0) % TOK
    wide = jnp.where(lane // SLOTS == token, wide, 0.0).astype(BF16)
    slot = lax.broadcasted_iota(jnp.int32, (DEPTH, 2 * DEPTH), 0) % SLOTS
    part = lax.broadcasted_iota(jnp.int32, (DEPTH, 2 * DEPTH), 1) // DEPTH
    pick = jnp.where(jnp.logical_and(slot < 6, slot // 3 == part), 1.0, 0.0).astype(BF16)
    both = jnp.dot(wide, pick, preferred_element_type=F32)
    return both[:, :DEPTH], both[:, DEPTH:]


def write_rows(rows):
    return rows.reshape(-1, TOK // 2, 2, DEPTH).astype(BF16)


def read_rows(pairs):
    return pairs.astype(F32).reshape(-1, DEPTH)


def local_kernel(q_ref, kv_ref, attn_ref, top_ref, total_ref):
    n = GROUP * TOK
    row = lax.broadcasted_iota(jnp.int32, (n, n), 0)
    col = lax.broadcasted_iota(jnp.int32, (n, n), 1)
    same = row // TOK == col // TOK

    for g in range(HEADS // GROUP):
        heads = range(g * GROUP, (g + 1) * GROUP)
        query, key, value = (
            jnp.concatenate([ref[i, :, h * DEPTH : (h + 1) * DEPTH] for h in heads], 0)
            for ref, i in ((q_ref, 0), (kv_ref, 0), (kv_ref, 1))
        )
        score = jnp.where(same, dot_t(query, key), -jnp.inf)
        top = jnp.max(score, axis=1, keepdims=True)
        weight = jnp.exp2((score - top) * FACTOR)
        total = jnp.sum(weight, axis=1, keepdims=True)
        summed = jnp.dot(weight.astype(BF16), value, preferred_element_type=F32)
        here = slice(g * n, (g + 1) * n)
        attn_ref[here] = summed / total
        top_ref[here] = jnp.broadcast_to(top, (n, DEPTH))
        total_ref[here] = jnp.broadcast_to(total, (n, DEPTH))


def attend_own_kernel(x_ref, kv_ref, *refs):
    attend(x_ref, [kv_ref.at[half] for half in range(SIDES)], *refs)


def attend_both_kernel(x_ref, *refs):
    pair = 2 * TOK
    attend(x_ref, [x_ref.at[:, pair * (1 + half) : pair * (2 + half), :] for half in range(SIDES)], *refs)


def attend(x_ref, pairs, out_ref, score, weight, top, total):
    side = lax.axis_index("patch") % SIDES
    row = lax.broadcasted_iota(jnp.int32, (BLOCK, BLOCK), 0)
    col = lax.broadcasted_iota(jnp.int32, (BLOCK, BLOCK), 1)
    same = row // TOK == col // TOK
    n = BLOCK // TOK
    steps = [slice(step * NEAR, (step + 1) * NEAR) for step in range(2)]
    for step in range(2):
        query = x_ref[:, step * TOK : (step + 1) * TOK, :].reshape(NEAR, DEPTH)
        for half in range(SIDES):
            keys = pairs[half][:, 0:TOK, :].reshape(NEAR, DEPTH)
            score[steps[step], half * NEAR : (half + 1) * NEAR] = dot_t(query, keys)
    for step in range(2):
        for i in range(NEAR // BLOCK):
            here = slice(step * NEAR + i * BLOCK, step * NEAR + (i + 1) * BLOCK)
            if step == 1:
                for half in range(SIDES):
                    cols = slice(half * NEAR + i * BLOCK, half * NEAR + (i + 1) * BLOCK)
                    own = jnp.logical_and(same, side == half)
                    score[here, cols] = jnp.where(own, -jnp.inf, score[here, cols])
            block = score[here]
            most = jnp.max(block, axis=1, keepdims=True)
            weights = jnp.exp2((block - most) * FACTOR)
            added = jnp.sum(weights, axis=1, keepdims=True)
            top[here] = jnp.broadcast_to(most, (BLOCK, DEPTH))
            total[here] = jnp.broadcast_to(added, (BLOCK, DEPTH))
            weight[here] = weights.astype(BF16)
    values = jnp.concatenate([pair[:, TOK:, :].reshape(NEAR, DEPTH) for pair in pairs], 0)
    for step in range(2):
        rows = steps[step]
        attn = jnp.dot(weight[rows], values, preferred_element_type=F32) / total[rows]
        out_ref[:, step * PAIRS : (step + 1) * PAIRS] = write_rows(attn)
    for i in range(NEAR // BLOCK):
        rows = slice(NEAR + i * BLOCK, NEAR + (i + 1) * BLOCK)
        out_ref[i * n : (i + 1) * n, 2 * PAIRS] = write_stats(top[rows], total[rows])


def merge_kernel(y_ref, near_ref, top_ref, total_ref, out_ref):
    lower = lax.broadcasted_iota(jnp.int32, (NEAR, DEPTH), 1) < HALF
    first = read_rows(y_ref[:, 0:PAIRS])
    far = read_rows(y_ref[:, PAIRS : 2 * PAIRS])
    far_top, far_total = read_stats(y_ref[:, 2 * PAIRS])
    near_top = top_ref[...]
    top = jnp.maximum(far_top, near_top)
    far_share = jnp.exp2((far_top - top) * FACTOR) * far_total
    near_share = jnp.exp2((near_top - top) * FACTOR) * total_ref[...]
    second = (far_share * far + near_share * near_ref[...]) / (far_share + near_share)
    out_ref[0] = jnp.where(lower, first, pltpu.roll(second, HALF, 1)).astype(BF16)
    out_ref[1] = jnp.where(lower, pltpu.roll(first, HALF, 1), second).astype(BF16)


def guide_kernel(both_ref, gate_ref, out_ref, held):
    core = lax.axis_index("cfg")
    cond = both_ref[0, core].astype(F32)
    uncond = both_ref[1, core].astype(F32)
    mixed = (uncond + 5.0 * (cond - uncond)).reshape(HEADS, TOK, DEPTH)
    held[...] = (gate_ref[...].reshape(HEADS, 1, DEPTH) * mixed).reshape(NEAR, DEPTH)
    for t in range(TOK):
        rows = held[pl.ds(t, HEADS, stride=TOK), :]
        out_ref[0, t] = rows[:, :HALF].astype(BF16)
        out_ref[1, t] = rows[:, HALF:].astype(BF16)


def call(kernel, out, args, specs=None, scratch=(), flops=0, out_space=pltpu.VMEM, limit=32):
    many = isinstance(out, list)
    shapes = out if many else [out]
    moved = sum(a.size * a.dtype.itemsize for a in list(args) + list(shapes))
    vmem = pl.BlockSpec(memory_space=pltpu.VMEM)
    result = pl.BlockSpec(memory_space=out_space)
    return pl.pallas_call(
        kernel,
        grid=(1,),
        out_shape=out,
        in_specs=specs or [vmem] * len(args),
        out_specs=[result] * len(shapes) if many else result,
        scratch_shapes=list(scratch),
        cost_estimate=pl.CostEstimate(flops=flops, bytes_accessed=moved, transcendentals=0),
        compiler_params=pltpu.CompilerParams(vmem_limit_bytes=limit << 20),
    )(*args)


def body(queries, keys_values, timesteps, gate_table):
    width = HEADS * DEPTH
    sides = [[SIDES * i + side for i in range(HEADS)] for side in range(SIDES)]
    pairs = [[SIDES * i, SIDES * i + 1] for i in range(HEADS)]
    whole = pl.BlockSpec(memory_space=pltpu.HBM)

    def pack(kernel, stale, fields):
        return call(
            kernel,
            SHAPE((HEADS, fields * TOK, DEPTH), BF16),
            (queries, stale),
            [whole, whole],
            [
                pltpu.VMEM((fields, TOK, width), BF16),
                pltpu.VMEM((fields, HEADS, TOK, DEPTH), BF16),
                pltpu.SemaphoreType.DMA((fields,)),
                pltpu.SemaphoreType.DMA((fields,)),
            ],
            out_space=pltpu.HBM,
            limit=60,
        )

    def to_heads(sent):
        return lax.all_to_all(
            sent, "patch", split_axis=0, concat_axis=0, tiled=True, axis_index_groups=sides
        )

    def over_y(field):
        return lax.all_gather(field, "patch", axis=0, tiled=False, axis_index_groups=pairs)

    def beside():
        near = call(
            local_kernel,
            [SHAPE((NEAR, DEPTH), F32)] * 3,
            (queries, keys_values),
            [
                pl.BlockSpec((None, 1, TOK, width), lambda i: (0, 1, 0, 0)),
                pl.BlockSpec((None, None, 2, TOK, width), lambda i: (0, 1, 0, 0, 0)),
            ],
        )
        gates = jnp.take(gate_table, timesteps, axis=0, mode="clip").reshape(2, HEADS, 2, HALF)
        gate = lax.dynamic_index_in_dim(gates, lax.axis_index("cfg"), 2, keepdims=False)
        return near, jnp.concatenate([gate[0], gate[1]], axis=1)

    def attended(kernel, args):
        return call(
            kernel,
            SHAPE((HEADS, 2 * PAIRS + 1, 2, DEPTH), BF16),
            args,
            scratch=[
                pltpu.VMEM((ROWS, TOKENS), F32),
                pltpu.VMEM((ROWS, TOKENS), BF16),
                pltpu.VMEM((ROWS, DEPTH), F32),
                pltpu.VMEM((ROWS, DEPTH), F32),
            ],
            flops=4 * ROWS * TOKENS * DEPTH,
        )

    def heads_first():
        held = to_heads(pack(pack_own_kernel, keys_values, 4))
        held, rest = lax.optimization_barrier((held, beside()))
        return attended(attend_own_kernel, (held, over_y(held[:, 2 * TOK :, :]))), rest

    def y_first():
        held = to_heads(pack(pack_both_kernel, over_y(keys_values[0, 0]), 6))
        held, rest = lax.optimization_barrier((held, beside()))
        return attended(attend_both_kernel, (held,)), rest

    far, (near, gate) = lax.cond(lax.axis_index("cfg") == Y_FIRST, y_first, heads_first)
    back = to_heads(far)
    attn = call(merge_kernel, SHAPE((2, NEAR, DEPTH), BF16), (back, *near))
    both = lax.all_gather(attn, "cfg", axis=0, tiled=False)
    return call(
        guide_kernel,
        SHAPE((2, TOK, HEADS, HALF), BF16),
        (both, gate),
        scratch=[pltpu.VMEM((NEAR, DEPTH), F32)],
    )


def solution(mesh):
    placed = (
        P("cfg", None, ("clip", "patch"), None),
        P("cfg", None, None, ("clip", "patch"), None),
        P("clip"),
        P(),
    )
    return jax.shard_map(
        body,
        mesh=mesh,
        in_specs=placed,
        out_specs=P(None, ("clip", "patch"), None, "cfg"),
        check_vma=False,
    )
```

```python
import math

import jax
import jax.numpy as jnp
from jax import lax
from jax.experimental import pallas as pl
from jax.experimental.pallas import tpu as pltpu
from jax.sharding import PartitionSpec as P

HEADS = 32
DEPTH = 128
HALF = DEPTH // 2
TOK = 16
SIDES = 2
Y_FIRST = 1
NEAR = HEADS * TOK
ROWS = 2 * NEAR
PAIRS = TOK // 2
SLOTS = DEPTH // TOK
GROUP = 8
TOKENS = SIDES * NEAR
BLOCK = 128
FACTOR = math.log2(math.e) / math.sqrt(DEPTH)
BF16 = jnp.bfloat16
F32 = jnp.float32
SHAPE = jax.ShapeDtypeStruct


def dot_t(a, b):
    return lax.dot_general(a, b, (((1,), (1,)), ((), ())), preferred_element_type=F32)


def pack_kernel(fields, out_ref, held, in_sems, packed, out_sems):
    loads = [
        pltpu.make_async_copy(field, held.at[i], in_sems.at[i]) for i, field in enumerate(fields)
    ]
    for load in loads:
        load.start()
    stores = []
    for i, load in enumerate(loads):
        load.wait()
        for h in range(HEADS):
            packed[i, h] = held[i, :, h * DEPTH : (h + 1) * DEPTH]
        rows = out_ref.at[:, i * TOK : (i + 1) * TOK, :]
        stores.append(pltpu.make_async_copy(packed.at[i], rows, out_sems.at[i]))
        stores[-1].start()
    for store in stores:
        store.wait()


def pack_own_kernel(q_ref, kv_ref, *refs):
    fields = [q_ref.at[0, i] for i in range(2)] + [kv_ref.at[0, 0, i] for i in range(2)]
    pack_kernel(fields, *refs)


def pack_both_kernel(q_ref, stale_ref, out_ref, packed, sems):
    fields = [q_ref.at[i] for i in range(2)]
    fields += [stale_ref.at[side, i] for side in range(SIDES) for i in range(2)]
    stores = []
    for i, field in enumerate(fields):
        for h in range(HEADS):
            packed[i, h] = field[:, h * DEPTH : (h + 1) * DEPTH]
        rows = out_ref.at[:, i * TOK : (i + 1) * TOK, :]
        stores.append(pltpu.make_async_copy(packed.at[i], rows, sems.at[i]))
        stores[-1].start()
    for store in stores:
        store.wait()


def split_value(value):
    high = value.astype(BF16).astype(F32)
    rest = value - high
    mid = rest.astype(BF16).astype(F32)
    return high, mid, rest - mid


def write_stats(top, total):
    rows = top.shape[0]
    n = rows // TOK
    lane = lax.broadcasted_iota(jnp.int32, (rows, DEPTH), 1)
    token = lax.broadcasted_iota(jnp.int32, (rows, DEPTH), 0) % TOK
    slot = jnp.where(lane // SLOTS == token, lane % SLOTS, SLOTS)
    value = jnp.where(slot < 3, top, total)
    high, mid, low = split_value(value)
    piece = jnp.where(slot % 3 == 0, high, jnp.where(slot % 3 == 1, mid, low))
    piece = jnp.where(slot < 6, piece, 0.0).astype(BF16)
    out_row = lax.broadcasted_iota(jnp.int32, (2 * n, rows), 0)
    in_row = lax.broadcasted_iota(jnp.int32, (2 * n, rows), 1)
    gather = jnp.where(out_row == in_row // TOK * 2, 1.0, 0.0).astype(BF16)
    return jnp.dot(gather, piece, preferred_element_type=F32).reshape(n, 2, DEPTH).astype(BF16)


def read_stats(stats):
    n = stats.shape[0]
    out_row = lax.broadcasted_iota(jnp.int32, (n * TOK, 2 * n), 0)
    in_row = lax.broadcasted_iota(jnp.int32, (n * TOK, 2 * n), 1)
    spread = jnp.where(in_row == out_row // TOK * 2, 1.0, 0.0).astype(BF16)
    flat = stats.astype(F32).reshape(2 * n, DEPTH).astype(BF16)
    wide = jnp.dot(spread, flat, preferred_element_type=F32)
    lane = lax.broadcasted_iota(jnp.int32, (n * TOK, DEPTH), 1)
    token = lax.broadcasted_iota(jnp.int32, (n * TOK, DEPTH), 0) % TOK
    wide = jnp.where(lane // SLOTS == token, wide, 0.0).astype(BF16)
    slot = lax.broadcasted_iota(jnp.int32, (DEPTH, 2 * DEPTH), 0) % SLOTS
    part = lax.broadcasted_iota(jnp.int32, (DEPTH, 2 * DEPTH), 1) // DEPTH
    pick = jnp.where(jnp.logical_and(slot < 6, slot // 3 == part), 1.0, 0.0).astype(BF16)
    both = jnp.dot(wide, pick, preferred_element_type=F32)
    return both[:, :DEPTH], both[:, DEPTH:]


def write_rows(rows):
    return rows.reshape(-1, TOK // 2, 2, DEPTH).astype(BF16)


def read_rows(pairs):
    return pairs.astype(F32).reshape(-1, DEPTH)


def local_kernel(q_ref, kv_ref, attn_ref, top_ref, total_ref):
    n = GROUP * TOK
    row = lax.broadcasted_iota(jnp.int32, (n, n), 0)
    col = lax.broadcasted_iota(jnp.int32, (n, n), 1)
    same = row // TOK == col // TOK

    for g in range(HEADS // GROUP):
        heads = range(g * GROUP, (g + 1) * GROUP)
        query, key, value = (
            jnp.concatenate([ref[i, :, h * DEPTH : (h + 1) * DEPTH] for h in heads], 0)
            for ref, i in ((q_ref, 0), (kv_ref, 0), (kv_ref, 1))
        )
        score = jnp.where(same, dot_t(query, key), -jnp.inf)
        top = jnp.max(score, axis=1, keepdims=True)
        weight = jnp.exp2((score - top) * FACTOR)
        total = jnp.sum(weight, axis=1, keepdims=True)
        summed = jnp.dot(weight.astype(BF16), value, preferred_element_type=F32)
        here = slice(g * n, (g + 1) * n)
        attn_ref[here] = summed / total
        top_ref[here] = jnp.broadcast_to(top, (n, DEPTH))
        total_ref[here] = jnp.broadcast_to(total, (n, DEPTH))


def attend_own_kernel(x_ref, kv_ref, *refs):
    attend(x_ref, [kv_ref.at[half] for half in range(SIDES)], *refs)


def attend_both_kernel(x_ref, *refs):
    pair = 2 * TOK
    pairs = [x_ref.at[:, pair * (1 + half) : pair * (2 + half), :] for half in range(SIDES)]
    attend(x_ref, pairs, *refs)


def attend(x_ref, pairs, out_ref, score, weight, top, total):
    side = lax.axis_index("patch") % SIDES
    row = lax.broadcasted_iota(jnp.int32, (BLOCK, BLOCK), 0)
    col = lax.broadcasted_iota(jnp.int32, (BLOCK, BLOCK), 1)
    same = row // TOK == col // TOK
    n = BLOCK // TOK
    steps = [slice(step * NEAR, (step + 1) * NEAR) for step in range(2)]
    for step in range(2):
        query = x_ref[:, step * TOK : (step + 1) * TOK, :].reshape(NEAR, DEPTH)
        for half in range(SIDES):
            keys = pairs[half][:, 0:TOK, :].reshape(NEAR, DEPTH)
            score[steps[step], half * NEAR : (half + 1) * NEAR] = dot_t(query, keys)
    for step in range(2):
        for i in range(NEAR // BLOCK):
            here = slice(step * NEAR + i * BLOCK, step * NEAR + (i + 1) * BLOCK)
            if step == 1:
                for half in range(SIDES):
                    cols = slice(half * NEAR + i * BLOCK, half * NEAR + (i + 1) * BLOCK)
                    own = jnp.logical_and(same, side == half)
                    score[here, cols] = jnp.where(own, -jnp.inf, score[here, cols])
            block = score[here]
            most = jnp.max(block, axis=1, keepdims=True)
            weights = jnp.exp2((block - most) * FACTOR)
            added = jnp.sum(weights, axis=1, keepdims=True)
            top[here] = jnp.broadcast_to(most, (BLOCK, DEPTH))
            total[here] = jnp.broadcast_to(added, (BLOCK, DEPTH))
            weight[here] = weights.astype(BF16)
    values = jnp.concatenate([pair[:, TOK:, :].reshape(NEAR, DEPTH) for pair in pairs], 0)
    for step in range(2):
        rows = steps[step]
        attn = jnp.dot(weight[rows], values, preferred_element_type=F32) / total[rows]
        out_ref[:, step * PAIRS : (step + 1) * PAIRS] = write_rows(attn)
    for i in range(NEAR // BLOCK):
        rows = slice(NEAR + i * BLOCK, NEAR + (i + 1) * BLOCK)
        out_ref[i * n : (i + 1) * n, 2 * PAIRS] = write_stats(top[rows], total[rows])


def merge_kernel(y_ref, near_ref, top_ref, total_ref, out_ref):
    lower = lax.broadcasted_iota(jnp.int32, (NEAR, DEPTH), 1) < HALF
    first = read_rows(y_ref[:, 0:PAIRS])
    far = read_rows(y_ref[:, PAIRS : 2 * PAIRS])
    far_top, far_total = read_stats(y_ref[:, 2 * PAIRS])
    near_top = top_ref[...]
    top = jnp.maximum(far_top, near_top)
    far_share = jnp.exp2((far_top - top) * FACTOR) * far_total
    near_share = jnp.exp2((near_top - top) * FACTOR) * total_ref[...]
    second = (far_share * far + near_share * near_ref[...]) / (far_share + near_share)
    out_ref[0] = jnp.where(lower, first, pltpu.roll(second, HALF, 1)).astype(BF16)
    out_ref[1] = jnp.where(lower, pltpu.roll(first, HALF, 1), second).astype(BF16)


def guide_kernel(both_ref, gate_ref, out_ref, held):
    core = lax.axis_index("cfg")
    cond = both_ref[0, core].astype(F32)
    uncond = both_ref[1, core].astype(F32)
    mixed = (uncond + 5.0 * (cond - uncond)).reshape(HEADS, TOK, DEPTH)
    held[...] = (gate_ref[...].reshape(HEADS, 1, DEPTH) * mixed).reshape(NEAR, DEPTH)
    for t in range(TOK):
        rows = held[pl.ds(t, HEADS, stride=TOK), :]
        out_ref[0, t] = rows[:, :HALF].astype(BF16)
        out_ref[1, t] = rows[:, HALF:].astype(BF16)


def call(kernel, out, args, specs=None, scratch=(), flops=0, out_space=pltpu.VMEM, limit=32):
    many = isinstance(out, list)
    shapes = out if many else [out]
    moved = sum(a.size * a.dtype.itemsize for a in list(args) + list(shapes))
    vmem = pl.BlockSpec(memory_space=pltpu.VMEM)
    result = pl.BlockSpec(memory_space=out_space)
    return pl.pallas_call(
        kernel,
        grid=(1,),
        out_shape=out,
        in_specs=specs or [vmem] * len(args),
        out_specs=[result] * len(shapes) if many else result,
        scratch_shapes=list(scratch),
        cost_estimate=pl.CostEstimate(flops=flops, bytes_accessed=moved, transcendentals=0),
        compiler_params=pltpu.CompilerParams(vmem_limit_bytes=limit << 20),
    )(*args)


def body(queries, keys_values, timesteps, gate_table):
    width = HEADS * DEPTH
    sides = [[SIDES * i + side for i in range(HEADS)] for side in range(SIDES)]
    pairs = [[SIDES * i, SIDES * i + 1] for i in range(HEADS)]
    whole = pl.BlockSpec(memory_space=pltpu.HBM)

    def packed(kernel, stale, specs, fields, scratch, limit):
        return call(
            kernel,
            SHAPE((HEADS, fields * TOK, DEPTH), BF16),
            (queries, stale),
            specs,
            scratch
            + [
                pltpu.VMEM((fields, HEADS, TOK, DEPTH), BF16),
                pltpu.SemaphoreType.DMA((fields,)),
            ],
            out_space=pltpu.HBM,
            limit=limit,
        )

    def pack_own():
        loads = [pltpu.VMEM((4, TOK, width), BF16), pltpu.SemaphoreType.DMA((4,))]
        return packed(pack_own_kernel, keys_values, [whole, whole], 4, loads, 60)

    def pack_both(stale):
        specs = [
            pl.BlockSpec((None, 2, TOK, width), lambda i: (0, 0, 0, 0)),
            pl.BlockSpec(memory_space=pltpu.VMEM),
        ]
        return packed(pack_both_kernel, stale, specs, 6, [], 32)

    def to_heads(sent):
        return lax.all_to_all(
            sent, "patch", split_axis=0, concat_axis=0, tiled=True, axis_index_groups=sides
        )

    def over_y(field):
        return lax.all_gather(field, "patch", axis=0, tiled=False, axis_index_groups=pairs)

    def beside():
        near = call(
            local_kernel,
            [SHAPE((NEAR, DEPTH), F32)] * 3,
            (queries, keys_values),
            [
                pl.BlockSpec((None, 1, TOK, width), lambda i: (0, 1, 0, 0)),
                pl.BlockSpec((None, None, 2, TOK, width), lambda i: (0, 1, 0, 0, 0)),
            ],
        )
        gates = jnp.take(gate_table, timesteps, axis=0, mode="clip").reshape(2, HEADS, 2, HALF)
        gate = lax.dynamic_index_in_dim(gates, lax.axis_index("cfg"), 2, keepdims=False)
        return near, jnp.concatenate([gate[0], gate[1]], axis=1)

    def attended(kernel, args):
        return call(
            kernel,
            SHAPE((HEADS, 2 * PAIRS + 1, 2, DEPTH), BF16),
            args,
            scratch=[
                pltpu.VMEM((ROWS, TOKENS), F32),
                pltpu.VMEM((ROWS, TOKENS), BF16),
                pltpu.VMEM((ROWS, DEPTH), F32),
                pltpu.VMEM((ROWS, DEPTH), F32),
            ],
            flops=4 * ROWS * TOKENS * DEPTH,
        )

    def heads_first():
        held = to_heads(pack_own())
        held, rest = lax.optimization_barrier((held, beside()))
        return attended(attend_own_kernel, (held, over_y(held[:, 2 * TOK :, :]))), rest

    def y_first():
        held = to_heads(pack_both(over_y(keys_values[0, 0])))
        held, rest = lax.optimization_barrier((held, beside()))
        return attended(attend_both_kernel, (held,)), rest

    far, (near, gate) = lax.cond(lax.axis_index("cfg") == Y_FIRST, y_first, heads_first)
    back = to_heads(far)
    attn = call(merge_kernel, SHAPE((2, NEAR, DEPTH), BF16), (back, *near))
    both = lax.all_gather(attn, "cfg", axis=0, tiled=False)
    return call(
        guide_kernel,
        SHAPE((2, TOK, HEADS, HALF), BF16),
        (both, gate),
        scratch=[pltpu.VMEM((NEAR, DEPTH), F32)],
    )


def solution(mesh):
    placed = (
        P("cfg", None, ("clip", "patch"), None),
        P("cfg", None, None, ("clip", "patch"), None),
        P("clip"),
        P(),
    )
    return jax.shard_map(
        body,
        mesh=mesh,
        in_specs=placed,
        out_specs=P(None, ("clip", "patch"), None, "cfg"),
        check_vma=False,
    )
```

```python
import math

import jax
import jax.numpy as jnp
from jax import lax
from jax.experimental import pallas as pl
from jax.experimental.pallas import tpu as pltpu
from jax.sharding import PartitionSpec as P

HEADS = 32
DEPTH = 128
HALF = DEPTH // 2
TOK = 16
SIDES = 2
Y_FIRST = 0
NEAR = HEADS * TOK
ROWS = 2 * NEAR
PAIRS = TOK // 2
SLOTS = DEPTH // TOK
GROUP = 8
TOKENS = SIDES * NEAR
BLOCK = 128
FACTOR = math.log2(math.e) / math.sqrt(DEPTH)
BF16 = jnp.bfloat16
F32 = jnp.float32
SHAPE = jax.ShapeDtypeStruct


def dot_t(a, b):
    return lax.dot_general(a, b, (((1,), (1,)), ((), ())), preferred_element_type=F32)


def pack_kernel(fields, out_ref, held, in_sems, packed, out_sems):
    loads = [
        pltpu.make_async_copy(field, held.at[i], in_sems.at[i]) for i, field in enumerate(fields)
    ]
    for load in loads:
        load.start()
    stores = []
    for i, load in enumerate(loads):
        load.wait()
        for h in range(HEADS):
            packed[i, h] = held[i, :, h * DEPTH : (h + 1) * DEPTH]
        rows = out_ref.at[:, i * TOK : (i + 1) * TOK, :]
        stores.append(pltpu.make_async_copy(packed.at[i], rows, out_sems.at[i]))
        stores[-1].start()
    for store in stores:
        store.wait()


def pack_own_kernel(q_ref, kv_ref, *refs):
    fields = [q_ref.at[0, i] for i in range(2)] + [kv_ref.at[0, 0, i] for i in range(2)]
    pack_kernel(fields, *refs)


def pack_both_kernel(q_ref, stale_ref, out_ref, packed, sems):
    fields = [q_ref.at[i] for i in range(2)]
    fields += [stale_ref.at[side, i] for side in range(SIDES) for i in range(2)]
    stores = []
    for i, field in enumerate(fields):
        for h in range(HEADS):
            packed[i, h] = field[:, h * DEPTH : (h + 1) * DEPTH]
        rows = out_ref.at[:, i * TOK : (i + 1) * TOK, :]
        stores.append(pltpu.make_async_copy(packed.at[i], rows, sems.at[i]))
        stores[-1].start()
    for store in stores:
        store.wait()


def split_value(value):
    high = value.astype(BF16).astype(F32)
    rest = value - high
    mid = rest.astype(BF16).astype(F32)
    return high, mid, rest - mid


def write_stats(top, total):
    rows = top.shape[0]
    n = rows // TOK
    lane = lax.broadcasted_iota(jnp.int32, (rows, DEPTH), 1)
    token = lax.broadcasted_iota(jnp.int32, (rows, DEPTH), 0) % TOK
    slot = jnp.where(lane // SLOTS == token, lane % SLOTS, SLOTS)
    value = jnp.where(slot < 3, top, total)
    high, mid, low = split_value(value)
    piece = jnp.where(slot % 3 == 0, high, jnp.where(slot % 3 == 1, mid, low))
    piece = jnp.where(slot < 6, piece, 0.0).astype(BF16)
    out_row = lax.broadcasted_iota(jnp.int32, (2 * n, rows), 0)
    in_row = lax.broadcasted_iota(jnp.int32, (2 * n, rows), 1)
    gather = jnp.where(out_row == in_row // TOK * 2, 1.0, 0.0).astype(BF16)
    return jnp.dot(gather, piece, preferred_element_type=F32).reshape(n, 2, DEPTH).astype(BF16)


def read_stats(stats):
    n = stats.shape[0]
    out_row = lax.broadcasted_iota(jnp.int32, (n * TOK, 2 * n), 0)
    in_row = lax.broadcasted_iota(jnp.int32, (n * TOK, 2 * n), 1)
    spread = jnp.where(in_row == out_row // TOK * 2, 1.0, 0.0).astype(BF16)
    flat = stats.astype(F32).reshape(2 * n, DEPTH).astype(BF16)
    wide = jnp.dot(spread, flat, preferred_element_type=F32)
    lane = lax.broadcasted_iota(jnp.int32, (n * TOK, DEPTH), 1)
    token = lax.broadcasted_iota(jnp.int32, (n * TOK, DEPTH), 0) % TOK
    wide = jnp.where(lane // SLOTS == token, wide, 0.0).astype(BF16)
    slot = lax.broadcasted_iota(jnp.int32, (DEPTH, 2 * DEPTH), 0) % SLOTS
    part = lax.broadcasted_iota(jnp.int32, (DEPTH, 2 * DEPTH), 1) // DEPTH
    pick = jnp.where(jnp.logical_and(slot < 6, slot // 3 == part), 1.0, 0.0).astype(BF16)
    both = jnp.dot(wide, pick, preferred_element_type=F32)
    return both[:, :DEPTH], both[:, DEPTH:]


def write_rows(rows):
    return rows.reshape(-1, TOK // 2, 2, DEPTH).astype(BF16)


def read_rows(pairs):
    return pairs.astype(F32).reshape(-1, DEPTH)


def local_kernel(q_ref, kv_ref, attn_ref, top_ref, total_ref):
    n = GROUP * TOK
    row = lax.broadcasted_iota(jnp.int32, (n, n), 0)
    col = lax.broadcasted_iota(jnp.int32, (n, n), 1)
    same = row // TOK == col // TOK

    for g in range(HEADS // GROUP):
        heads = range(g * GROUP, (g + 1) * GROUP)
        query, key, value = (
            jnp.concatenate([ref[i, :, h * DEPTH : (h + 1) * DEPTH] for h in heads], 0)
            for ref, i in ((q_ref, 0), (kv_ref, 0), (kv_ref, 1))
        )
        score = jnp.where(same, dot_t(query, key), -jnp.inf)
        top = jnp.max(score, axis=1, keepdims=True)
        weight = jnp.exp2((score - top) * FACTOR)
        total = jnp.sum(weight, axis=1, keepdims=True)
        summed = jnp.dot(weight.astype(BF16), value, preferred_element_type=F32)
        here = slice(g * n, (g + 1) * n)
        attn_ref[here] = summed / total
        top_ref[here] = jnp.broadcast_to(top, (n, DEPTH))
        total_ref[here] = jnp.broadcast_to(total, (n, DEPTH))


def attend_own_kernel(x_ref, kv_ref, *refs):
    attend(x_ref, [kv_ref.at[half] for half in range(SIDES)], *refs)


def attend_both_kernel(x_ref, *refs):
    pair = 2 * TOK
    pairs = [x_ref.at[:, pair * (1 + half) : pair * (2 + half), :] for half in range(SIDES)]
    attend(x_ref, pairs, *refs)


def attend(x_ref, pairs, out_ref, score, weight, top, total):
    side = lax.axis_index("patch") % SIDES
    row = lax.broadcasted_iota(jnp.int32, (BLOCK, BLOCK), 0)
    col = lax.broadcasted_iota(jnp.int32, (BLOCK, BLOCK), 1)
    same = row // TOK == col // TOK
    n = BLOCK // TOK
    steps = [slice(step * NEAR, (step + 1) * NEAR) for step in range(2)]
    for step in range(2):
        query = x_ref[:, step * TOK : (step + 1) * TOK, :].reshape(NEAR, DEPTH)
        for half in range(SIDES):
            keys = pairs[half][:, 0:TOK, :].reshape(NEAR, DEPTH)
            score[steps[step], half * NEAR : (half + 1) * NEAR] = dot_t(query, keys)
    for step in range(2):
        for i in range(NEAR // BLOCK):
            here = slice(step * NEAR + i * BLOCK, step * NEAR + (i + 1) * BLOCK)
            if step == 1:
                for half in range(SIDES):
                    cols = slice(half * NEAR + i * BLOCK, half * NEAR + (i + 1) * BLOCK)
                    own = jnp.logical_and(same, side == half)
                    score[here, cols] = jnp.where(own, -jnp.inf, score[here, cols])
            block = score[here]
            most = jnp.max(block, axis=1, keepdims=True)
            weights = jnp.exp2((block - most) * FACTOR)
            added = jnp.sum(weights, axis=1, keepdims=True)
            top[here] = jnp.broadcast_to(most, (BLOCK, DEPTH))
            total[here] = jnp.broadcast_to(added, (BLOCK, DEPTH))
            weight[here] = weights.astype(BF16)
    values = jnp.concatenate([pair[:, TOK:, :].reshape(NEAR, DEPTH) for pair in pairs], 0)
    for step in range(2):
        rows = steps[step]
        attn = jnp.dot(weight[rows], values, preferred_element_type=F32) / total[rows]
        out_ref[:, step * PAIRS : (step + 1) * PAIRS] = write_rows(attn)
    for i in range(NEAR // BLOCK):
        rows = slice(NEAR + i * BLOCK, NEAR + (i + 1) * BLOCK)
        out_ref[i * n : (i + 1) * n, 2 * PAIRS] = write_stats(top[rows], total[rows])


def merge_kernel(y_ref, near_ref, top_ref, total_ref, out_ref):
    lower = lax.broadcasted_iota(jnp.int32, (NEAR, DEPTH), 1) < HALF
    first = read_rows(y_ref[:, 0:PAIRS])
    far = read_rows(y_ref[:, PAIRS : 2 * PAIRS])
    far_top, far_total = read_stats(y_ref[:, 2 * PAIRS])
    near_top = top_ref[...]
    top = jnp.maximum(far_top, near_top)
    far_share = jnp.exp2((far_top - top) * FACTOR) * far_total
    near_share = jnp.exp2((near_top - top) * FACTOR) * total_ref[...]
    second = (far_share * far + near_share * near_ref[...]) / (far_share + near_share)
    out_ref[0] = jnp.where(lower, first, pltpu.roll(second, HALF, 1)).astype(BF16)
    out_ref[1] = jnp.where(lower, pltpu.roll(first, HALF, 1), second).astype(BF16)


def guide_kernel(both_ref, gate_ref, out_ref, held):
    core = lax.axis_index("cfg")
    cond = both_ref[0, core].astype(F32)
    uncond = both_ref[1, core].astype(F32)
    mixed = (uncond + 5.0 * (cond - uncond)).reshape(HEADS, TOK, DEPTH)
    held[...] = (gate_ref[...].reshape(HEADS, 1, DEPTH) * mixed).reshape(NEAR, DEPTH)
    for t in range(TOK):
        rows = held[pl.ds(t, HEADS, stride=TOK), :]
        out_ref[0, t] = rows[:, :HALF].astype(BF16)
        out_ref[1, t] = rows[:, HALF:].astype(BF16)


def call(kernel, out, args, specs=None, scratch=(), flops=0, out_space=pltpu.VMEM, limit=32):
    many = isinstance(out, list)
    shapes = out if many else [out]
    moved = sum(a.size * a.dtype.itemsize for a in list(args) + list(shapes))
    vmem = pl.BlockSpec(memory_space=pltpu.VMEM)
    result = pl.BlockSpec(memory_space=out_space)
    return pl.pallas_call(
        kernel,
        grid=(1,),
        out_shape=out,
        in_specs=specs or [vmem] * len(args),
        out_specs=[result] * len(shapes) if many else result,
        scratch_shapes=list(scratch),
        cost_estimate=pl.CostEstimate(flops=flops, bytes_accessed=moved, transcendentals=0),
        compiler_params=pltpu.CompilerParams(vmem_limit_bytes=limit << 20),
    )(*args)


def body(queries, keys_values, timesteps, gate_table):
    width = HEADS * DEPTH
    sides = [[SIDES * i + side for i in range(HEADS)] for side in range(SIDES)]
    pairs = [[SIDES * i, SIDES * i + 1] for i in range(HEADS)]
    whole = pl.BlockSpec(memory_space=pltpu.HBM)

    def packed(kernel, stale, specs, fields, scratch, limit):
        return call(
            kernel,
            SHAPE((HEADS, fields * TOK, DEPTH), BF16),
            (queries, stale),
            specs,
            scratch
            + [
                pltpu.VMEM((fields, HEADS, TOK, DEPTH), BF16),
                pltpu.SemaphoreType.DMA((fields,)),
            ],
            out_space=pltpu.HBM,
            limit=limit,
        )

    def pack_own():
        loads = [pltpu.VMEM((4, TOK, width), BF16), pltpu.SemaphoreType.DMA((4,))]
        return packed(pack_own_kernel, keys_values, [whole, whole], 4, loads, 60)

    def pack_both(stale):
        specs = [
            pl.BlockSpec((None, 2, TOK, width), lambda i: (0, 0, 0, 0)),
            pl.BlockSpec(memory_space=pltpu.VMEM),
        ]
        return packed(pack_both_kernel, stale, specs, 6, [], 32)

    def to_heads(sent):
        return lax.all_to_all(
            sent, "patch", split_axis=0, concat_axis=0, tiled=True, axis_index_groups=sides
        )

    def over_y(field):
        return lax.all_gather(field, "patch", axis=0, tiled=False, axis_index_groups=pairs)

    def beside():
        near = call(
            local_kernel,
            [SHAPE((NEAR, DEPTH), F32)] * 3,
            (queries, keys_values),
            [
                pl.BlockSpec((None, 1, TOK, width), lambda i: (0, 1, 0, 0)),
                pl.BlockSpec((None, None, 2, TOK, width), lambda i: (0, 1, 0, 0, 0)),
            ],
        )
        gates = jnp.take(gate_table, timesteps, axis=0, mode="clip").reshape(2, HEADS, 2, HALF)
        gate = lax.dynamic_index_in_dim(gates, lax.axis_index("cfg"), 2, keepdims=False)
        return near, jnp.concatenate([gate[0], gate[1]], axis=1)

    def attended(kernel, args):
        return call(
            kernel,
            SHAPE((HEADS, 2 * PAIRS + 1, 2, DEPTH), BF16),
            args,
            scratch=[
                pltpu.VMEM((ROWS, TOKENS), F32),
                pltpu.VMEM((ROWS, TOKENS), BF16),
                pltpu.VMEM((ROWS, DEPTH), F32),
                pltpu.VMEM((ROWS, DEPTH), F32),
            ],
            flops=4 * ROWS * TOKENS * DEPTH,
        )

    def heads_first():
        held = to_heads(pack_own())
        held, rest = lax.optimization_barrier((held, beside()))
        return attended(attend_own_kernel, (held, over_y(held[:, 2 * TOK :, :]))), rest

    def y_first():
        held = to_heads(pack_both(over_y(keys_values[0, 0])))
        held, rest = lax.optimization_barrier((held, beside()))
        return attended(attend_both_kernel, (held,)), rest

    far, (near, gate) = lax.cond(lax.axis_index("cfg") == Y_FIRST, y_first, heads_first)
    back = to_heads(far)
    attn = call(merge_kernel, SHAPE((2, NEAR, DEPTH), BF16), (back, *near))
    both = lax.all_gather(attn, "cfg", axis=0, tiled=False)
    return call(
        guide_kernel,
        SHAPE((2, TOK, HEADS, HALF), BF16),
        (both, gate),
        scratch=[pltpu.VMEM((NEAR, DEPTH), F32)],
    )


def solution(mesh):
    placed = (
        P("cfg", None, ("clip", "patch"), None),
        P("cfg", None, None, ("clip", "patch"), None),
        P("clip"),
        P(),
    )
    return jax.shard_map(
        body,
        mesh=mesh,
        in_specs=placed,
        out_specs=P(None, ("clip", "patch"), None, "cfg"),
        check_vma=False,
    )
```

```python
import math

import jax
import jax.numpy as jnp
from jax import lax
from jax.experimental import pallas as pl
from jax.experimental.pallas import tpu as pltpu
from jax.sharding import PartitionSpec as P

HEADS = 32
DEPTH = 128
HALF = DEPTH // 2
TOK = 16
SIDES = 2
Y_FIRST = 1
NEAR = HEADS * TOK
ROWS = 2 * NEAR
PAIRS = TOK // 2
SLOTS = DEPTH // TOK
GROUP = 8
TOKENS = SIDES * NEAR
BLOCK = 128
FACTOR = math.log2(math.e) / math.sqrt(DEPTH)
BF16 = jnp.bfloat16
F32 = jnp.float32
SHAPE = jax.ShapeDtypeStruct


def dot_t(a, b):
    return lax.dot_general(a, b, (((1,), (1,)), ((), ())), preferred_element_type=F32)


def pack_kernel(fields, out_ref, packed, sems):
    stores = []
    for i, field in enumerate(fields):
        for h in range(HEADS):
            packed[i, h] = field[:, h * DEPTH : (h + 1) * DEPTH]
        rows = out_ref.at[:, i * TOK : (i + 1) * TOK, :]
        stores.append(pltpu.make_async_copy(packed.at[i], rows, sems.at[i]))
        stores[-1].start()
    for store in stores:
        store.wait()


def pack_own_kernel(q_ref, kv_ref, *refs):
    pack_kernel([ref.at[i] for ref in (q_ref, kv_ref) for i in range(2)], *refs)


def pack_both_kernel(q_ref, stale_ref, *refs):
    fields = [q_ref.at[i] for i in range(2)]
    fields += [stale_ref.at[side, i] for side in range(SIDES) for i in range(2)]
    pack_kernel(fields, *refs)


def split_value(value):
    high = value.astype(BF16).astype(F32)
    rest = value - high
    mid = rest.astype(BF16).astype(F32)
    return high, mid, rest - mid


def write_stats(top, total):
    rows = top.shape[0]
    n = rows // TOK
    lane = lax.broadcasted_iota(jnp.int32, (rows, DEPTH), 1)
    token = lax.broadcasted_iota(jnp.int32, (rows, DEPTH), 0) % TOK
    slot = jnp.where(lane // SLOTS == token, lane % SLOTS, SLOTS)
    value = jnp.where(slot < 3, top, total)
    high, mid, low = split_value(value)
    piece = jnp.where(slot % 3 == 0, high, jnp.where(slot % 3 == 1, mid, low))
    piece = jnp.where(slot < 6, piece, 0.0).astype(BF16)
    out_row = lax.broadcasted_iota(jnp.int32, (2 * n, rows), 0)
    in_row = lax.broadcasted_iota(jnp.int32, (2 * n, rows), 1)
    gather = jnp.where(out_row == in_row // TOK * 2, 1.0, 0.0).astype(BF16)
    return jnp.dot(gather, piece, preferred_element_type=F32).reshape(n, 2, DEPTH).astype(BF16)


def read_stats(stats):
    n = stats.shape[0]
    out_row = lax.broadcasted_iota(jnp.int32, (n * TOK, 2 * n), 0)
    in_row = lax.broadcasted_iota(jnp.int32, (n * TOK, 2 * n), 1)
    spread = jnp.where(in_row == out_row // TOK * 2, 1.0, 0.0).astype(BF16)
    flat = stats.astype(F32).reshape(2 * n, DEPTH).astype(BF16)
    wide = jnp.dot(spread, flat, preferred_element_type=F32)
    lane = lax.broadcasted_iota(jnp.int32, (n * TOK, DEPTH), 1)
    token = lax.broadcasted_iota(jnp.int32, (n * TOK, DEPTH), 0) % TOK
    wide = jnp.where(lane // SLOTS == token, wide, 0.0).astype(BF16)
    slot = lax.broadcasted_iota(jnp.int32, (DEPTH, 2 * DEPTH), 0) % SLOTS
    part = lax.broadcasted_iota(jnp.int32, (DEPTH, 2 * DEPTH), 1) // DEPTH
    pick = jnp.where(jnp.logical_and(slot < 6, slot // 3 == part), 1.0, 0.0).astype(BF16)
    both = jnp.dot(wide, pick, preferred_element_type=F32)
    return both[:, :DEPTH], both[:, DEPTH:]


def write_rows(rows):
    return rows.reshape(-1, TOK // 2, 2, DEPTH).astype(BF16)


def read_rows(pairs):
    return pairs.astype(F32).reshape(-1, DEPTH)


def local_kernel(q_ref, kv_ref, attn_ref, top_ref, total_ref):
    n = GROUP * TOK
    row = lax.broadcasted_iota(jnp.int32, (n, n), 0)
    col = lax.broadcasted_iota(jnp.int32, (n, n), 1)
    same = row // TOK == col // TOK

    for g in range(HEADS // GROUP):
        heads = range(g * GROUP, (g + 1) * GROUP)
        query, key, value = (
            jnp.concatenate([ref[i, :, h * DEPTH : (h + 1) * DEPTH] for h in heads], 0)
            for ref, i in ((q_ref, 0), (kv_ref, 0), (kv_ref, 1))
        )
        score = jnp.where(same, dot_t(query, key), -jnp.inf)
        top = jnp.max(score, axis=1, keepdims=True)
        weight = jnp.exp2((score - top) * FACTOR)
        total = jnp.sum(weight, axis=1, keepdims=True)
        summed = jnp.dot(weight.astype(BF16), value, preferred_element_type=F32)
        here = slice(g * n, (g + 1) * n)
        attn_ref[here] = summed / total
        top_ref[here] = jnp.broadcast_to(top, (n, DEPTH))
        total_ref[here] = jnp.broadcast_to(total, (n, DEPTH))


def attend_own_kernel(x_ref, kv_ref, *refs):
    attend(x_ref, [kv_ref.at[half] for half in range(SIDES)], *refs)


def attend_both_kernel(x_ref, *refs):
    pair = 2 * TOK
    pairs = [x_ref.at[:, pair * (1 + half) : pair * (2 + half), :] for half in range(SIDES)]
    attend(x_ref, pairs, *refs)


def attend(x_ref, pairs, out_ref, score, weight, top, total):
    side = lax.axis_index("patch") % SIDES
    row = lax.broadcasted_iota(jnp.int32, (BLOCK, BLOCK), 0)
    col = lax.broadcasted_iota(jnp.int32, (BLOCK, BLOCK), 1)
    same = row // TOK == col // TOK
    n = BLOCK // TOK
    steps = [slice(step * NEAR, (step + 1) * NEAR) for step in range(2)]
    for step in range(2):
        query = x_ref[:, step * TOK : (step + 1) * TOK, :].reshape(NEAR, DEPTH)
        for half in range(SIDES):
            keys = pairs[half][:, 0:TOK, :].reshape(NEAR, DEPTH)
            score[steps[step], half * NEAR : (half + 1) * NEAR] = dot_t(query, keys)
    for step in range(2):
        for i in range(NEAR // BLOCK):
            here = slice(step * NEAR + i * BLOCK, step * NEAR + (i + 1) * BLOCK)
            if step == 1:
                for half in range(SIDES):
                    cols = slice(half * NEAR + i * BLOCK, half * NEAR + (i + 1) * BLOCK)
                    own = jnp.logical_and(same, side == half)
                    score[here, cols] = jnp.where(own, -jnp.inf, score[here, cols])
            block = score[here]
            most = jnp.max(block, axis=1, keepdims=True)
            weights = jnp.exp2((block - most) * FACTOR)
            added = jnp.sum(weights, axis=1, keepdims=True)
            top[here] = jnp.broadcast_to(most, (BLOCK, DEPTH))
            total[here] = jnp.broadcast_to(added, (BLOCK, DEPTH))
            weight[here] = weights.astype(BF16)
    values = jnp.concatenate([pair[:, TOK:, :].reshape(NEAR, DEPTH) for pair in pairs], 0)
    for step in range(2):
        rows = steps[step]
        attn = jnp.dot(weight[rows], values, preferred_element_type=F32) / total[rows]
        out_ref[:, step * PAIRS : (step + 1) * PAIRS] = write_rows(attn)
    for i in range(NEAR // BLOCK):
        rows = slice(NEAR + i * BLOCK, NEAR + (i + 1) * BLOCK)
        out_ref[i * n : (i + 1) * n, 2 * PAIRS] = write_stats(top[rows], total[rows])


def merge_kernel(y_ref, near_ref, top_ref, total_ref, out_ref):
    lower = lax.broadcasted_iota(jnp.int32, (NEAR, DEPTH), 1) < HALF
    first = read_rows(y_ref[:, 0:PAIRS])
    far = read_rows(y_ref[:, PAIRS : 2 * PAIRS])
    far_top, far_total = read_stats(y_ref[:, 2 * PAIRS])
    near_top = top_ref[...]
    top = jnp.maximum(far_top, near_top)
    far_share = jnp.exp2((far_top - top) * FACTOR) * far_total
    near_share = jnp.exp2((near_top - top) * FACTOR) * total_ref[...]
    second = (far_share * far + near_share * near_ref[...]) / (far_share + near_share)
    out_ref[0] = jnp.where(lower, first, pltpu.roll(second, HALF, 1)).astype(BF16)
    out_ref[1] = jnp.where(lower, pltpu.roll(first, HALF, 1), second).astype(BF16)


def guide_kernel(plan_ref, both_ref, table_ref, out_ref, held, gate):
    core = lax.axis_index("cfg")
    upper = core == 1
    lower = lax.broadcasted_iota(jnp.int32, (1, DEPTH), 1) < HALF
    first, second = (table_ref[pl.ds(plan_ref[step], 1), :] for step in range(2))
    for h in range(HEADS):
        lanes = slice(h * DEPTH, (h + 1) * DEPTH)
        turned = pltpu.roll(jnp.where(upper, first[:, lanes], second[:, lanes]), HALF, 1)
        gate[h : h + 1] = jnp.where(
            lower,
            jnp.where(upper, turned, first[:, lanes]),
            jnp.where(upper, second[:, lanes], turned),
        )
    cond = both_ref[0, core].astype(F32)
    uncond = both_ref[1, core].astype(F32)
    mixed = (uncond + 5.0 * (cond - uncond)).reshape(HEADS, TOK, DEPTH)
    held[...] = (gate[...].reshape(HEADS, 1, DEPTH) * mixed).reshape(NEAR, DEPTH)
    for t in range(TOK):
        rows = held[pl.ds(t, HEADS, stride=TOK), :]
        out_ref[0, t] = rows[:, :HALF].astype(BF16)
        out_ref[1, t] = rows[:, HALF:].astype(BF16)


def call(kernel, out, args, specs=None, scratch=(), flops=0, out_space=pltpu.VMEM, limit=32):
    many = isinstance(out, list)
    shapes = out if many else [out]
    moved = sum(a.size * a.dtype.itemsize for a in list(args) + list(shapes))
    vmem = pl.BlockSpec(memory_space=pltpu.VMEM)
    result = pl.BlockSpec(memory_space=out_space)
    return pl.pallas_call(
        kernel,
        grid=(1,),
        out_shape=out,
        in_specs=specs or [vmem] * len(args),
        out_specs=[result] * len(shapes) if many else result,
        scratch_shapes=list(scratch),
        cost_estimate=pl.CostEstimate(flops=flops, bytes_accessed=moved, transcendentals=0),
        compiler_params=pltpu.CompilerParams(vmem_limit_bytes=limit << 20),
    )(*args)


def body(queries, keys_values, timesteps, gate_table):
    width = HEADS * DEPTH
    sides = [[SIDES * i + side for i in range(HEADS)] for side in range(SIDES)]
    pairs = [[SIDES * i, SIDES * i + 1] for i in range(HEADS)]

    first_pairs = keys_values[0, 0]

    def packed(kernel, pairs, fields):
        return call(
            kernel,
            SHAPE((HEADS, fields * TOK, DEPTH), BF16),
            (queries, pairs),
            [
                pl.BlockSpec((None, 2, TOK, width), lambda i: (0, 0, 0, 0)),
                pl.BlockSpec(memory_space=pltpu.VMEM),
            ],
            [
                pltpu.VMEM((fields, HEADS, TOK, DEPTH), BF16),
                pltpu.SemaphoreType.DMA((fields,)),
            ],
            out_space=pltpu.HBM,
        )

    def to_heads(sent):
        return lax.all_to_all(
            sent, "patch", split_axis=0, concat_axis=0, tiled=True, axis_index_groups=sides
        )

    def over_y(field):
        return lax.all_gather(field, "patch", axis=0, tiled=False, axis_index_groups=pairs)

    def own_patch():
        return call(
            local_kernel,
            [SHAPE((NEAR, DEPTH), F32)] * 3,
            (queries, keys_values),
            [
                pl.BlockSpec((None, 1, TOK, width), lambda i: (0, 1, 0, 0)),
                pl.BlockSpec((None, None, 2, TOK, width), lambda i: (0, 1, 0, 0, 0)),
            ],
        )

    def attended(kernel, args):
        return call(
            kernel,
            SHAPE((HEADS, 2 * PAIRS + 1, 2, DEPTH), BF16),
            args,
            scratch=[
                pltpu.VMEM((ROWS, TOKENS), F32),
                pltpu.VMEM((ROWS, TOKENS), BF16),
                pltpu.VMEM((ROWS, DEPTH), F32),
                pltpu.VMEM((ROWS, DEPTH), F32),
            ],
            flops=4 * ROWS * TOKENS * DEPTH,
        )

    def heads_first():
        held = to_heads(packed(pack_own_kernel, first_pairs, 4))
        held, near = lax.optimization_barrier((held, own_patch()))
        return attended(attend_own_kernel, (held, over_y(held[:, 2 * TOK :, :]))), near

    def y_first():
        held = to_heads(packed(pack_both_kernel, over_y(first_pairs), 6))
        held, near = lax.optimization_barrier((held, own_patch()))
        return attended(attend_both_kernel, (held,)), near

    far, near = lax.cond(lax.axis_index("cfg") == Y_FIRST, y_first, heads_first)
    back = to_heads(far)
    attn = call(merge_kernel, SHAPE((2, NEAR, DEPTH), BF16), (back, *near))
    both = lax.all_gather(attn, "cfg", axis=0, tiled=False)
    vmem = pl.BlockSpec(memory_space=pltpu.VMEM)
    return call(
        guide_kernel,
        SHAPE((2, TOK, HEADS, HALF), BF16),
        (timesteps, both, gate_table),
        [pl.BlockSpec(memory_space=pltpu.SMEM), vmem, vmem],
        scratch=[pltpu.VMEM((NEAR, DEPTH), F32), pltpu.VMEM((HEADS, DEPTH), F32)],
    )


def solution(mesh):
    placed = (
        P("cfg", None, ("clip", "patch"), None),
        P("cfg", None, None, ("clip", "patch"), None),
        P("clip"),
        P(),
    )
    return jax.shard_map(
        body,
        mesh=mesh,
        in_specs=placed,
        out_specs=P(None, ("clip", "patch"), None, "cfg"),
        check_vma=False,
    )
```

```python
import math

import jax
import jax.numpy as jnp
from jax import lax
from jax.experimental import pallas as pl
from jax.experimental.pallas import tpu as pltpu
from jax.sharding import PartitionSpec as P

HEADS = 32
DEPTH = 128
HALF = DEPTH // 2
TOK = 16
SIDES = 2
Y_FIRST = 1
NEAR = HEADS * TOK
ROWS = 2 * NEAR
PAIRS = TOK // 2
SLOTS = DEPTH // TOK
GROUP = 8
TOKENS = SIDES * NEAR
BLOCK = 128
FACTOR = math.log2(math.e) / math.sqrt(DEPTH)
BF16 = jnp.bfloat16
F32 = jnp.float32
SHAPE = jax.ShapeDtypeStruct


def dot_t(a, b):
    return lax.dot_general(a, b, (((1,), (1,)), ((), ())), preferred_element_type=F32)


def pack_kernel(fields, out_ref, packed, sems):
    stores = []
    for i, field in enumerate(fields):
        for h in range(HEADS):
            packed[i, h] = field[:, h * DEPTH : (h + 1) * DEPTH]
        rows = out_ref.at[:, i * TOK : (i + 1) * TOK, :]
        stores.append(pltpu.make_async_copy(packed.at[i], rows, sems.at[i]))
        stores[-1].start()
    for store in stores:
        store.wait()


def pack_own_kernel(q_ref, kv_ref, *refs):
    pack_kernel([ref.at[i] for ref in (q_ref, kv_ref) for i in range(2)], *refs)


def pack_both_kernel(q_ref, stale_ref, *refs):
    fields = [q_ref.at[i] for i in range(2)]
    fields += [stale_ref.at[side, i] for side in range(SIDES) for i in range(2)]
    pack_kernel(fields, *refs)


def split_value(value):
    high = value.astype(BF16).astype(F32)
    rest = value - high
    mid = rest.astype(BF16).astype(F32)
    return high, mid, rest - mid


def write_stats(top, total):
    rows = top.shape[0]
    n = rows // TOK
    lane = lax.broadcasted_iota(jnp.int32, (rows, DEPTH), 1)
    token = lax.broadcasted_iota(jnp.int32, (rows, DEPTH), 0) % TOK
    slot = jnp.where(lane // SLOTS == token, lane % SLOTS, SLOTS)
    value = jnp.where(slot < 3, top, total)
    high, mid, low = split_value(value)
    piece = jnp.where(slot % 3 == 0, high, jnp.where(slot % 3 == 1, mid, low))
    piece = jnp.where(slot < 6, piece, 0.0).astype(BF16)
    out_row = lax.broadcasted_iota(jnp.int32, (2 * n, rows), 0)
    in_row = lax.broadcasted_iota(jnp.int32, (2 * n, rows), 1)
    gather = jnp.where(out_row == in_row // TOK * 2, 1.0, 0.0).astype(BF16)
    return jnp.dot(gather, piece, preferred_element_type=F32).reshape(n, 2, DEPTH).astype(BF16)


def read_stats(stats):
    n = stats.shape[0]
    out_row = lax.broadcasted_iota(jnp.int32, (n * TOK, 2 * n), 0)
    in_row = lax.broadcasted_iota(jnp.int32, (n * TOK, 2 * n), 1)
    spread = jnp.where(in_row == out_row // TOK * 2, 1.0, 0.0).astype(BF16)
    flat = stats.astype(F32).reshape(2 * n, DEPTH).astype(BF16)
    wide = jnp.dot(spread, flat, preferred_element_type=F32)
    lane = lax.broadcasted_iota(jnp.int32, (n * TOK, DEPTH), 1)
    token = lax.broadcasted_iota(jnp.int32, (n * TOK, DEPTH), 0) % TOK
    wide = jnp.where(lane // SLOTS == token, wide, 0.0).astype(BF16)
    slot = lax.broadcasted_iota(jnp.int32, (DEPTH, 2 * DEPTH), 0) % SLOTS
    part = lax.broadcasted_iota(jnp.int32, (DEPTH, 2 * DEPTH), 1) // DEPTH
    pick = jnp.where(jnp.logical_and(slot < 6, slot // 3 == part), 1.0, 0.0).astype(BF16)
    both = jnp.dot(wide, pick, preferred_element_type=F32)
    return both[:, :DEPTH], both[:, DEPTH:]


def write_rows(rows):
    return rows.reshape(-1, TOK // 2, 2, DEPTH).astype(BF16)


def read_rows(pairs):
    return pairs.astype(F32).reshape(-1, DEPTH)


def local_kernel(q_ref, kv_ref, attn_ref, top_ref, total_ref):
    n = GROUP * TOK
    row = lax.broadcasted_iota(jnp.int32, (n, n), 0)
    col = lax.broadcasted_iota(jnp.int32, (n, n), 1)
    same = row // TOK == col // TOK

    for g in range(HEADS // GROUP):
        heads = range(g * GROUP, (g + 1) * GROUP)
        query, key, value = (
            jnp.concatenate([ref[i, :, h * DEPTH : (h + 1) * DEPTH] for h in heads], 0)
            for ref, i in ((q_ref, 0), (kv_ref, 0), (kv_ref, 1))
        )
        score = jnp.where(same, dot_t(query, key), -jnp.inf)
        top = jnp.max(score, axis=1, keepdims=True)
        weight = jnp.exp2((score - top) * FACTOR)
        total = jnp.sum(weight, axis=1, keepdims=True)
        summed = jnp.dot(weight.astype(BF16), value, preferred_element_type=F32)
        here = slice(g * n, (g + 1) * n)
        attn_ref[here] = summed / total
        top_ref[here] = jnp.broadcast_to(top, (n, DEPTH))
        total_ref[here] = jnp.broadcast_to(total, (n, DEPTH))


def attend_own_kernel(x_ref, kv_ref, *refs):
    attend(x_ref, [kv_ref.at[half] for half in range(SIDES)], *refs)


def attend_both_kernel(x_ref, *refs):
    pair = 2 * TOK
    pairs = [x_ref.at[:, pair * (1 + half) : pair * (2 + half), :] for half in range(SIDES)]
    attend(x_ref, pairs, *refs)


def attend(x_ref, pairs, out_ref, score, weight, top, total):
    side = lax.axis_index("patch") % SIDES
    row = lax.broadcasted_iota(jnp.int32, (BLOCK, BLOCK), 0)
    col = lax.broadcasted_iota(jnp.int32, (BLOCK, BLOCK), 1)
    same = row // TOK == col // TOK
    n = BLOCK // TOK
    steps = [slice(step * NEAR, (step + 1) * NEAR) for step in range(2)]
    for step in range(2):
        query = x_ref[:, step * TOK : (step + 1) * TOK, :].reshape(NEAR, DEPTH)
        for half in range(SIDES):
            keys = pairs[half][:, 0:TOK, :].reshape(NEAR, DEPTH)
            score[steps[step], half * NEAR : (half + 1) * NEAR] = dot_t(query, keys)
    for step in range(2):
        for i in range(NEAR // BLOCK):
            here = slice(step * NEAR + i * BLOCK, step * NEAR + (i + 1) * BLOCK)
            if step == 1:
                for half in range(SIDES):
                    cols = slice(half * NEAR + i * BLOCK, half * NEAR + (i + 1) * BLOCK)
                    own = jnp.logical_and(same, side == half)
                    score[here, cols] = jnp.where(own, -jnp.inf, score[here, cols])
            block = score[here]
            most = jnp.max(block, axis=1, keepdims=True)
            weights = jnp.exp2((block - most) * FACTOR)
            added = jnp.sum(weights, axis=1, keepdims=True)
            top[here] = jnp.broadcast_to(most, (BLOCK, DEPTH))
            total[here] = jnp.broadcast_to(added, (BLOCK, DEPTH))
            weight[here] = weights.astype(BF16)
    values = jnp.concatenate([pair[:, TOK:, :].reshape(NEAR, DEPTH) for pair in pairs], 0)
    for step in range(2):
        rows = steps[step]
        attn = jnp.dot(weight[rows], values, preferred_element_type=F32) / total[rows]
        out_ref[:, step * PAIRS : (step + 1) * PAIRS] = write_rows(attn)
    for i in range(NEAR // BLOCK):
        rows = slice(NEAR + i * BLOCK, NEAR + (i + 1) * BLOCK)
        out_ref[i * n : (i + 1) * n, 2 * PAIRS] = write_stats(top[rows], total[rows])


def merge_kernel(y_ref, near_ref, top_ref, total_ref, out_ref):
    lower = lax.broadcasted_iota(jnp.int32, (NEAR, DEPTH), 1) < HALF
    first = read_rows(y_ref[:, 0:PAIRS])
    far = read_rows(y_ref[:, PAIRS : 2 * PAIRS])
    far_top, far_total = read_stats(y_ref[:, 2 * PAIRS])
    near_top = top_ref[...]
    top = jnp.maximum(far_top, near_top)
    far_share = jnp.exp2((far_top - top) * FACTOR) * far_total
    near_share = jnp.exp2((near_top - top) * FACTOR) * total_ref[...]
    second = (far_share * far + near_share * near_ref[...]) / (far_share + near_share)
    out_ref[0] = jnp.where(lower, first, pltpu.roll(second, HALF, 1)).astype(BF16)
    out_ref[1] = jnp.where(lower, pltpu.roll(first, HALF, 1), second).astype(BF16)


def guide_kernel(both_ref, gate_ref, out_ref, held):
    core = lax.axis_index("cfg")
    cond = both_ref[0, core].astype(F32)
    uncond = both_ref[1, core].astype(F32)
    mixed = (uncond + 5.0 * (cond - uncond)).reshape(HEADS, TOK, DEPTH)
    held[...] = (gate_ref[...].reshape(HEADS, 1, DEPTH) * mixed).reshape(NEAR, DEPTH)
    for t in range(TOK):
        rows = held[pl.ds(t, HEADS, stride=TOK), :]
        out_ref[0, t] = rows[:, :HALF].astype(BF16)
        out_ref[1, t] = rows[:, HALF:].astype(BF16)


def call(kernel, out, args, specs=None, scratch=(), flops=0, out_space=pltpu.VMEM, limit=32):
    many = isinstance(out, list)
    shapes = out if many else [out]
    moved = sum(a.size * a.dtype.itemsize for a in list(args) + list(shapes))
    vmem = pl.BlockSpec(memory_space=pltpu.VMEM)
    result = pl.BlockSpec(memory_space=out_space)
    return pl.pallas_call(
        kernel,
        grid=(1,),
        out_shape=out,
        in_specs=specs or [vmem] * len(args),
        out_specs=[result] * len(shapes) if many else result,
        scratch_shapes=list(scratch),
        cost_estimate=pl.CostEstimate(flops=flops, bytes_accessed=moved, transcendentals=0),
        compiler_params=pltpu.CompilerParams(vmem_limit_bytes=limit << 20),
    )(*args)


def body(queries, keys_values, timesteps, gate_table):
    width = HEADS * DEPTH
    sides = [[SIDES * i + side for i in range(HEADS)] for side in range(SIDES)]
    pairs = [[SIDES * i, SIDES * i + 1] for i in range(HEADS)]

    first_pairs = keys_values[0, 0]

    def packed(kernel, pairs, fields):
        return call(
            kernel,
            SHAPE((HEADS, fields * TOK, DEPTH), BF16),
            (queries, pairs),
            [
                pl.BlockSpec((None, 2, TOK, width), lambda i: (0, 0, 0, 0)),
                pl.BlockSpec(memory_space=pltpu.VMEM),
            ],
            [
                pltpu.VMEM((fields, HEADS, TOK, DEPTH), BF16),
                pltpu.SemaphoreType.DMA((fields,)),
            ],
            out_space=pltpu.HBM,
        )

    def to_heads(sent):
        return lax.all_to_all(
            sent, "patch", split_axis=0, concat_axis=0, tiled=True, axis_index_groups=sides
        )

    def over_y(field):
        return lax.all_gather(field, "patch", axis=0, tiled=False, axis_index_groups=pairs)

    def own_patch():
        return call(
            local_kernel,
            [SHAPE((NEAR, DEPTH), F32)] * 3,
            (queries, keys_values),
            [
                pl.BlockSpec((None, 1, TOK, width), lambda i: (0, 1, 0, 0)),
                pl.BlockSpec((None, None, 2, TOK, width), lambda i: (0, 1, 0, 0, 0)),
            ],
        )

    def attended(kernel, args):
        return call(
            kernel,
            SHAPE((HEADS, 2 * PAIRS + 1, 2, DEPTH), BF16),
            args,
            scratch=[
                pltpu.VMEM((ROWS, TOKENS), F32),
                pltpu.VMEM((ROWS, TOKENS), BF16),
                pltpu.VMEM((ROWS, DEPTH), F32),
                pltpu.VMEM((ROWS, DEPTH), F32),
            ],
            flops=4 * ROWS * TOKENS * DEPTH,
        )

    def heads_first():
        held = to_heads(packed(pack_own_kernel, first_pairs, 4))
        held, near = lax.optimization_barrier((held, own_patch()))
        return attended(attend_own_kernel, (held, over_y(held[:, 2 * TOK :, :]))), near

    def y_first():
        held = to_heads(packed(pack_both_kernel, over_y(first_pairs), 6))
        held, near = lax.optimization_barrier((held, own_patch()))
        return attended(attend_both_kernel, (held,)), near

    far, near = lax.cond(lax.axis_index("cfg") == Y_FIRST, y_first, heads_first)
    back = to_heads(far)
    gates = jnp.take(gate_table, timesteps, axis=0, mode="clip").reshape(2, HEADS, 2, HALF)
    gate = lax.dynamic_index_in_dim(gates, lax.axis_index("cfg"), 2, keepdims=False)
    gate = jnp.concatenate([gate[0], gate[1]], axis=1)
    back, gate = lax.optimization_barrier((back, gate))
    attn = call(merge_kernel, SHAPE((2, NEAR, DEPTH), BF16), (back, *near))
    both = lax.all_gather(attn, "cfg", axis=0, tiled=False)
    return call(
        guide_kernel,
        SHAPE((2, TOK, HEADS, HALF), BF16),
        (both, gate),
        scratch=[pltpu.VMEM((NEAR, DEPTH), F32)],
    )


def solution(mesh):
    placed = (
        P("cfg", None, ("clip", "patch"), None),
        P("cfg", None, None, ("clip", "patch"), None),
        P("clip"),
        P(),
    )
    return jax.shard_map(
        body,
        mesh=mesh,
        in_specs=placed,
        out_specs=P(None, ("clip", "patch"), None, "cfg"),
        check_vma=False,
    )
```

```python
import math

import jax
import jax.numpy as jnp
from jax import lax
from jax.experimental import pallas as pl
from jax.experimental.pallas import tpu as pltpu
from jax.sharding import PartitionSpec as P

HEADS = 32
DEPTH = 128
HALF = DEPTH // 2
TOK = 16
SIDES = 2
Y_FIRST = 1
NEAR = HEADS * TOK
ROWS = 2 * NEAR
PAIRS = TOK // 2
SLOTS = DEPTH // TOK
GROUP = 8
TOKENS = SIDES * NEAR
BLOCK = 128
FACTOR = math.log2(math.e) / math.sqrt(DEPTH)
BF16 = jnp.bfloat16
F32 = jnp.float32
SHAPE = jax.ShapeDtypeStruct


def dot_t(a, b):
    return lax.dot_general(a, b, (((1,), (1,)), ((), ())), preferred_element_type=F32)


def pack_kernel(fields, out_ref, packed, sems):
    stores = []
    for i, field in enumerate(fields):
        for h in range(HEADS):
            packed[i, h] = field[:, h * DEPTH : (h + 1) * DEPTH]
        rows = out_ref.at[:, i * TOK : (i + 1) * TOK, :]
        stores.append(pltpu.make_async_copy(packed.at[i], rows, sems.at[i]))
        stores[-1].start()
    for store in stores:
        store.wait()


def pack_own_kernel(q_ref, kv_ref, *refs):
    pack_kernel([ref.at[i] for ref in (q_ref, kv_ref) for i in range(2)], *refs)


def pack_both_kernel(q_ref, stale_ref, *refs):
    fields = [q_ref.at[i] for i in range(2)]
    fields += [stale_ref.at[side, i] for side in range(SIDES) for i in range(2)]
    pack_kernel(fields, *refs)


def split_value(value):
    high = value.astype(BF16).astype(F32)
    rest = value - high
    mid = rest.astype(BF16).astype(F32)
    return high, mid, rest - mid


def write_stats(top, total):
    rows = top.shape[0]
    n = rows // TOK
    lane = lax.broadcasted_iota(jnp.int32, (rows, DEPTH), 1)
    token = lax.broadcasted_iota(jnp.int32, (rows, DEPTH), 0) % TOK
    slot = jnp.where(lane // SLOTS == token, lane % SLOTS, SLOTS)
    value = jnp.where(slot < 3, top, total)
    high, mid, low = split_value(value)
    piece = jnp.where(slot % 3 == 0, high, jnp.where(slot % 3 == 1, mid, low))
    piece = jnp.where(slot < 6, piece, 0.0).astype(BF16)
    out_row = lax.broadcasted_iota(jnp.int32, (2 * n, rows), 0)
    in_row = lax.broadcasted_iota(jnp.int32, (2 * n, rows), 1)
    gather = jnp.where(out_row == in_row // TOK * 2, 1.0, 0.0).astype(BF16)
    return jnp.dot(gather, piece, preferred_element_type=F32).reshape(n, 2, DEPTH).astype(BF16)


def read_stats(stats):
    n = stats.shape[0]
    out_row = lax.broadcasted_iota(jnp.int32, (n * TOK, 2 * n), 0)
    in_row = lax.broadcasted_iota(jnp.int32, (n * TOK, 2 * n), 1)
    spread = jnp.where(in_row == out_row // TOK * 2, 1.0, 0.0).astype(BF16)
    flat = stats.astype(F32).reshape(2 * n, DEPTH).astype(BF16)
    wide = jnp.dot(spread, flat, preferred_element_type=F32)
    lane = lax.broadcasted_iota(jnp.int32, (n * TOK, DEPTH), 1)
    token = lax.broadcasted_iota(jnp.int32, (n * TOK, DEPTH), 0) % TOK
    wide = jnp.where(lane // SLOTS == token, wide, 0.0).astype(BF16)
    slot = lax.broadcasted_iota(jnp.int32, (DEPTH, 2 * DEPTH), 0) % SLOTS
    part = lax.broadcasted_iota(jnp.int32, (DEPTH, 2 * DEPTH), 1) // DEPTH
    pick = jnp.where(jnp.logical_and(slot < 6, slot // 3 == part), 1.0, 0.0).astype(BF16)
    both = jnp.dot(wide, pick, preferred_element_type=F32)
    return both[:, :DEPTH], both[:, DEPTH:]


def write_rows(rows):
    return rows.reshape(-1, TOK // 2, 2, DEPTH).astype(BF16)


def read_rows(pairs):
    return pairs.astype(F32).reshape(-1, DEPTH)


def local_kernel(q_ref, kv_ref, attn_ref, top_ref, total_ref):
    n = GROUP * TOK
    row = lax.broadcasted_iota(jnp.int32, (n, n), 0)
    col = lax.broadcasted_iota(jnp.int32, (n, n), 1)
    same = row // TOK == col // TOK

    for g in range(HEADS // GROUP):
        heads = range(g * GROUP, (g + 1) * GROUP)
        query, key, value = (
            jnp.concatenate([ref[i, :, h * DEPTH : (h + 1) * DEPTH] for h in heads], 0)
            for ref, i in ((q_ref, 0), (kv_ref, 0), (kv_ref, 1))
        )
        score = jnp.where(same, dot_t(query, key), -jnp.inf)
        top = jnp.max(score, axis=1, keepdims=True)
        weight = jnp.exp2((score - top) * FACTOR)
        total = jnp.sum(weight, axis=1, keepdims=True)
        summed = jnp.dot(weight.astype(BF16), value, preferred_element_type=F32)
        here = slice(g * n, (g + 1) * n)
        attn_ref[here] = summed / total
        top_ref[here] = jnp.broadcast_to(top, (n, DEPTH))
        total_ref[here] = jnp.broadcast_to(total, (n, DEPTH))


def attend_own_kernel(x_ref, kv_ref, *refs):
    attend(x_ref, [kv_ref.at[half] for half in range(SIDES)], *refs)


def attend_both_kernel(x_ref, *refs):
    pair = 2 * TOK
    pairs = [x_ref.at[:, pair * (1 + half) : pair * (2 + half), :] for half in range(SIDES)]
    attend(x_ref, pairs, *refs)


def attend(x_ref, pairs, out_ref, staged, sems, score, weight, top, total):
    side = lax.axis_index("patch") % SIDES
    row = lax.broadcasted_iota(jnp.int32, (BLOCK, BLOCK), 0)
    col = lax.broadcasted_iota(jnp.int32, (BLOCK, BLOCK), 1)
    same = row // TOK == col // TOK
    n = BLOCK // TOK
    steps = [slice(step * NEAR, (step + 1) * NEAR) for step in range(2)]
    for step in range(2):
        query = x_ref[:, step * TOK : (step + 1) * TOK, :].reshape(NEAR, DEPTH)
        for half in range(SIDES):
            keys = pairs[half][:, 0:TOK, :].reshape(NEAR, DEPTH)
            score[steps[step], half * NEAR : (half + 1) * NEAR] = dot_t(query, keys)
    values = jnp.concatenate([pair[:, TOK:, :].reshape(NEAR, DEPTH) for pair in pairs], 0)
    stores = []
    for step in range(2):
        for i in range(NEAR // BLOCK):
            here = slice(step * NEAR + i * BLOCK, step * NEAR + (i + 1) * BLOCK)
            if step == 1:
                for half in range(SIDES):
                    cols = slice(half * NEAR + i * BLOCK, half * NEAR + (i + 1) * BLOCK)
                    own = jnp.logical_and(same, side == half)
                    score[here, cols] = jnp.where(own, -jnp.inf, score[here, cols])
            block = score[here]
            most = jnp.max(block, axis=1, keepdims=True)
            weights = jnp.exp2((block - most) * FACTOR)
            added = jnp.sum(weights, axis=1, keepdims=True)
            top[here] = jnp.broadcast_to(most, (BLOCK, DEPTH))
            total[here] = jnp.broadcast_to(added, (BLOCK, DEPTH))
            weight[here] = weights.astype(BF16)
        rows = steps[step]
        attn = jnp.dot(weight[rows], values, preferred_element_type=F32) / total[rows]
        done = slice(step * PAIRS, (step + 1) * PAIRS + step)
        staged[:, step * PAIRS : (step + 1) * PAIRS] = write_rows(attn)
        if step == 1:
            for i in range(NEAR // BLOCK):
                rows = slice(NEAR + i * BLOCK, NEAR + (i + 1) * BLOCK)
                staged[i * n : (i + 1) * n, 2 * PAIRS] = write_stats(top[rows], total[rows])
        store = pltpu.make_async_copy(staged.at[:, done], out_ref.at[:, done], sems.at[step])
        store.start()
        stores.append(store)
    for store in stores:
        store.wait()


def merge_kernel(y_ref, near_ref, top_ref, total_ref, out_ref):
    lower = lax.broadcasted_iota(jnp.int32, (NEAR, DEPTH), 1) < HALF
    first = read_rows(y_ref[:, 0:PAIRS])
    far = read_rows(y_ref[:, PAIRS : 2 * PAIRS])
    far_top, far_total = read_stats(y_ref[:, 2 * PAIRS])
    near_top = top_ref[...]
    top = jnp.maximum(far_top, near_top)
    far_share = jnp.exp2((far_top - top) * FACTOR) * far_total
    near_share = jnp.exp2((near_top - top) * FACTOR) * total_ref[...]
    second = (far_share * far + near_share * near_ref[...]) / (far_share + near_share)
    out_ref[0] = jnp.where(lower, first, pltpu.roll(second, HALF, 1)).astype(BF16)
    out_ref[1] = jnp.where(lower, pltpu.roll(first, HALF, 1), second).astype(BF16)


def guide_kernel(both_ref, gate_ref, out_ref, held):
    core = lax.axis_index("cfg")
    cond = both_ref[0, core].astype(F32)
    uncond = both_ref[1, core].astype(F32)
    mixed = (uncond + 5.0 * (cond - uncond)).reshape(HEADS, TOK, DEPTH)
    held[...] = (gate_ref[...].reshape(HEADS, 1, DEPTH) * mixed).reshape(NEAR, DEPTH)
    for t in range(TOK):
        rows = held[pl.ds(t, HEADS, stride=TOK), :]
        out_ref[0, t] = rows[:, :HALF].astype(BF16)
        out_ref[1, t] = rows[:, HALF:].astype(BF16)


def call(kernel, out, args, specs=None, scratch=(), flops=0, out_space=pltpu.VMEM, limit=32):
    many = isinstance(out, list)
    shapes = out if many else [out]
    moved = sum(a.size * a.dtype.itemsize for a in list(args) + list(shapes))
    vmem = pl.BlockSpec(memory_space=pltpu.VMEM)
    result = pl.BlockSpec(memory_space=out_space)
    return pl.pallas_call(
        kernel,
        grid=(1,),
        out_shape=out,
        in_specs=specs or [vmem] * len(args),
        out_specs=[result] * len(shapes) if many else result,
        scratch_shapes=list(scratch),
        cost_estimate=pl.CostEstimate(flops=flops, bytes_accessed=moved, transcendentals=0),
        compiler_params=pltpu.CompilerParams(vmem_limit_bytes=limit << 20),
    )(*args)


def body(queries, keys_values, timesteps, gate_table):
    width = HEADS * DEPTH
    sides = [[SIDES * i + side for i in range(HEADS)] for side in range(SIDES)]
    pairs = [[SIDES * i, SIDES * i + 1] for i in range(HEADS)]

    first_pairs = keys_values[0, 0]

    def packed(kernel, pairs, fields):
        return call(
            kernel,
            SHAPE((HEADS, fields * TOK, DEPTH), BF16),
            (queries, pairs),
            [
                pl.BlockSpec((None, 2, TOK, width), lambda i: (0, 0, 0, 0)),
                pl.BlockSpec(memory_space=pltpu.VMEM),
            ],
            [
                pltpu.VMEM((fields, HEADS, TOK, DEPTH), BF16),
                pltpu.SemaphoreType.DMA((fields,)),
            ],
            out_space=pltpu.HBM,
        )

    def to_heads(sent):
        return lax.all_to_all(
            sent, "patch", split_axis=0, concat_axis=0, tiled=True, axis_index_groups=sides
        )

    def over_y(field):
        return lax.all_gather(field, "patch", axis=0, tiled=False, axis_index_groups=pairs)

    def own_patch():
        return call(
            local_kernel,
            [SHAPE((NEAR, DEPTH), F32)] * 3,
            (queries, keys_values),
            [
                pl.BlockSpec((None, 1, TOK, width), lambda i: (0, 1, 0, 0)),
                pl.BlockSpec((None, None, 2, TOK, width), lambda i: (0, 1, 0, 0, 0)),
            ],
        )

    def attended(kernel, args):
        return call(
            kernel,
            SHAPE((HEADS, 2 * PAIRS + 1, 2, DEPTH), BF16),
            args,
            scratch=[
                pltpu.VMEM((HEADS, 2 * PAIRS + 1, 2, DEPTH), BF16),
                pltpu.SemaphoreType.DMA((2,)),
                pltpu.VMEM((ROWS, TOKENS), F32),
                pltpu.VMEM((ROWS, TOKENS), BF16),
                pltpu.VMEM((ROWS, DEPTH), F32),
                pltpu.VMEM((ROWS, DEPTH), F32),
            ],
            flops=4 * ROWS * TOKENS * DEPTH,
            out_space=pltpu.HBM,
        )

    def heads_first():
        held = to_heads(packed(pack_own_kernel, first_pairs, 4))
        held, near = lax.optimization_barrier((held, own_patch()))
        return attended(attend_own_kernel, (held, over_y(held[:, 2 * TOK :, :]))), near

    def y_first():
        held = to_heads(packed(pack_both_kernel, over_y(first_pairs), 6))
        held, near = lax.optimization_barrier((held, own_patch()))
        return attended(attend_both_kernel, (held,)), near

    far, near = lax.cond(lax.axis_index("cfg") == Y_FIRST, y_first, heads_first)
    back = to_heads(far)
    gates = jnp.take(gate_table, timesteps, axis=0, mode="clip").reshape(2, HEADS, 2, HALF)
    gate = lax.dynamic_index_in_dim(gates, lax.axis_index("cfg"), 2, keepdims=False)
    gate = jnp.concatenate([gate[0], gate[1]], axis=1)
    back, gate = lax.optimization_barrier((back, gate))
    attn = call(merge_kernel, SHAPE((2, NEAR, DEPTH), BF16), (back, *near))
    both = lax.all_gather(attn, "cfg", axis=0, tiled=False)
    return call(
        guide_kernel,
        SHAPE((2, TOK, HEADS, HALF), BF16),
        (both, gate),
        scratch=[pltpu.VMEM((NEAR, DEPTH), F32)],
    )


def solution(mesh):
    placed = (
        P("cfg", None, ("clip", "patch"), None),
        P("cfg", None, None, ("clip", "patch"), None),
        P("clip"),
        P(),
    )
    return jax.shard_map(
        body,
        mesh=mesh,
        in_specs=placed,
        out_specs=P(None, ("clip", "patch"), None, "cfg"),
        check_vma=False,
    )
```
